32 devices in a mesh: groups: 2 (over y), pts: 4 (over z), chan: 2 (over x), lev: 2 (over core).
Axes of the slice: x: 2, y: 2, z: 4, core: 2. Of those that a mesh axis runs over, the one named last changes fastest.
Arguments:
- cot_first: float32 [100, 73728], P('chan', ('groups', 'pts', 'lev')), parts along dimension 1, may hold values from -6 to 6
- cot_second: float32 [100, 73728], P('chan', ('groups', 'pts', 'lev')), parts along dimension 1, may hold values from -6 to 6
- strength: float32 [2, 200], P(None, ('groups', 'chan')), parts along dimension 1, may hold values from 0.1 to 1
- lengths: int32 [32], P('groups'), parts along dimension 0, may hold values from 1536 to 3072, as said below
- latitude: float32 [32], P('groups'), parts along dimension 0, may hold values from -0.5 to 0.5
- weights: float32 [32], P('groups'), parts along dimension 0, may hold values from 0.0625 to 0.25
Outputs:
- grad_state: float32 [100, 73728], P('chan', ('groups', 'pts', 'lev')), parts along dimension 1
- grad_target: float32 [2, 200, 2, 64, 64], P(None, ('groups', 'chan'), None, ('pts', 'lev')), parts along dimension 1
The draws below stay inside these ranges and needn't reach their ends.
There are 2 independent parts, one for each index of `groups`. The reference program is written for one: setup_inputs(seed, part) draws one part's arguments, and reference() takes and returns one part's arrays. A program takes and returns all parts, laid end to end along the dimension named above; each array names one. Nothing has to cross between parts.
Inputs may be any that keep to these rules, and one draw needn't show every extreme that they name: Every length is a multiple of 4, and the lengths sum to 36864.
All inputs are finite; a program needn't handle non-finite values.
Results may differ from the reference program's by a relative error of at most 0.0003.
Values sent between devices are 32-bit elements; how exact they have to be, the bound alone decides.
No kernel may reach another device: no remote copies, remote signals or barrier semaphores. Data moves between devices by JAX's collectives and lax.ppermute only.
A program may use at most 128 MiB of HBM per device.

```python
import math
import jax
import jax.numpy as jnp
from jax import lax

CHANNELS = 100
MAXLEN = 3072
WAVES = 64
ROWS = 16
POINTS = 36864


def draw_lengths(key, part):
    key = jax.random.fold_in(key, 7)
    half_rows = ROWS // 2
    top_step = MAXLEN // 8
    step_draw = jax.random.randint(jax.random.fold_in(key, 1), (half_rows,), 0, top_step + 1)
    chosen = jax.random.randint(jax.random.fold_in(key, 2), (), 0, half_rows)
    step_draw = jnp.where(jnp.arange(half_rows) == chosen, top_step, step_draw)
    first_rows = MAXLEN // 2 + 4 * step_draw
    second_rows = MAXLEN - 4 * step_draw
    ordering = jax.random.permutation(jax.random.fold_in(key, 3), ROWS)
    return jnp.concatenate([first_rows, second_rows])[ordering].astype(jnp.int32)


def steps_of(stream_key, dims, cuts, least, top_value):
    def one(position, blocks):
        steps = jax.random.uniform(jax.random.fold_in(jax.random.fold_in(stream_key, 6), position), (blocks,), jnp.float32, least / len(cuts), top_value / len(cuts))
        return jnp.repeat(jnp.exp(steps), dims[position] // blocks).reshape((-1,) + (1,) * (len(dims) - position - 1))

    level = one(*cuts[0])
    for cut in cuts[1:]:
        level = level * one(*cut)
    return level


def scatter_about(key, dims, spread, most, cuts=(), held_as=jnp.bfloat16):
    gain = steps_of(key, dims, cuts, -0.22, 0.18) if cuts else 1.0
    drawn = jax.random.normal(key, dims, jnp.float32) * spread * gain
    return jnp.minimum(jnp.maximum(drawn, -most), most).astype(held_as)


def setup_inputs(seed: int = 0, part: int = 0) -> dict:
    key_of = jax.random.split(jax.random.key(seed), 7)
    own_keys = jax.random.split(jax.random.fold_in(key_of[6], part), 7)
    cot_first = scatter_about(own_keys[0], (CHANNELS, POINTS), 1.0, 6.0, ((0, 2), (1, 8)), jnp.float32)
    cot_second = scatter_about(own_keys[1], (CHANNELS, POINTS), 1.0, 6.0, ((0, 2), (1, 8)), jnp.float32)
    strength = jnp.clip(jnp.exp(math.log(1.0) - 2.3025851 * jax.random.uniform(own_keys[2], (2, CHANNELS), jnp.float32) ** steps_of(own_keys[2], (2, CHANNELS), ((1, 2),), -0.2, 0.2)), 0.1, 1.0)
    lengths = draw_lengths(jax.random.fold_in(jax.random.fold_in(key_of[6], part), 71), part)
    latitude = jnp.clip(jax.random.uniform(own_keys[4], (ROWS,), jnp.float32, -0.5, 0.5), -0.5, 0.5)
    weights = jnp.clip(jnp.exp(jax.random.uniform(own_keys[5], (ROWS,), jnp.float32, math.log(0.0625), math.log(0.25))), 0.0625, 0.25)
    return {"cot_first": cot_first, "cot_second": cot_second, "strength": strength, "lengths": lengths, "latitude": latitude, "weights": weights}


HIGHEST = lax.Precision.HIGHEST

def order_factors(wave_count):
    running = 0.0
    values = [0.0]
    for step_id in range(1, wave_count):
        running = running + 0.5 * math.log((2.0 * step_id + 1.0) / (2.0 * step_id))
        values.append(running)
    return values

def legendre(latitude_rows, orders, wave_count):
    log_factors = jnp.asarray(order_factors(wave_count), jnp.float32)
    order_scale = lax.optimization_barrier(jnp.sum(jnp.where(orders[:, None] == jnp.arange(wave_count)[None, :], log_factors[None, :], 0.0), axis=1))
    order_value = orders.astype(jnp.float32)[None, :]
    sine_col = jnp.sqrt(1.0 - latitude_rows * latitude_rows)[:, None]
    diagonal = jnp.sqrt(0.5) * jnp.exp(order_scale[None, :] + order_value * jnp.log(sine_col))
    latitude_col = latitude_rows[:, None]
    previous = jnp.zeros_like(diagonal)
    current = jnp.zeros_like(diagonal)
    degrees = []
    for degree in range(wave_count):
        degree_f = float(degree)
        upper_term = max(4.0 * degree_f * degree_f - 1.0, 0.0)
        lower_term = jnp.maximum(degree_f * degree_f - order_value * order_value, 1.0)
        factor_upper = jnp.sqrt(upper_term / lower_term)
        factor_lower = jnp.sqrt(jnp.maximum((degree_f - 1.0) ** 2 - order_value * order_value, 0.0) / max(4.0 * (degree_f - 1.0) ** 2 - 1.0, 1.0))
        recurrence = factor_upper * (latitude_col * current - factor_lower * previous)
        degree_value = jnp.where(order_value > degree_f, 0.0, jnp.where(order_value == degree_f, diagonal, recurrence))
        previous, current = (current, degree_value)
        degrees.append(degree_value)
    return jnp.stack(degrees, axis=-1)

def row_basis(row_size, row_valid):
    point_ids = jnp.arange(MAXLEN, dtype=jnp.int32)
    wave_ids = jnp.arange(WAVES, dtype=jnp.int32)
    phase_turns = point_ids[None, :, None] * wave_ids[None, None, :] % row_size[:, None, None]
    angle_values = phase_turns.astype(jnp.float32) * (2.0 * jnp.pi / row_size.astype(jnp.float32))[:, None, None]
    inside = ((point_ids[None, :] < row_size[:, None]) & row_valid[:, None]).astype(jnp.float32)[:, :, None]
    return jnp.concatenate([jnp.cos(angle_values) * inside, jnp.sin(angle_values) * inside], axis=-1)

def reference(cot_first, cot_second, strength, lengths, latitude, weights):
    row_total = lengths.shape[0]
    channels, point_total = cot_first.shape
    starts = (jnp.cumsum(lengths) - lengths).astype(jnp.int32)
    wave_ids = jnp.arange(WAVES, dtype=jnp.int32)
    legendre_values = legendre(latitude, wave_ids, WAVES)
    doubling = jnp.where(wave_ids == 0, 1.0, 2.0).astype(jnp.float32)
    row_scale = weights / lengths.astype(jnp.float32)
    everywhere = jnp.ones((1,), jnp.int32) > 0

    def adjoint_synthesis(field_in):
        padded = jnp.pad(field_in, ((0, 0), (0, MAXLEN)))

        def row_fourier(row_id):
            row_piece = lax.dynamic_slice_in_dim(padded, starts[row_id], MAXLEN, 1)
            trig_basis = row_basis(lengths[row_id][None], everywhere)[0]
            return jnp.dot(row_piece, trig_basis, precision=HIGHEST, preferred_element_type=jnp.float32)
        coeff = lax.map(row_fourier, jnp.arange(row_total, dtype=jnp.int32))
        real_part = jnp.einsum('rmn,rcm->cmn', legendre_values, coeff[..., :WAVES], precision=HIGHEST) * doubling[None, :, None]
        imag_part = -jnp.einsum('rmn,rcm->cmn', legendre_values, coeff[..., WAVES:], precision=HIGHEST) * doubling[None, :, None]
        return jnp.stack([real_part, imag_part], axis=1)

    def adjoint_analysis(spectrum):
        cosine = jnp.einsum('rmn,cmn->rcm', legendre_values, spectrum[:, 0], precision=HIGHEST) * row_scale[:, None, None]
        sine_part = -jnp.einsum('rmn,cmn->rcm', legendre_values, spectrum[:, 1], precision=HIGHEST) * row_scale[:, None, None]
        mixed_coeff = jnp.concatenate([cosine, sine_part], axis=-1)

        def place_row(accum, row_id):
            trig_basis = row_basis(lengths[row_id][None], everywhere)[0]
            values = jnp.dot(mixed_coeff[row_id], trig_basis.T, precision=HIGHEST, preferred_element_type=jnp.float32)
            current = lax.dynamic_slice_in_dim(accum, starts[row_id], MAXLEN, 1)
            return (lax.dynamic_update_slice_in_dim(accum, current + values, starts[row_id], 1), None)
        accum = jnp.zeros((channels, point_total + MAXLEN), jnp.float32)
        accum, _ = lax.scan(place_row, accum, jnp.arange(row_total, dtype=jnp.int32))
        return accum[:, :point_total]
    spec_second = adjoint_synthesis(strength[1][:, None] * cot_second)
    carried = cot_first + cot_second - adjoint_analysis(spec_second)
    spec_first = adjoint_synthesis(strength[0][:, None] * carried)
    grad_state = carried - adjoint_analysis(spec_first)
    scaling = float(POINTS) ** (-0.5)
    grad_target = jnp.stack([spec_first, spec_second]) * scaling
    return (grad_state, grad_target)
```

```python
import functools
import math

import jax
import jax.numpy as jnp
import numpy as np
from jax import lax
from jax.experimental import pallas as pl
from jax.experimental.pallas import tpu as pltpu
from jax.sharding import PartitionSpec as P

MAXLEN = 3072
WAVES = 64
BLOCK = 256
LANES = 128
SHARES = 4
GROUP = WAVES // SHARES
PAD = 64
HIGHEST = lax.Precision.HIGHEST
AXES = ("pts", "lev")


def cosine_coefficients():
    nodes = np.cos(np.pi * (np.arange(64) + 0.5) / 64)
    squares = 0.12525 * (nodes + 1.0)
    fitted = np.polynomial.Polynomial.fit(squares, np.cos(2.0 * np.pi * np.sqrt(squares)), 7)
    return [float(value) for value in fitted.convert().coef]


COSINE = cosine_coefficients()


def cos_turns(turns):
    turns = turns - jnp.floor(turns + 0.5)
    square = turns * turns
    value = jnp.full_like(square, COSINE[-1])
    for coefficient in COSINE[-2::-1]:
        value = value * square + coefficient
    return value


def turns_of(wave, point, size):
    inverse = 1.0 / size
    product = wave * point
    whole = jnp.floor(product * inverse + 0.5)
    return (product - whole * size) * inverse


def lane_waves(lane, me, per_device):
    share = (lane >> 4) & 3
    within = lane & (GROUP - 1)
    shift = per_device.bit_length() - 1
    outer = within >> shift
    return per_device * (((me ^ share) & 3) + SHARES * outer) + (within & (per_device - 1))


def device_id():
    return lax.axis_index("pts") * lax.axis_size("lev") + lax.axis_index("lev")


def row_table(lengths, table, me, local, rows):
    begin = me * local
    for slot in range(SHARES):
        table[slot] = 0
        table[SHARES + slot] = MAXLEN
        table[2 * SHARES + slot] = local

    def step(row, carry):
        start, first = carry
        size = lengths[row]
        stop = start + size
        first = first + jnp.where(stop <= begin, 1, 0)

        @pl.when((stop > begin) & (start < begin + local))
        def _():
            table[row & 3] = start - begin
            table[SHARES + (row & 3)] = size
            table[2 * SHARES + row - first] = start - begin

        return stop, first

    _, first = lax.fori_loop(0, rows, step, (jnp.int32(0), jnp.int32(0)))
    table[3 * SHARES] = first


def fill_phases(table, me, per_device, blocks, cosine, sine, sign):
    rows = cosine.shape[1]
    lane = lax.broadcasted_iota(jnp.int32, (rows, LANES), 1)
    begin = BLOCK * lax.broadcasted_iota(jnp.int32, (rows, LANES), 0)
    wave = lane_waves(lane, me, per_device).astype(jnp.float32)
    signs = jnp.where(lane >= PAD, sign, -sign)
    for slot in range(SHARES):
        size = jnp.full((rows, LANES), table[SHARES + slot], jnp.int32).astype(jnp.float32)
        turns = turns_of(wave, (begin - table[slot]).astype(jnp.float32), size)
        cosine[slot] = cos_turns(turns)
        sine[slot] = cos_turns(turns - 0.25) * signs


def basis_of(wave_index, point, size_int, me, per_device):
    wave = lane_waves(wave_index, me, per_device).astype(jnp.float32)
    size = jnp.full(wave.shape, size_int, jnp.int32).astype(jnp.float32)
    turns = turns_of(wave, point.astype(jnp.float32), size)
    value = cos_turns(turns - jnp.where(wave_index >= PAD, 0.25, 0.0))
    high = value.astype(jnp.bfloat16)
    low = (value - high.astype(jnp.float32)).astype(jnp.bfloat16)
    return high, low


def column(row):
    count = row.shape[1]
    down = lax.broadcasted_iota(jnp.int32, (count, count), 0)
    across = lax.broadcasted_iota(jnp.int32, (count, count), 1)
    return jnp.sum(jnp.where(down == across, row, 0.0), axis=1, keepdims=True)


def load_fields(second, first, fields, sems, pieces):
    width = fields.shape[2] // pieces
    copies = []
    for piece in range(pieces):
        for index, source in enumerate((second, first)):
            copies.append(
                pltpu.make_async_copy(
                    source.at[:, pl.ds(piece * width, width)],
                    fields.at[index, :, pl.ds(piece * width, width)],
                    sems.at[piece, index],
                )
            )
    for copy in copies:
        copy.start()
    return copies


def analyse_kernel(per_device, lengths, strength, second, first, *refs):
    messages, (fields, basis, cosine, sine, lhs, total, table, sems) = refs[:SHARES], refs[SHARES:]
    channels, local = second.shape
    blocks = local // BLOCK
    pieces = sems.shape[0]
    copies = load_fields(second, first, fields, sems, pieces)
    me = device_id()
    row_table(lengths, table, me, local, lengths.shape[0])
    fill_phases(table, me, per_device, blocks, cosine, sine, 1.0)
    wave_index = lax.broadcasted_iota(jnp.int32, (BLOCK, LANES), 1)
    point = lax.broadcasted_iota(jnp.int32, (BLOCK, LANES), 0)
    for slot in range(SHARES):
        high, low = basis_of(wave_index, point, table[SHARES + slot], me, per_device)
        basis[slot, :, :LANES] = high
        basis[slot, :, LANES:] = low
    total[...] = jnp.zeros_like(total)
    lhs[...] = jnp.zeros_like(lhs)
    within = lax.broadcasted_iota(jnp.int32, (1, BLOCK), 1)

    def add_block(block, place, slot, low_end, high_end, buffer):
        keep = (within >= low_end) & (within < high_end)
        for index in range(2):
            piece = jnp.where(keep, fields[index, :, pl.ds(place, BLOCK)], 0.0)
            high = piece.astype(jnp.bfloat16)
            low = (piece - high.astype(jnp.float32)).astype(jnp.bfloat16)
            lhs[buffer, pl.ds(index * PAD, channels), :] = high
            lhs[buffer, pl.ds((2 + index) * PAD, channels), :] = low
        product = jnp.dot(lhs[buffer], basis[slot], preferred_element_type=jnp.float32)
        value = (
            product[: 2 * PAD, :LANES] + product[: 2 * PAD, LANES:] + product[2 * PAD :, :LANES]
        )
        turned = (
            value * cosine[slot, pl.ds(block, 1), :]
            + pltpu.roll(value, PAD, 1) * sine[slot, pl.ds(block, 1), :]
        )
        total[slot] = total[slot] + turned

    begin_slot = table[3 * SHARES]
    waited = 0
    for block in range(blocks):
        while waited * (local // pieces) < (block + 1) * BLOCK:
            copies[2 * waited].wait()
            copies[2 * waited + 1].wait()
            waited += 1
        place = block * BLOCK
        slot = begin_slot
        for later in range(1, SHARES):
            slot = slot + jnp.where(table[2 * SHARES + later] <= place, 1, 0)
        slot = slot & 3
        add_block(
            block, place, slot, 0, table[slot] + table[SHARES + slot] - place, block % lhs.shape[0]
        )
    for later in range(1, SHARES):
        begin = table[2 * SHARES + later]

        @pl.when((begin < local) & ((begin & (BLOCK - 1)) != 0))
        def _():
            block = begin >> 8
            place = pl.multiple_of(block * BLOCK, BLOCK)
            add_block(block, place, (begin_slot + later) & 3, begin & (BLOCK - 1), BLOCK, later)

    rate_first = column(strength[0:1, :])
    rate_second = column(strength[1:2, :])
    lane = lax.broadcasted_iota(jnp.int32, (1, LANES), 1)
    chunk = (lane >> 4) & 3
    pairs = []
    for slot in range(SHARES):
        value_second = total[slot, :channels, :]
        value_first = total[slot, PAD : PAD + channels, :]
        part_second = rate_second * value_second
        pairs.append((rate_first * (value_first + value_second) + part_second, part_second))
    for share in range(SHARES):
        for which in range(2):
            value = jnp.zeros((channels, LANES), jnp.float32)
            for slot in range(SHARES):
                moved = pairs[slot][which]
                if slot != share:
                    moved = pltpu.roll(moved, ((slot - share) * GROUP) % LANES, 1)
                value = jnp.where(chunk == slot, moved, value)
            messages[share][pl.ds(which * channels, channels), :] = value


def analyse(lengths, strength, second, first, per_device):
    channels, local = second.shape
    blocks = local // BLOCK
    pieces = 3
    phase_rows = -(-blocks // 8) * 8
    return pl.pallas_call(
        functools.partial(analyse_kernel, per_device),
        out_shape=[jax.ShapeDtypeStruct((2 * channels, LANES), jnp.float32)] * SHARES,
        in_specs=[
            pl.BlockSpec(memory_space=pltpu.SMEM),
            pl.BlockSpec(memory_space=pltpu.VMEM),
            pl.BlockSpec(memory_space=pl.ANY),
            pl.BlockSpec(memory_space=pl.ANY),
        ],
        out_specs=[pl.BlockSpec(memory_space=pltpu.VMEM)] * SHARES,
        scratch_shapes=[
            pltpu.VMEM((2, channels, local), jnp.float32),
            pltpu.VMEM((SHARES, BLOCK, 2 * LANES), jnp.bfloat16),
            pltpu.VMEM((SHARES, phase_rows, LANES), jnp.float32),
            pltpu.VMEM((SHARES, phase_rows, LANES), jnp.float32),
            pltpu.VMEM((4, 4 * PAD, BLOCK), jnp.bfloat16),
            pltpu.VMEM((SHARES, 2 * PAD, LANES), jnp.float32),
            pltpu.SMEM((16,), jnp.int32),
            pltpu.SemaphoreType.DMA((pieces, 2)),
        ],
        compiler_params=pltpu.CompilerParams(vmem_limit_bytes=32 * 1024 * 1024),
        name="analyse",
    )(lengths, strength, second, first)


def restore_kernel(per_device, lengths, *refs):
    messages, (second, first, out, fields, basis, cosine, sine, coeff, table, sems) = (
        refs[:SHARES],
        refs[SHARES:],
    )
    channels, local = second.shape
    blocks = local // BLOCK
    pieces = sems.shape[0]
    copies = load_fields(second, first, fields, sems, pieces)
    me = device_id()
    row_table(lengths, table, me, local, lengths.shape[0])
    fill_phases(table, me, per_device, blocks, cosine, sine, -1.0)
    wave_index = lax.broadcasted_iota(jnp.int32, (LANES, BLOCK), 0)
    point = lax.broadcasted_iota(jnp.int32, (LANES, BLOCK), 1)
    for slot in range(SHARES):
        high, low = basis_of(wave_index, point, table[SHARES + slot], me, per_device)
        basis[slot, :LANES, :] = high
        basis[slot, LANES:, :] = low
    lane = lax.broadcasted_iota(jnp.int32, (1, LANES), 1)
    chunk = (lane >> 4) & 3
    coeff[...] = jnp.zeros_like(coeff)
    for slot in range(SHARES):
        value = jnp.zeros((channels, LANES), jnp.float32)
        for share in range(SHARES):
            moved = messages[share][...]
            if slot != share:
                moved = pltpu.roll(moved, ((share - slot) * GROUP) % LANES, 1)
            value = jnp.where(chunk == share, moved, value)
        coeff[slot, :channels, :] = value
    within = lax.broadcasted_iota(jnp.int32, (1, BLOCK), 1)

    def block_value(block, place, slot):
        value = coeff[slot]
        turned = (
            value * cosine[slot, pl.ds(block, 1), :]
            + pltpu.roll(value, PAD, 1) * sine[slot, pl.ds(block, 1), :]
        )
        high = turned.astype(jnp.bfloat16)
        low = (turned - high.astype(jnp.float32)).astype(jnp.bfloat16)
        left = jnp.concatenate([high, low], axis=0)
        left = jnp.concatenate([left, left], axis=1)
        product = jnp.dot(left, basis[slot], preferred_element_type=jnp.float32)
        value = product[:PAD] + product[PAD:]
        kept = fields[0, :, pl.ds(place, BLOCK)] + fields[1, :, pl.ds(place, BLOCK)]
        return kept - value[:channels]

    begin_slot = table[3 * SHARES]
    waited = 0
    for block in range(blocks):
        while waited * (local // pieces) < (block + 1) * BLOCK:
            copies[2 * waited].wait()
            copies[2 * waited + 1].wait()
            waited += 1
        place = block * BLOCK
        slot = begin_slot
        for later in range(1, SHARES):
            slot = slot + jnp.where(table[2 * SHARES + later] <= place, 1, 0)
        out[:, pl.ds(place, BLOCK)] = block_value(block, place, slot & 3)
    for later in range(1, SHARES):
        begin = table[2 * SHARES + later]

        @pl.when((begin < local) & ((begin & (BLOCK - 1)) != 0))
        def _():
            block = begin >> 8
            place = pl.multiple_of(block * BLOCK, BLOCK)
            value = block_value(block, place, (begin_slot + later) & 3)
            before = out[:, pl.ds(place, BLOCK)]
            out[:, pl.ds(place, BLOCK)] = jnp.where(within >= (begin & (BLOCK - 1)), value, before)


def restore(lengths, messages, second, first, per_device):
    channels, local = second.shape
    blocks = local // BLOCK
    pieces = 3
    phase_rows = -(-blocks // 8) * 8
    return pl.pallas_call(
        functools.partial(restore_kernel, per_device),
        out_shape=jax.ShapeDtypeStruct((channels, local), jnp.float32),
        in_specs=[pl.BlockSpec(memory_space=pltpu.SMEM)]
        + [pl.BlockSpec(memory_space=pltpu.VMEM)] * SHARES
        + [pl.BlockSpec(memory_space=pl.ANY)] * 2,
        out_specs=pl.BlockSpec(memory_space=pltpu.VMEM),
        scratch_shapes=[
            pltpu.VMEM((2, channels, local), jnp.float32),
            pltpu.VMEM((SHARES, 2 * LANES, BLOCK), jnp.bfloat16),
            pltpu.VMEM((SHARES, phase_rows, LANES), jnp.float32),
            pltpu.VMEM((SHARES, phase_rows, LANES), jnp.float32),
            pltpu.VMEM((SHARES, PAD, LANES), jnp.float32),
            pltpu.SMEM((16,), jnp.int32),
            pltpu.SemaphoreType.DMA((pieces, 2)),
        ],
        compiler_params=pltpu.CompilerParams(vmem_limit_bytes=32 * 1024 * 1024),
        name="restore",
    )(lengths, *messages, second, first)


def swapped(value, mask):
    count = lax.axis_size(AXES)
    return lax.ppermute(value, AXES, [(i, i ^ mask) for i in range(count)])


def legendre(latitude, waves):
    order = waves.astype(jnp.float32)[None, :]
    sine = jnp.sqrt(1.0 - latitude * latitude)[:, None]
    place = latitude[:, None]
    diagonal = jnp.full((latitude.shape[0], waves.shape[0]), math.sqrt(0.5), jnp.float32)
    previous = jnp.zeros_like(diagonal)
    current = jnp.zeros_like(diagonal)
    degrees = []
    for degree in range(WAVES):
        if degree:
            diagonal = diagonal * (sine * math.sqrt((2.0 * degree + 1.0) / (2.0 * degree)))
        upper = max(4.0 * degree * degree - 1.0, 0.0)
        below = float(degree - 1) ** 2
        factor_upper = jnp.sqrt(upper / jnp.maximum(float(degree * degree) - order * order, 1.0))
        factor_lower = jnp.sqrt(
            jnp.maximum(below - order * order, 0.0) / max(4.0 * below - 1.0, 1.0)
        )
        value = factor_upper * (place * current - factor_lower * previous)
        value = jnp.where(order > degree, 0.0, jnp.where(order == degree, diagonal, value))
        previous, current = current, value
        degrees.append(value)
    return jnp.stack(degrees, axis=-1)


def middle_general(received, strength, lengths, latitude, weights, local, per_device):
    rows = lengths.shape[0]
    count = lax.axis_size(AXES)
    channels = strength.shape[1]
    me = device_id()
    stops = jnp.cumsum(lengths)
    row_ids = jnp.arange(rows, dtype=jnp.int32)
    slots = jnp.arange(SHARES, dtype=jnp.int32)
    picks = []
    for share in range(SHARES):
        first = jnp.sum((stops <= (me ^ share) * local).astype(jnp.int32))
        held = first + ((slots - first) & 3)
        picks.append((held[:, None] == row_ids[None, :]).astype(jnp.float32))
    total = 0.0
    for pick, message in zip(picks, received):
        total = total + jnp.einsum(
            "gj,fcrgm->jfcrm",
            pick,
            message.reshape(2, channels, 2, SHARES, GROUP),
            precision=HIGHEST,
        )
    mask = SHARES
    while mask < count:
        total = total + swapped(total, mask)
        mask *= 2
    outer = jnp.arange(GROUP, dtype=jnp.int32) // per_device
    waves = per_device * ((me & 3) + SHARES * outer) + jnp.arange(GROUP) % per_device
    values = legendre(latitude, waves)
    gram = jnp.einsum("jmn,kmn->mjk", values, values, precision=HIGHEST)
    scale = jnp.where(waves == 0, 1.0, 2.0)
    rate_first = strength[0][:, None, None]
    both, second = total[:, 0], total[:, 1]
    once = jnp.einsum("mjk,kcrm->jcrm", gram, second, precision=HIGHEST)
    first = both - second - rate_first * weights[:, None, None, None] * once
    back = jnp.einsum("mjk,kcrm->jcrm", gram, first + second, precision=HIGHEST)
    back = back * (weights / lengths.astype(jnp.float32))[:, None, None, None] * scale
    replies = [
        jnp.einsum("gj,jcrm->crgm", pick, back, precision=HIGHEST).reshape(channels, LANES)
        for pick in picks
    ]
    spectrum = jnp.stack([first, second])
    begin = (me // SHARES) * per_device
    spectrum = lax.dynamic_slice_in_dim(spectrum, begin, per_device, 4)
    mine = lax.dynamic_slice_in_dim(values, begin, per_device, 1)
    factor = lax.dynamic_slice_in_dim(scale, begin, per_device, 0)
    factor = factor * (float(local * count) ** -0.5)
    result = jnp.einsum("jmn,sjcrm->scrmn", mine, spectrum, precision=HIGHEST)
    result = result * factor[:, None] * jnp.array([1.0, -1.0])[:, None, None]
    return replies, result


def on_device(cot_first, cot_second, strength, lengths, latitude, weights):
    local = cot_first.shape[1]
    per_device = WAVES // lax.axis_size(AXES)
    messages = analyse(lengths, strength, cot_second, cot_first, per_device)
    received = [messages[0]] + [swapped(messages[i], i) for i in range(1, SHARES)]
    replies, grad_target = middle_general(
        received, strength, lengths, latitude, weights, local, per_device
    )
    answers = [replies[0]] + [swapped(replies[i], i) for i in range(1, SHARES)]
    grad_state = restore(lengths, answers, cot_second, cot_first, per_device)
    return (grad_state, grad_target)


def solution(mesh):
    return jax.shard_map(
        on_device,
        mesh=mesh,
        in_specs=(
            P("chan", ("groups", "pts", "lev")),
            P("chan", ("groups", "pts", "lev")),
            P(None, ("groups", "chan")),
            P("groups"),
            P("groups"),
            P("groups"),
        ),
        out_specs=(
            P("chan", ("groups", "pts", "lev")),
            P(None, ("groups", "chan"), None, ("pts", "lev"), None),
        ),
        check_vma=False,
    )
```

```python
import functools
import math

import jax
import jax.numpy as jnp
import numpy as np
from jax import lax
from jax.experimental import pallas as pl
from jax.experimental.pallas import tpu as pltpu
from jax.sharding import PartitionSpec as P

MAXLEN = 3072
WAVES = 64
BLOCK = 256
LANES = 128
SHARES = 4
GROUP = WAVES // SHARES
PAD = 64
FULL = 60 * 1024 * 1024
SMALL = 8 * 1024 * 1024
HIGHEST = lax.Precision.HIGHEST
AXES = ("pts", "lev")


def cosine_coefficients():
    nodes = np.cos(np.pi * (np.arange(64) + 0.5) / 64)
    squares = 0.12525 * (nodes + 1.0)
    fitted = np.polynomial.Polynomial.fit(squares, np.cos(2.0 * np.pi * np.sqrt(squares)), 7)
    return [float(value) for value in fitted.convert().coef]


COSINE = cosine_coefficients()


def cos_turns(turns):
    turns = turns - jnp.floor(turns + 0.5)
    square = turns * turns
    value = jnp.full_like(square, COSINE[-1])
    for coefficient in COSINE[-2::-1]:
        value = value * square + coefficient
    return value


def turns_of(wave, point, size):
    inverse = 1.0 / size
    product = wave * point
    whole = jnp.floor(product * inverse + 0.5)
    return (product - whole * size) * inverse


def lane_waves(lane, me, per_device):
    share = (lane >> 4) & 3
    within = lane & (GROUP - 1)
    shift = per_device.bit_length() - 1
    outer = within >> shift
    return per_device * (((me ^ share) & 3) + SHARES * outer) + (within & (per_device - 1))


def device_id():
    return lax.axis_index("pts") * lax.axis_size("lev") + lax.axis_index("lev")


def row_table(lengths, table, me, local, rows):
    begin = me * local
    for slot in range(SHARES):
        table[slot] = 0
        table[SHARES + slot] = MAXLEN
        table[2 * SHARES + slot] = local

    def step(row, carry):
        start, first = carry
        size = lengths[row]
        stop = start + size
        first = first + jnp.where(stop <= begin, 1, 0)

        @pl.when((stop > begin) & (start < begin + local))
        def _():
            table[row & 3] = start - begin
            table[SHARES + (row & 3)] = size
            table[2 * SHARES + row - first] = start - begin

        return stop, first

    _, first = lax.fori_loop(0, rows, step, (jnp.int32(0), jnp.int32(0)))
    table[3 * SHARES] = first


def fill_phases(table, me, per_device, blocks, cosine, sine, sign):
    rows = cosine.shape[1]
    lane = lax.broadcasted_iota(jnp.int32, (rows, LANES), 1)
    begin = BLOCK * lax.broadcasted_iota(jnp.int32, (rows, LANES), 0)
    wave = lane_waves(lane, me, per_device).astype(jnp.float32)
    signs = jnp.where(lane >= PAD, sign, -sign)
    for slot in range(SHARES):
        size = jnp.full((rows, LANES), table[SHARES + slot], jnp.int32).astype(jnp.float32)
        turns = turns_of(wave, (begin - table[slot]).astype(jnp.float32), size)
        cosine[slot] = cos_turns(turns)
        sine[slot] = cos_turns(turns - 0.25) * signs


def basis_of(wave_index, point, size_int, me, per_device):
    wave = lane_waves(wave_index, me, per_device).astype(jnp.float32)
    size = jnp.full(wave.shape, size_int, jnp.int32).astype(jnp.float32)
    turns = turns_of(wave, point.astype(jnp.float32), size)
    value = cos_turns(turns - jnp.where(wave_index >= PAD, 0.25, 0.0))
    high = value.astype(jnp.bfloat16)
    low = (value - high.astype(jnp.float32)).astype(jnp.bfloat16)
    return high, low


def column(row):
    count = row.shape[1]
    down = lax.broadcasted_iota(jnp.int32, (count, count), 0)
    across = lax.broadcasted_iota(jnp.int32, (count, count), 1)
    return jnp.sum(jnp.where(down == across, row, 0.0), axis=1, keepdims=True)


def group_roll(value, step):
    if step == 0:
        return value
    lane = lax.broadcasted_iota(jnp.int32, (1, LANES), 1)
    near = ((lane >> 4) & 3) < SHARES - step
    return jnp.where(
        near,
        pltpu.roll(value, LANES - GROUP * step, 1),
        pltpu.roll(value, GROUP * (SHARES - step), 1),
    )


def first_rows(lengths, me, local):
    begins = [(me ^ share) * local for share in range(SHARES)]

    def step(row, carry):
        stop = carry[0] + lengths[row]
        return (stop,) + tuple(
            first + jnp.where(stop <= begin, 1, 0) for first, begin in zip(carry[1:], begins)
        )

    zero = jnp.int32(0)
    return lax.fori_loop(0, lengths.shape[0], step, (zero,) * (1 + SHARES), unroll=True)[1:]


def row_arrays(first):
    lane = lax.broadcasted_iota(jnp.int32, (1, LANES), 1)
    group = (lane >> 4) & 3
    return (first + ((group - first) & 3)) >> 2


def by_row(messages, firsts):
    held = [row_arrays(first) for first in firsts]
    arrays = []
    for index in range(SHARES):
        value = jnp.zeros(messages[0].shape, jnp.float32)
        for array, message in zip(held, messages):
            value = value + jnp.where(array == index, message, 0.0)
        arrays.append(value)
    return arrays


def load_fields(second, first, fields, sems, pieces):
    width = fields.shape[2] // pieces
    copies = []
    for piece in range(pieces):
        for index, source in enumerate((second, first)):
            copies.append(
                pltpu.make_async_copy(
                    source.at[:, pl.ds(piece * width, width)],
                    fields.at[index, :, pl.ds(piece * width, width)],
                    sems.at[piece, index],
                )
            )
    for copy in copies:
        copy.start()
    return copies


def analyse_kernel(per_device, lengths, strength, second, first, *refs):
    messages, (fields, basis, cosine, sine, lhs, total, table, sems) = refs[:SHARES], refs[SHARES:]
    channels, local = second.shape
    blocks = local // BLOCK
    pieces = sems.shape[0]
    copies = load_fields(second, first, fields, sems, pieces)
    me = device_id()
    row_table(lengths, table, me, local, lengths.shape[0])
    fill_phases(table, me, per_device, blocks, cosine, sine, 1.0)
    wave_index = lax.broadcasted_iota(jnp.int32, (BLOCK, LANES), 1)
    point = lax.broadcasted_iota(jnp.int32, (BLOCK, LANES), 0)
    for slot in range(SHARES):
        high, low = basis_of(wave_index, point, table[SHARES + slot], me, per_device)
        basis[slot, :, :LANES] = high
        basis[slot, :, LANES:] = low
    total[...] = jnp.zeros_like(total)
    lhs[...] = jnp.zeros_like(lhs)
    within = lax.broadcasted_iota(jnp.int32, (1, BLOCK), 1)

    def add_block(block, place, slot, low_end, high_end, buffer):
        keep = (within >= low_end) & (within < high_end)
        for index in range(2):
            piece = jnp.where(keep, fields[index, :, pl.ds(place, BLOCK)], 0.0)
            high = piece.astype(jnp.bfloat16)
            low = (piece - high.astype(jnp.float32)).astype(jnp.bfloat16)
            lhs[buffer, pl.ds(index * PAD, channels), :] = high
            lhs[buffer, pl.ds((2 + index) * PAD, channels), :] = low
        product = jnp.dot(lhs[buffer], basis[slot], preferred_element_type=jnp.float32)
        value = (
            product[: 2 * PAD, :LANES] + product[: 2 * PAD, LANES:] + product[2 * PAD :, :LANES]
        )
        turned = (
            value * cosine[slot, pl.ds(block, 1), :]
            + pltpu.roll(value, PAD, 1) * sine[slot, pl.ds(block, 1), :]
        )
        total[slot] = total[slot] + turned

    begin_slot = table[3 * SHARES]
    waited = 0
    for block in range(blocks):
        while waited * (local // pieces) < (block + 1) * BLOCK:
            copies[2 * waited].wait()
            copies[2 * waited + 1].wait()
            waited += 1
        place = block * BLOCK
        slot = begin_slot
        for later in range(1, SHARES):
            slot = slot + jnp.where(table[2 * SHARES + later] <= place, 1, 0)
        slot = slot & 3
        add_block(
            block, place, slot, 0, table[slot] + table[SHARES + slot] - place, block % lhs.shape[0]
        )
    for later in range(1, SHARES):
        begin = table[2 * SHARES + later]

        @pl.when((begin < local) & ((begin & (BLOCK - 1)) != 0))
        def _():
            block = begin >> 8
            place = pl.multiple_of(block * BLOCK, BLOCK)
            add_block(block, place, (begin_slot + later) & 3, begin & (BLOCK - 1), BLOCK, later)

    rate_first = column(strength[0:1, :])
    rate_second = column(strength[1:2, :])
    lane = lax.broadcasted_iota(jnp.int32, (1, LANES), 1)
    chunk = (lane >> 4) & 3
    pairs = []
    for slot in range(SHARES):
        value_second = total[slot, :channels, :]
        value_first = total[slot, PAD : PAD + channels, :]
        part_second = rate_second * value_second
        pairs.append((rate_first * (value_first + value_second) + part_second, part_second))
    for share in range(SHARES):
        for which in range(2):
            value = jnp.zeros((channels, LANES), jnp.float32)
            for slot in range(SHARES):
                moved = pairs[slot][which]
                if slot != share:
                    moved = pltpu.roll(moved, ((slot - share) * GROUP) % LANES, 1)
                value = jnp.where(chunk == slot, moved, value)
            messages[share][pl.ds(which * channels, channels), :] = value


def analyse(lengths, strength, second, first, per_device):
    channels, local = second.shape
    blocks = local // BLOCK
    pieces = 3
    phase_rows = -(-blocks // 8) * 8
    return pl.pallas_call(
        functools.partial(analyse_kernel, per_device),
        out_shape=[jax.ShapeDtypeStruct((2 * channels, LANES), jnp.float32)] * SHARES,
        in_specs=[
            pl.BlockSpec(memory_space=pltpu.SMEM),
            pl.BlockSpec(memory_space=pltpu.VMEM),
            pl.BlockSpec(memory_space=pltpu.HBM),
            pl.BlockSpec(memory_space=pltpu.HBM),
        ],
        out_specs=[pl.BlockSpec(memory_space=pltpu.VMEM)] * SHARES,
        scratch_shapes=[
            pltpu.VMEM((2, channels, local), jnp.float32),
            pltpu.VMEM((SHARES, BLOCK, 2 * LANES), jnp.bfloat16),
            pltpu.VMEM((SHARES, phase_rows, LANES), jnp.float32),
            pltpu.VMEM((SHARES, phase_rows, LANES), jnp.float32),
            pltpu.VMEM((4, 4 * PAD, BLOCK), jnp.bfloat16),
            pltpu.VMEM((SHARES, 2 * PAD, LANES), jnp.float32),
            pltpu.SMEM((16,), jnp.int32),
            pltpu.SemaphoreType.DMA((pieces, 2)),
        ],
        compiler_params=pltpu.CompilerParams(vmem_limit_bytes=FULL),
        name="analyse",
    )(lengths, strength, second, first)


def restore_kernel(per_device, lengths, *refs):
    messages, (second, first, out, basis, cosine, sine, coeff, table) = refs[:SHARES], refs[SHARES:]
    channels, local = second.shape
    blocks = local // BLOCK
    me = device_id()
    row_table(lengths, table, me, local, lengths.shape[0])
    fill_phases(table, me, per_device, blocks, cosine, sine, -1.0)
    wave_index = lax.broadcasted_iota(jnp.int32, (LANES, BLOCK), 0)
    point = lax.broadcasted_iota(jnp.int32, (LANES, BLOCK), 1)
    for slot in range(SHARES):
        high, low = basis_of(wave_index, point, table[SHARES + slot], me, per_device)
        basis[slot, :LANES, :] = high
        basis[slot, LANES:, :] = low
    lane = lax.broadcasted_iota(jnp.int32, (1, LANES), 1)
    chunk = (lane >> 4) & 3
    coeff[...] = jnp.zeros_like(coeff)
    for slot in range(SHARES):
        value = jnp.zeros((channels, LANES), jnp.float32)
        for share in range(SHARES):
            moved = messages[share][...]
            if slot != share:
                moved = pltpu.roll(moved, ((share - slot) * GROUP) % LANES, 1)
            value = jnp.where(chunk == share, moved, value)
        coeff[slot, :channels, :] = value
    within = lax.broadcasted_iota(jnp.int32, (1, BLOCK), 1)

    def block_value(block, place, slot):
        value = coeff[slot]
        turned = (
            value * cosine[slot, pl.ds(block, 1), :]
            + pltpu.roll(value, PAD, 1) * sine[slot, pl.ds(block, 1), :]
        )
        high = turned.astype(jnp.bfloat16)
        low = (turned - high.astype(jnp.float32)).astype(jnp.bfloat16)
        left = jnp.concatenate([high, low], axis=0)
        left = jnp.concatenate([left, left], axis=1)
        product = jnp.dot(left, basis[slot], preferred_element_type=jnp.float32)
        value = product[:PAD] + product[PAD:]
        kept = second[:, pl.ds(place, BLOCK)] + first[:, pl.ds(place, BLOCK)]
        return kept - value[:channels]

    begin_slot = table[3 * SHARES]
    for block in range(blocks):
        place = block * BLOCK
        slot = begin_slot
        for later in range(1, SHARES):
            slot = slot + jnp.where(table[2 * SHARES + later] <= place, 1, 0)
        out[:, pl.ds(place, BLOCK)] = block_value(block, place, slot & 3)
    for later in range(1, SHARES):
        begin = table[2 * SHARES + later]

        @pl.when((begin < local) & ((begin & (BLOCK - 1)) != 0))
        def _():
            block = begin >> 8
            place = pl.multiple_of(block * BLOCK, BLOCK)
            value = block_value(block, place, (begin_slot + later) & 3)
            before = out[:, pl.ds(place, BLOCK)]
            out[:, pl.ds(place, BLOCK)] = jnp.where(within >= (begin & (BLOCK - 1)), value, before)


def restore(lengths, messages, second, first, per_device):
    channels, local = second.shape
    blocks = local // BLOCK
    phase_rows = -(-blocks // 8) * 8
    return pl.pallas_call(
        functools.partial(restore_kernel, per_device),
        out_shape=jax.ShapeDtypeStruct((channels, local), jnp.float32),
        in_specs=[pl.BlockSpec(memory_space=pltpu.SMEM)]
        + [pl.BlockSpec(memory_space=pltpu.VMEM)] * (SHARES + 2),
        out_specs=pl.BlockSpec(memory_space=pltpu.VMEM),
        scratch_shapes=[
            pltpu.VMEM((SHARES, 2 * LANES, BLOCK), jnp.bfloat16),
            pltpu.VMEM((SHARES, phase_rows, LANES), jnp.float32),
            pltpu.VMEM((SHARES, phase_rows, LANES), jnp.float32),
            pltpu.VMEM((SHARES, PAD, LANES), jnp.float32),
            pltpu.SMEM((16,), jnp.int32),
        ],
        compiler_params=pltpu.CompilerParams(vmem_limit_bytes=32 * 1024 * 1024),
        name="restore",
    )(lengths, *messages, second, first)


def swapped(value, mask):
    count = lax.axis_size(AXES)
    return lax.ppermute(value, AXES, [(i, i ^ mask) for i in range(count)])


def legendre(latitude, waves):
    order = waves.astype(jnp.float32)[None, :]
    sine = jnp.sqrt(1.0 - latitude * latitude)[:, None]
    place = latitude[:, None]
    diagonal = jnp.full((latitude.shape[0], waves.shape[0]), math.sqrt(0.5), jnp.float32)
    previous = jnp.zeros_like(diagonal)
    current = jnp.zeros_like(diagonal)
    degrees = []
    for degree in range(WAVES):
        if degree:
            diagonal = diagonal * (sine * math.sqrt((2.0 * degree + 1.0) / (2.0 * degree)))
        upper = max(4.0 * degree * degree - 1.0, 0.0)
        below = float(degree - 1) ** 2
        factor_upper = jnp.sqrt(upper / jnp.maximum(float(degree * degree) - order * order, 1.0))
        factor_lower = jnp.sqrt(
            jnp.maximum(below - order * order, 0.0) / max(4.0 * below - 1.0, 1.0)
        )
        value = factor_upper * (place * current - factor_lower * previous)
        value = jnp.where(order > degree, 0.0, jnp.where(order == degree, diagonal, value))
        previous, current = current, value
        degrees.append(value)
    return jnp.stack(degrees, axis=-1)


def middle_general(received, strength, lengths, latitude, weights, local, per_device):
    rows = lengths.shape[0]
    count = lax.axis_size(AXES)
    channels = strength.shape[1]
    me = device_id()
    stops = jnp.cumsum(lengths)
    row_ids = jnp.arange(rows, dtype=jnp.int32)
    slots = jnp.arange(SHARES, dtype=jnp.int32)
    picks = []
    for share in range(SHARES):
        first = jnp.sum((stops <= (me ^ share) * local).astype(jnp.int32))
        held = first + ((slots - first) & 3)
        picks.append((held[:, None] == row_ids[None, :]).astype(jnp.float32))
    total = 0.0
    for pick, message in zip(picks, received):
        total = total + jnp.einsum(
            "gj,fcrgm->jfcrm",
            pick,
            message.reshape(2, channels, 2, SHARES, GROUP),
            precision=HIGHEST,
        )
    mask = SHARES
    while mask < count:
        total = total + swapped(total, mask)
        mask *= 2
    outer = jnp.arange(GROUP, dtype=jnp.int32) // per_device
    waves = per_device * ((me & 3) + SHARES * outer) + jnp.arange(GROUP) % per_device
    values = legendre(latitude, waves)
    gram = jnp.einsum("jmn,kmn->mjk", values, values, precision=HIGHEST)
    scale = jnp.where(waves == 0, 1.0, 2.0)
    rate_first = strength[0][:, None, None]
    both, second = total[:, 0], total[:, 1]
    once = jnp.einsum("mjk,kcrm->jcrm", gram, second, precision=HIGHEST)
    first = both - second - rate_first * weights[:, None, None, None] * once
    back = jnp.einsum("mjk,kcrm->jcrm", gram, first + second, precision=HIGHEST)
    back = back * (weights / lengths.astype(jnp.float32))[:, None, None, None] * scale
    replies = [
        jnp.einsum("gj,jcrm->crgm", pick, back, precision=HIGHEST).reshape(channels, LANES)
        for pick in picks
    ]
    spectrum = jnp.stack([first, second])
    begin = (me // SHARES) * per_device
    spectrum = lax.dynamic_slice_in_dim(spectrum, begin, per_device, 4)
    mine = lax.dynamic_slice_in_dim(values, begin, per_device, 1)
    factor = lax.dynamic_slice_in_dim(scale, begin, per_device, 0)
    factor = factor * (float(local * count) ** -0.5)
    result = jnp.einsum("jmn,sjcrm->scrmn", mine, spectrum, precision=HIGHEST)
    result = result * factor[:, None] * jnp.array([1.0, -1.0])[:, None, None]
    return replies, result


def prepare_kernel(per_device, count, local, lengths, latitude, weights, coupling, poly, gram, pt, square):
    me = device_id()
    down = lax.broadcasted_iota(jnp.int32, (8, LANES), 0)
    lane = lax.broadcasted_iota(jnp.int32, (8, LANES), 1)
    group = (lane >> 4) & 3
    packed = down >= SHARES
    array = jnp.where(packed, (lane >> 6) * 2 + ((lane >> 3) & 1), down)
    row = SHARES * array + group
    within = lane & (GROUP - 1)
    outer = within >> 3
    order = jnp.where(
        packed, 8 * me + (lane & 7), 8 * ((me & 3) + SHARES * outer) + (lane & 7)
    ).astype(jnp.float32)
    place = jnp.zeros((8, LANES), jnp.float32)
    weight = jnp.zeros((8, LANES), jnp.float32)
    size = jnp.zeros((8, LANES), jnp.int32)
    for index in range(lengths.shape[0]):
        here = row == index
        place = jnp.where(here, latitude[index], place)
        weight = jnp.where(here, weights[index], weight)
        size = jnp.where(here, lengths[index], size)
    doubling = jnp.where(order == 0.0, 1.0, 2.0)
    scale = weight / size.astype(jnp.float32) * doubling
    sine = jnp.sqrt(1.0 - place * place)
    order_square = order * order
    diagonal = jnp.full((8, LANES), math.sqrt(0.5), jnp.float32)
    previous = jnp.zeros((8, LANES), jnp.float32)
    current = previous
    for degree in range(WAVES):
        if degree:
            diagonal = diagonal * (sine * math.sqrt((2.0 * degree + 1.0) / (2.0 * degree)))
        upper = math.sqrt(max(4.0 * degree * degree - 1.0, 0.0))
        below = float(degree - 1) ** 2
        factor_upper = upper * lax.rsqrt(jnp.maximum(float(degree * degree) - order_square, 1.0))
        factor_lower = jnp.sqrt(
            jnp.maximum(below - order_square, 0.0) * (1.0 / max(4.0 * below - 1.0, 1.0))
        )
        value = (factor_upper * place) * current - (factor_upper * factor_lower) * previous
        value = jnp.where(order > degree, 0.0, jnp.where(order == degree, diagonal, value))
        previous, current = current, value
        for index in range(SHARES + 1):
            pt[index, pl.ds(degree, 1), :] = value[index : index + 1, :]
    for step in range(SHARES):
        for source in range(SHARES):
            moved = group_roll(pt[source], step)
            for target in range(SHARES):
                square[target, pl.ds(step * SHARES + source, 1), :] = jnp.sum(
                    pt[target] * moved, axis=0, keepdims=True
                )
    twice = [jnp.zeros((GROUP, LANES), jnp.float32)] * SHARES
    for through in range(SHARES):
        weighted = square[through] * weight[through : through + 1, :]
        for step in range(SHARES):
            moved = group_roll(weighted, step)
            if step:
                moved = jnp.concatenate(
                    [moved[GROUP - SHARES * step :], moved[: GROUP - SHARES * step]], axis=0
                )
            for target in range(SHARES):
                factor = square[target, pl.ds(step * SHARES + through, 1), :]
                twice[target] = twice[target] + factor * moved
    for target in range(SHARES):
        coupling[0, target] = square[target] * scale[target : target + 1, :]
        coupling[1, target] = twice[target] * scale[target : target + 1, :]
    mine = pt[SHARES]
    factor = doubling[SHARES : SHARES + 1, :] * (float(local * count) ** -0.5)
    poly[...] = mine * factor
    for step in range(GROUP):
        moved = pltpu.roll(mine, (LANES - 8 * step) % LANES, 1) if step else mine
        gram[pl.ds(step, 1), :] = weight[SHARES : SHARES + 1, :] * jnp.sum(
            mine * moved, axis=0, keepdims=True
        )


SMEM = pl.BlockSpec(memory_space=pltpu.SMEM)
VMEM = pl.BlockSpec(memory_space=pltpu.VMEM)


def floats(*shape):
    return jax.ShapeDtypeStruct(shape, jnp.float32)


def prepare(lengths, latitude, weights, per_device, count, local):
    return pl.pallas_call(
        functools.partial(prepare_kernel, per_device, count, local),
        out_shape=[
            floats(2, SHARES, GROUP, LANES),
            floats(WAVES, LANES),
            floats(GROUP, LANES),
        ],
        in_specs=[SMEM] * 3,
        out_specs=[VMEM] * 3,
        scratch_shapes=[
            pltpu.VMEM((SHARES + 1, WAVES, LANES), jnp.float32),
            pltpu.VMEM((SHARES, GROUP, LANES), jnp.float32),
        ],
        compiler_params=pltpu.CompilerParams(vmem_limit_bytes=SMALL),
        name="prepare",
    )(lengths, latitude, weights)


def couple_kernel(local, lengths, strength, coupling, *refs):
    messages, out = [ref[...] for ref in refs[:SHARES]], refs[SHARES]
    channels = strength.shape[1]
    firsts = first_rows(lengths, device_id(), local)
    arrays = by_row(messages, firsts)
    rate_first = column(strength[0:1, :])
    sums = [jnp.zeros((channels, LANES), jnp.float32)] * SHARES
    for source in range(SHARES):
        both = arrays[source][:channels]
        second = rate_first * arrays[source][channels:]
        for step in range(SHARES):
            moved_both = group_roll(both, step)
            moved_second = group_roll(second, step)
            at = pl.ds(step * SHARES + source, 1)
            for target in range(SHARES):
                sums[target] = (
                    sums[target]
                    + coupling[0, target, at, :] * moved_both
                    - coupling[1, target, at, :] * moved_second
                )
    for target in range(SHARES):
        out[pl.ds(target * channels, channels), :] = sums[target]


def couple(lengths, strength, coupling, messages, local):
    channels = strength.shape[1]
    return pl.pallas_call(
        functools.partial(couple_kernel, local),
        out_shape=floats(SHARES * channels, LANES),
        in_specs=[SMEM] + [VMEM] * (2 + SHARES),
        out_specs=VMEM,
        compiler_params=pltpu.CompilerParams(vmem_limit_bytes=SMALL),
        name="couple",
    )(lengths, strength, coupling, *messages)


def pack_kernel(local, lengths, *refs):
    messages, (own, other) = [ref[...] for ref in refs[:SHARES]], refs[SHARES:]
    rows = messages[0].shape[0]
    me = device_id()
    arrays = by_row(messages, first_rows(lengths, me, local))
    lane = lax.broadcasted_iota(jnp.int32, (1, LANES), 1)
    array = (lane >> 6) * 2 + ((lane >> 3) & 1)
    upper = me >= SHARES
    for part in range(2):
        halves = []
        for half in range(2):
            value = jnp.zeros((rows, LANES), jnp.float32)
            for index in range(SHARES):
                shift = (64 * (index >> 1) + 8 * (index & 1) - 64 * part - 8 * half) % LANES
                moved = pltpu.roll(arrays[index], shift, 1) if shift else arrays[index]
                value = jnp.where(array == index, moved, value)
            halves.append(value)
        own[pl.ds(part * rows, rows), :] = jnp.where(upper, halves[1], halves[0])
        other[pl.ds(part * rows, rows), :] = jnp.where(upper, halves[0], halves[1])


def pack(lengths, messages, local):
    rows = messages[0].shape[0]
    return pl.pallas_call(
        functools.partial(pack_kernel, local),
        out_shape=[floats(2 * rows, LANES)] * 2,
        in_specs=[SMEM] + [VMEM] * SHARES,
        out_specs=[VMEM] * 2,
        compiler_params=pltpu.CompilerParams(vmem_limit_bytes=SMALL),
        name="pack",
    )(lengths, *messages)


def hand_out_kernel(local, lengths, own, other, *outs):
    channels = outs[0].shape[0]
    firsts = first_rows(lengths, device_id(), local)
    sums = []
    for index in range(SHARES):
        at = pl.ds(index * channels, channels)
        sums.append(own[at, :] + other[at, :])
    for first, out in zip(firsts, outs):
        array = row_arrays(first)
        value = sums[0]
        for index in range(1, SHARES):
            value = jnp.where(array == index, sums[index], value)
        out[...] = value


def hand_out(lengths, own, other, local):
    channels = own.shape[0] // SHARES
    return pl.pallas_call(
        functools.partial(hand_out_kernel, local),
        out_shape=[floats(channels, LANES)] * SHARES,
        in_specs=[SMEM] + [VMEM] * 2,
        out_specs=[VMEM] * SHARES,
        compiler_params=pltpu.CompilerParams(vmem_limit_bytes=SMALL),
        name="hand_out",
    )(lengths, own, other)


def spectrum_kernel(strength, own, other, poly, gram, out):
    channels = strength.shape[1]
    rate_first = column(strength[0:1, :])
    down = lax.broadcasted_iota(jnp.int32, (8, LANES), 0)
    lane = lax.broadcasted_iota(jnp.int32, (8, LANES), 1)
    match = jnp.where(down == (lane & 7), 1.0, 0.0)[None]
    high = poly[...].astype(jnp.bfloat16)
    low = (poly[...] - high.astype(jnp.float32)).astype(jnp.bfloat16)
    right = jnp.concatenate(
        [
            jnp.concatenate([high, high], axis=1),
            jnp.concatenate([low, jnp.zeros_like(low)], axis=1),
        ],
        axis=0,
    )
    for part in range(2):
        at = pl.ds(2 * part * channels, channels)
        both = own[at, :] + other[at, :]
        at = pl.ds((2 * part + 1) * channels, channels)
        second = own[at, :] + other[at, :]
        first = both - second
        for step in range(GROUP):
            moved = pltpu.roll(second, (LANES - 8 * step) % LANES, 1) if step else second
            first = first - rate_first * (gram[pl.ds(step, 1), :] * moved)
        for index, value in enumerate((first, second)):
            if part:
                value = -value
            rounded = value.astype(jnp.bfloat16).astype(jnp.float32)
            sides = []
            for side in (rounded, value - rounded):
                spread = side[:, None, :] * match
                sides.append(spread.reshape(8 * channels, LANES).astype(jnp.bfloat16))
            product = lax.dot_general(
                jnp.concatenate(sides, axis=1),
                right,
                (((1,), (1,)), ((), ())),
                preferred_element_type=jnp.float32,
            )
            result = product[:, :WAVES] + product[:, WAVES:]
            out[index, :, part] = result.reshape(channels, 8, WAVES)


def spectrum(strength, own, other, poly, gram):
    channels = strength.shape[1]
    return pl.pallas_call(
        spectrum_kernel,
        out_shape=floats(2, channels, 2, 8, WAVES),
        in_specs=[VMEM] * 5,
        out_specs=VMEM,
        compiler_params=pltpu.CompilerParams(vmem_limit_bytes=SMALL),
        name="spectrum",
    )(strength, own, other, poly, gram)


def middle_small(received, strength, lengths, latitude, weights, local, per_device, count):
    coupling, poly, gram = prepare(lengths, latitude, weights, per_device, count, local)
    part = couple(lengths, strength, coupling, received, local)
    other_part = swapped(part, SHARES)
    own, sent = pack(lengths, received, local)
    other = swapped(sent, SHARES)
    replies = hand_out(lengths, part, other_part, local)
    return replies, (strength, own, other, poly, gram)


def on_device(cot_first, cot_second, strength, lengths, latitude, weights):
    local = cot_first.shape[1]
    count = lax.axis_size(AXES)
    per_device = WAVES // count
    messages = analyse(lengths, strength, cot_second, cot_first, per_device)
    received = [messages[0]] + [swapped(messages[i], i) for i in range(1, SHARES)]
    arguments = (received, strength, lengths, latitude, weights, local, per_device)
    small = count == 2 * SHARES and lengths.shape[0] == GROUP
    if small:
        replies, pieces = middle_small(*arguments, count)
    else:
        replies, grad_target = middle_general(*arguments)
    answers = [replies[0]] + [swapped(replies[i], i) for i in range(1, SHARES)]
    grad_state = restore(lengths, answers, cot_second, cot_first, per_device)
    if small:
        grad_target = spectrum(*pieces)
    return (grad_state, grad_target)


def solution(mesh):
    return jax.shard_map(
        on_device,
        mesh=mesh,
        in_specs=(
            P("chan", ("groups", "pts", "lev")),
            P("chan", ("groups", "pts", "lev")),
            P(None, ("groups", "chan")),
            P("groups"),
            P("groups"),
            P("groups"),
        ),
        out_specs=(
            P("chan", ("groups", "pts", "lev")),
            P(None, ("groups", "chan"), None, ("pts", "lev"), None),
        ),
        check_vma=False,
    )
```

```python
import functools
import math

import jax
import jax.numpy as jnp
import numpy as np
from jax import lax
from jax.experimental import pallas as pl
from jax.experimental.pallas import tpu as pltpu
from jax.sharding import PartitionSpec as P

MAXLEN = 3072
WAVES = 64
BLOCK = 256
LANES = 128
SHARES = 4
GROUP = WAVES // SHARES
PAD = 64
FULL = 60 * 1024 * 1024
WINDOW = 3
SMALL = 8 * 1024 * 1024
HIGHEST = lax.Precision.HIGHEST
AXES = ("pts", "lev")


def cosine_coefficients():
    nodes = np.cos(np.pi * (np.arange(64) + 0.5) / 64)
    squares = 0.12525 * (nodes + 1.0)
    fitted = np.polynomial.Polynomial.fit(squares, np.cos(2.0 * np.pi * np.sqrt(squares)), 7)
    return [float(value) for value in fitted.convert().coef]


COSINE = cosine_coefficients()


def cos_turns(turns):
    turns = turns - jnp.floor(turns + 0.5)
    square = turns * turns
    value = jnp.full_like(square, COSINE[-1])
    for coefficient in COSINE[-2::-1]:
        value = value * square + coefficient
    return value


def turns_of(wave, point, size):
    inverse = 1.0 / size
    product = wave * point
    whole = jnp.floor(product * inverse + 0.5)
    return (product - whole * size) * inverse


def lane_waves(lane, me, per_device):
    share = (lane >> 4) & 3
    within = lane & (GROUP - 1)
    shift = per_device.bit_length() - 1
    outer = within >> shift
    return per_device * (((me ^ share) & 3) + SHARES * outer) + (within & (per_device - 1))


def device_id():
    return lax.axis_index("pts") * lax.axis_size("lev") + lax.axis_index("lev")


def row_table(lengths, table, me, local, rows):
    begin = me * local
    for slot in range(SHARES):
        table[slot] = 0
        table[SHARES + slot] = MAXLEN
        table[2 * SHARES + slot] = local

    def step(row, carry):
        start, first = carry
        size = lengths[row]
        stop = start + size
        first = first + jnp.where(stop <= begin, 1, 0)

        @pl.when((stop > begin) & (start < begin + local))
        def _():
            table[row & 3] = start - begin
            table[SHARES + (row & 3)] = size
            table[2 * SHARES + row - first] = start - begin

        return stop, first

    _, first = lax.fori_loop(0, rows, step, (jnp.int32(0), jnp.int32(0)))
    table[3 * SHARES] = first


def fill_phases(table, me, per_device, blocks, cosine, sine, sign):
    rows = cosine.shape[1]
    lane = lax.broadcasted_iota(jnp.int32, (rows, LANES), 1)
    begin = BLOCK * lax.broadcasted_iota(jnp.int32, (rows, LANES), 0)
    wave = lane_waves(lane, me, per_device).astype(jnp.float32)
    signs = jnp.where(lane >= PAD, sign, -sign)
    for slot in range(SHARES):
        size = jnp.full((rows, LANES), table[SHARES + slot], jnp.int32).astype(jnp.float32)
        turns = turns_of(wave, (begin - table[slot]).astype(jnp.float32), size)
        cosine[slot] = cos_turns(turns)
        sine[slot] = cos_turns(turns - 0.25) * signs


def basis_of(wave_index, point, size_int, me, per_device):
    wave = lane_waves(wave_index, me, per_device).astype(jnp.float32)
    size = jnp.full(wave.shape, size_int, jnp.int32).astype(jnp.float32)
    turns = turns_of(wave, point.astype(jnp.float32), size)
    value = cos_turns(turns - jnp.where(wave_index >= PAD, 0.25, 0.0))
    high = value.astype(jnp.bfloat16)
    low = (value - high.astype(jnp.float32)).astype(jnp.bfloat16)
    return high, low


def column(row):
    count = row.shape[1]
    down = lax.broadcasted_iota(jnp.int32, (count, count), 0)
    across = lax.broadcasted_iota(jnp.int32, (count, count), 1)
    return jnp.sum(jnp.where(down == across, row, 0.0), axis=1, keepdims=True)


def group_roll(value, step):
    if step == 0:
        return value
    lane = lax.broadcasted_iota(jnp.int32, (1, LANES), 1)
    near = ((lane >> 4) & 3) < SHARES - step
    return jnp.where(
        near,
        pltpu.roll(value, LANES - GROUP * step, 1),
        pltpu.roll(value, GROUP * (SHARES - step), 1),
    )


def first_rows(lengths, devices, local):
    begins = [device * local for device in devices]

    def step(row, carry):
        stop = carry[0] + lengths[row]
        return (stop,) + tuple(
            first + jnp.where(stop <= begin, 1, 0) for first, begin in zip(carry[1:], begins)
        )

    zero = jnp.int32(0)
    return lax.fori_loop(0, lengths.shape[0], step, (zero,) * (1 + len(devices)), unroll=True)[1:]


def near(me):
    return [me ^ share for share in range(SHARES)]


def row_arrays(first):
    lane = lax.broadcasted_iota(jnp.int32, (1, LANES), 1)
    group = (lane >> 4) & 3
    return (first + ((group - first) & 3)) >> 2


def by_row(messages, firsts):
    held = [row_arrays(first) for first in firsts]
    arrays = []
    for index in range(SHARES):
        value = jnp.zeros(messages[0].shape, jnp.float32)
        for array, message in zip(held, messages):
            value = value + jnp.where(array == index, message, 0.0)
        arrays.append(value)
    return arrays


def split_block(begin, blocks):
    within = begin & (BLOCK - 1)
    return jnp.minimum(begin >> 8, blocks - 1), jnp.where(within == 0, BLOCK, within)


def load_fields(second, first, fields, sems, pieces):
    width = fields.shape[2] // pieces
    copies = []
    for piece in range(pieces):
        for index, source in enumerate((second, first)):
            copies.append(
                pltpu.make_async_copy(
                    source.at[:, pl.ds(piece * width, width)],
                    fields.at[index, :, pl.ds(piece * width, width)],
                    sems.at[piece, index],
                )
            )
    for copy in copies:
        copy.start()
    return copies


def analyse_kernel(per_device, lengths, strength, second, first, *refs):
    messages, (fields, basis, cosine, sine, lhs, total, table, sems) = refs[:SHARES], refs[SHARES:]
    channels, local = second.shape
    blocks = local // BLOCK
    pieces = sems.shape[0]
    copies = load_fields(second, first, fields, sems, pieces)
    me = device_id()
    row_table(lengths, table, me, local, lengths.shape[0])
    fill_phases(table, me, per_device, blocks, cosine, sine, 1.0)
    wave_index = lax.broadcasted_iota(jnp.int32, (BLOCK, LANES), 1)
    point = lax.broadcasted_iota(jnp.int32, (BLOCK, LANES), 0)
    for slot in range(SHARES):
        high, low = basis_of(wave_index, point, table[SHARES + slot], me, per_device)
        basis[slot, :, :LANES] = high
        basis[slot, :, LANES:] = low
    total[...] = jnp.zeros_like(total)
    lhs[...] = jnp.zeros_like(lhs)
    within = lax.broadcasted_iota(jnp.int32, (1, BLOCK), 1)

    def add_block(block, place, slot, low_end, high_end, buffer):
        keep = (within >= low_end) & (within < high_end)
        for index in range(2):
            piece = jnp.where(keep, fields[index, :, pl.ds(place, BLOCK)], 0.0)
            high = piece.astype(jnp.bfloat16)
            low = (piece - high.astype(jnp.float32)).astype(jnp.bfloat16)
            lhs[buffer, pl.ds(index * PAD, channels), :] = high
            lhs[buffer, pl.ds((2 + index) * PAD, channels), :] = low
        product = jnp.dot(lhs[buffer], basis[slot], preferred_element_type=jnp.float32)
        value = (
            product[: 2 * PAD, :LANES] + product[: 2 * PAD, LANES:] + product[2 * PAD :, :LANES]
        )
        turned = (
            value * cosine[slot, pl.ds(block, 1), :]
            + pltpu.roll(value, PAD, 1) * sine[slot, pl.ds(block, 1), :]
        )
        total[slot] = total[slot] + turned

    begin_slot = table[3 * SHARES]
    waited = 0
    for block in range(blocks):
        while waited * (local // pieces) < (block + 1) * BLOCK:
            copies[2 * waited].wait()
            copies[2 * waited + 1].wait()
            waited += 1
        place = block * BLOCK
        slot = begin_slot
        for later in range(1, SHARES):
            slot = slot + jnp.where(table[2 * SHARES + later] <= place, 1, 0)
        slot = slot & 3
        add_block(
            block, place, slot, 0, table[slot] + table[SHARES + slot] - place, block % lhs.shape[0]
        )
    for later in range(1, SHARES):
        block, low_end = split_block(table[2 * SHARES + later], blocks)
        place = pl.multiple_of(block * BLOCK, BLOCK)
        add_block(block, place, (begin_slot + later) & 3, low_end, BLOCK, later)

    rate_first = column(strength[0:1, :])
    rate_second = column(strength[1:2, :])
    lane = lax.broadcasted_iota(jnp.int32, (1, LANES), 1)
    chunk = (lane >> 4) & 3
    pairs = []
    for slot in range(SHARES):
        value_second = total[slot, :channels, :]
        value_first = total[slot, PAD : PAD + channels, :]
        part_second = rate_second * value_second
        pairs.append((rate_first * (value_first + value_second) + part_second, part_second))
    for share in range(SHARES):
        for which in range(2):
            value = jnp.zeros((channels, LANES), jnp.float32)
            for slot in range(SHARES):
                moved = pairs[slot][which]
                if slot != share:
                    moved = pltpu.roll(moved, ((slot - share) * GROUP) % LANES, 1)
                value = jnp.where(chunk == slot, moved, value)
            messages[share][pl.ds(which * channels, channels), :] = value


def analyse(lengths, strength, second, first, per_device):
    channels, local = second.shape
    blocks = local // BLOCK
    pieces = 3
    phase_rows = -(-blocks // 8) * 8
    return pl.pallas_call(
        functools.partial(analyse_kernel, per_device),
        out_shape=[jax.ShapeDtypeStruct((2 * channels, LANES), jnp.float32)] * SHARES,
        in_specs=[
            pl.BlockSpec(memory_space=pltpu.SMEM),
            pl.BlockSpec(memory_space=pltpu.VMEM),
            pl.BlockSpec(memory_space=pltpu.HBM),
            pl.BlockSpec(memory_space=pltpu.HBM),
        ],
        out_specs=[pl.BlockSpec(memory_space=pltpu.VMEM)] * SHARES,
        scratch_shapes=[
            pltpu.VMEM((2, channels, local), jnp.float32),
            pltpu.VMEM((SHARES, BLOCK, 2 * LANES), jnp.bfloat16),
            pltpu.VMEM((SHARES, phase_rows, LANES), jnp.float32),
            pltpu.VMEM((SHARES, phase_rows, LANES), jnp.float32),
            pltpu.VMEM((4, 4 * PAD, BLOCK), jnp.bfloat16),
            pltpu.VMEM((SHARES, 2 * PAD, LANES), jnp.float32),
            pltpu.SMEM((16,), jnp.int32),
            pltpu.SemaphoreType.DMA((pieces, 2)),
        ],
        compiler_params=pltpu.CompilerParams(vmem_limit_bytes=FULL),
        name="analyse",
    )(lengths, strength, second, first)


def restore_kernel(lengths, *refs):
    messages, (second, first, basis, cosine, sine, out, coeff, table) = refs[:SHARES], refs[SHARES:]
    channels, local = second.shape
    blocks = local // BLOCK
    me = device_id()
    row_table(lengths, table, me, local, lengths.shape[0])
    lane = lax.broadcasted_iota(jnp.int32, (1, LANES), 1)
    chunk = (lane >> 4) & 3
    coeff[...] = jnp.zeros_like(coeff)
    for slot in range(SHARES):
        value = jnp.zeros((channels, LANES), jnp.float32)
        for share in range(SHARES):
            moved = messages[share][...]
            if slot != share:
                moved = pltpu.roll(moved, ((share - slot) * GROUP) % LANES, 1)
            value = jnp.where(chunk == share, moved, value)
        coeff[slot, :channels, :] = value
    within = lax.broadcasted_iota(jnp.int32, (1, BLOCK), 1)

    def block_value(block, place, slot):
        value = coeff[slot]
        turned = (
            value * cosine[slot, pl.ds(block, 1), :]
            + pltpu.roll(value, PAD, 1) * sine[slot, pl.ds(block, 1), :]
        )
        high = turned.astype(jnp.bfloat16)
        low = (turned - high.astype(jnp.float32)).astype(jnp.bfloat16)
        left = jnp.concatenate([high, low], axis=0)
        left = jnp.concatenate([left, left], axis=1)
        product = jnp.dot(left, basis[slot], preferred_element_type=jnp.float32)
        value = product[:PAD] + product[PAD:]
        kept = second[:, pl.ds(place, BLOCK)] + first[:, pl.ds(place, BLOCK)]
        return kept - value[:channels]

    begin_slot = table[3 * SHARES]
    for block in range(blocks):
        place = block * BLOCK
        slot = begin_slot
        for later in range(1, SHARES):
            slot = slot + jnp.where(table[2 * SHARES + later] <= place, 1, 0)
        out[:, pl.ds(place, BLOCK)] = block_value(block, place, slot & 3)
    for later in range(1, SHARES):
        block, low_end = split_block(table[2 * SHARES + later], blocks)
        place = pl.multiple_of(block * BLOCK, BLOCK)
        value = block_value(block, place, (begin_slot + later) & 3)
        before = out[:, pl.ds(place, BLOCK)]
        out[:, pl.ds(place, BLOCK)] = jnp.where(within >= low_end, value, before)


def restore(lengths, messages, second, first, tables):
    channels, local = second.shape
    return pl.pallas_call(
        restore_kernel,
        out_shape=jax.ShapeDtypeStruct((channels, local), jnp.float32),
        in_specs=[pl.BlockSpec(memory_space=pltpu.SMEM)]
        + [pl.BlockSpec(memory_space=pltpu.VMEM)] * (SHARES + 5),
        out_specs=pl.BlockSpec(memory_space=pltpu.VMEM),
        scratch_shapes=[
            pltpu.VMEM((SHARES, PAD, LANES), jnp.float32),
            pltpu.SMEM((16,), jnp.int32),
        ],
        compiler_params=pltpu.CompilerParams(vmem_limit_bytes=32 * 1024 * 1024),
        name="restore",
    )(lengths, *messages, second, first, *tables)


def fill_tables(table, me, per_device, basis, cosine, sine, blocks):
    fill_phases(table, me, per_device, blocks, cosine, sine, -1.0)
    wave_index = lax.broadcasted_iota(jnp.int32, (LANES, BLOCK), 0)
    point = lax.broadcasted_iota(jnp.int32, (LANES, BLOCK), 1)
    for slot in range(SHARES):
        high, low = basis_of(wave_index, point, table[SHARES + slot], me, per_device)
        basis[slot, :LANES, :] = high
        basis[slot, LANES:, :] = low


def tables_kernel(per_device, local, lengths, basis, cosine, sine, table):
    me = device_id()
    row_table(lengths, table, me, local, lengths.shape[0])
    fill_tables(table, me, per_device, basis, cosine, sine, local // BLOCK)


def table_shapes(local):
    phase_rows = -(-(local // BLOCK) // 8) * 8
    return [
        jax.ShapeDtypeStruct((SHARES, 2 * LANES, BLOCK), jnp.bfloat16),
        jax.ShapeDtypeStruct((SHARES, phase_rows, LANES), jnp.float32),
        jax.ShapeDtypeStruct((SHARES, phase_rows, LANES), jnp.float32),
    ]


def tables_of(lengths, local, per_device):
    return pl.pallas_call(
        functools.partial(tables_kernel, per_device, local),
        out_shape=table_shapes(local),
        in_specs=[pl.BlockSpec(memory_space=pltpu.SMEM)],
        out_specs=[pl.BlockSpec(memory_space=pltpu.VMEM)] * 3,
        scratch_shapes=[pltpu.SMEM((16,), jnp.int32)],
        compiler_params=pltpu.CompilerParams(vmem_limit_bytes=SMALL),
        name="tables",
    )(lengths)


def swapped(value, mask):
    count = lax.axis_size(AXES)
    return lax.ppermute(value, AXES, [(i, i ^ mask) for i in range(count)])


def legendre(latitude, waves):
    order = waves.astype(jnp.float32)[None, :]
    sine = jnp.sqrt(1.0 - latitude * latitude)[:, None]
    place = latitude[:, None]
    diagonal = jnp.full((latitude.shape[0], waves.shape[0]), math.sqrt(0.5), jnp.float32)
    previous = jnp.zeros_like(diagonal)
    current = jnp.zeros_like(diagonal)
    degrees = []
    for degree in range(WAVES):
        if degree:
            diagonal = diagonal * (sine * math.sqrt((2.0 * degree + 1.0) / (2.0 * degree)))
        upper = max(4.0 * degree * degree - 1.0, 0.0)
        below = float(degree - 1) ** 2
        factor_upper = jnp.sqrt(upper / jnp.maximum(float(degree * degree) - order * order, 1.0))
        factor_lower = jnp.sqrt(
            jnp.maximum(below - order * order, 0.0) / max(4.0 * below - 1.0, 1.0)
        )
        value = factor_upper * (place * current - factor_lower * previous)
        value = jnp.where(order > degree, 0.0, jnp.where(order == degree, diagonal, value))
        previous, current = current, value
        degrees.append(value)
    return jnp.stack(degrees, axis=-1)


def middle_general(received, strength, lengths, latitude, weights, local, per_device):
    rows = lengths.shape[0]
    count = lax.axis_size(AXES)
    channels = strength.shape[1]
    me = device_id()
    stops = jnp.cumsum(lengths)
    row_ids = jnp.arange(rows, dtype=jnp.int32)
    slots = jnp.arange(SHARES, dtype=jnp.int32)
    picks = []
    for share in range(SHARES):
        first = jnp.sum((stops <= (me ^ share) * local).astype(jnp.int32))
        held = first + ((slots - first) & 3)
        picks.append((held[:, None] == row_ids[None, :]).astype(jnp.float32))
    total = 0.0
    for pick, message in zip(picks, received):
        total = total + jnp.einsum(
            "gj,fcrgm->jfcrm",
            pick,
            message.reshape(2, channels, 2, SHARES, GROUP),
            precision=HIGHEST,
        )
    mask = SHARES
    while mask < count:
        total = total + swapped(total, mask)
        mask *= 2
    outer = jnp.arange(GROUP, dtype=jnp.int32) // per_device
    waves = per_device * ((me & 3) + SHARES * outer) + jnp.arange(GROUP) % per_device
    values = legendre(latitude, waves)
    gram = jnp.einsum("jmn,kmn->mjk", values, values, precision=HIGHEST)
    scale = jnp.where(waves == 0, 1.0, 2.0)
    rate_first = strength[0][:, None, None]
    both, second = total[:, 0], total[:, 1]
    once = jnp.einsum("mjk,kcrm->jcrm", gram, second, precision=HIGHEST)
    first = both - second - rate_first * weights[:, None, None, None] * once
    back = jnp.einsum("mjk,kcrm->jcrm", gram, first + second, precision=HIGHEST)
    back = back * (weights / lengths.astype(jnp.float32))[:, None, None, None] * scale
    replies = [
        jnp.einsum("gj,jcrm->crgm", pick, back, precision=HIGHEST).reshape(channels, LANES)
        for pick in picks
    ]
    spectrum = jnp.stack([first, second])
    begin = (me // SHARES) * per_device
    spectrum = lax.dynamic_slice_in_dim(spectrum, begin, per_device, 4)
    mine = lax.dynamic_slice_in_dim(values, begin, per_device, 1)
    factor = lax.dynamic_slice_in_dim(scale, begin, per_device, 0)
    factor = factor * (float(local * count) ** -0.5)
    result = jnp.einsum("jmn,sjcrm->scrmn", mine, spectrum, precision=HIGHEST)
    result = result * factor[:, None] * jnp.array([1.0, -1.0])[:, None, None]
    return replies, result


def least(values):
    result = values[0]
    for value in values[1:]:
        result = jnp.minimum(result, value)
    return result


def prepare_kernel(
    per_device, count, local, lengths, latitude, weights, message, coupling, poly, gram, kept, pt, square, sem
):
    copy = pltpu.make_async_copy(message, kept, sem)
    copy.start()
    me = device_id()
    down = lax.broadcasted_iota(jnp.int32, (8, LANES), 0)
    lane = lax.broadcasted_iota(jnp.int32, (8, LANES), 1)
    group = (lane >> 4) & 3
    packed = down >= SHARES
    array = jnp.where(packed, (lane >> 6) * 2 + ((lane >> 3) & 1), down)
    row = SHARES * array + group
    within = lane & (GROUP - 1)
    outer = within >> 3
    order = jnp.where(
        packed, 8 * me + (lane & 7), 8 * ((me & 3) + SHARES * outer) + (lane & 7)
    ).astype(jnp.float32)
    place = jnp.zeros((8, LANES), jnp.float32)
    weight = jnp.zeros((8, LANES), jnp.float32)
    size = jnp.zeros((8, LANES), jnp.int32)
    for index in range(lengths.shape[0]):
        here = row == index
        place = jnp.where(here, latitude[index], place)
        weight = jnp.where(here, weights[index], weight)
        size = jnp.where(here, lengths[index], size)
    doubling = jnp.where(order == 0.0, 1.0, 2.0)
    scale = weight / size.astype(jnp.float32) * doubling
    sine = jnp.sqrt(1.0 - place * place)
    order_square = order * order
    diagonal = jnp.full((8, LANES), math.sqrt(0.5), jnp.float32)
    previous = jnp.zeros((8, LANES), jnp.float32)
    current = previous
    for degree in range(WAVES):
        if degree:
            diagonal = diagonal * (sine * math.sqrt((2.0 * degree + 1.0) / (2.0 * degree)))
        upper = math.sqrt(max(4.0 * degree * degree - 1.0, 0.0))
        below = float(degree - 1) ** 2
        factor_upper = upper * lax.rsqrt(jnp.maximum(float(degree * degree) - order_square, 1.0))
        factor_lower = jnp.sqrt(
            jnp.maximum(below - order_square, 0.0) * (1.0 / max(4.0 * below - 1.0, 1.0))
        )
        value = (factor_upper * place) * current - (factor_upper * factor_lower) * previous
        value = jnp.where(order > degree, 0.0, jnp.where(order == degree, diagonal, value))
        previous, current = current, value
        for index in range(SHARES + 1):
            pt[index, pl.ds(degree, 1), :] = value[index : index + 1, :]
    for step in range(SHARES):
        for source in range(SHARES):
            moved = group_roll(pt[source], step)
            for target in range(SHARES):
                square[target, pl.ds(step * SHARES + source, 1), :] = jnp.sum(
                    pt[target] * moved, axis=0, keepdims=True
                )
    twice = [jnp.zeros((GROUP, LANES), jnp.float32)] * SHARES
    for through in range(SHARES):
        weighted = square[through] * weight[through : through + 1, :]
        for step in range(SHARES):
            moved = group_roll(weighted, step)
            if step:
                moved = jnp.concatenate(
                    [moved[GROUP - SHARES * step :], moved[: GROUP - SHARES * step]], axis=0
                )
            for target in range(SHARES):
                factor = square[target, pl.ds(step * SHARES + through, 1), :]
                twice[target] = twice[target] + factor * moved
    for target in range(SHARES):
        coupling[0, target] = square[target] * scale[target : target + 1, :]
        coupling[1, target] = twice[target] * scale[target : target + 1, :]
    mine = pt[SHARES]
    factor = doubling[SHARES : SHARES + 1, :] * (float(local * count) ** -0.5)
    poly[...] = mine * factor
    for step in range(GROUP):
        moved = pltpu.roll(mine, (LANES - 8 * step) % LANES, 1) if step else mine
        gram[pl.ds(step, 1), :] = weight[SHARES : SHARES + 1, :] * jnp.sum(
            mine * moved, axis=0, keepdims=True
        )
    copy.wait()


SMEM = pl.BlockSpec(memory_space=pltpu.SMEM)
VMEM = pl.BlockSpec(memory_space=pltpu.VMEM)


def floats(*shape):
    return jax.ShapeDtypeStruct(shape, jnp.float32)


def prepare(lengths, latitude, weights, message, per_device, count, local):
    return pl.pallas_call(
        functools.partial(prepare_kernel, per_device, count, local),
        out_shape=[
            floats(2, SHARES, GROUP, LANES),
            floats(WAVES, LANES),
            floats(GROUP, LANES),
            floats(*message.shape),
        ],
        in_specs=[SMEM] * 3 + [pl.BlockSpec(memory_space=pl.ANY)],
        out_specs=[VMEM] * 4,
        scratch_shapes=[
            pltpu.VMEM((SHARES + 1, WAVES, LANES), jnp.float32),
            pltpu.VMEM((SHARES, GROUP, LANES), jnp.float32),
            pltpu.SemaphoreType.DMA,
        ],
        compiler_params=pltpu.CompilerParams(vmem_limit_bytes=SMALL),
        name="prepare",
    )(lengths, latitude, weights, message)


def couple_kernel(local, lengths, strength, coupling, *refs):
    messages, (own, other) = [ref[...] for ref in refs[:SHARES]], refs[SHARES:]
    channels = strength.shape[1]
    me = device_id()
    *firsts, far = first_rows(lengths, near(me) + [(me ^ SHARES) & SHARES], local)
    arrays = by_row(messages, firsts)
    rate_first = column(strength[0:1, :])
    sums = [jnp.zeros((channels, LANES), jnp.float32)] * SHARES
    for source in range(SHARES):
        both = arrays[source][:channels]
        second = rate_first * arrays[source][channels:]
        for step in range(SHARES):
            moved_both = group_roll(both, step)
            moved_second = group_roll(second, step)
            at = pl.ds(step * SHARES + source, 1)
            for target in range(SHARES):
                sums[target] = (
                    sums[target]
                    + coupling[0, target, at, :] * moved_both
                    - coupling[1, target, at, :] * moved_second
                )
    for first, out in ((least(firsts), own), (far, other)):
        begin = row_arrays(first)
        for index in range(WINDOW):
            value = jnp.zeros((channels, LANES), jnp.float32)
            for target in range(SHARES):
                value = jnp.where(begin + index == target, sums[target], value)
            out[pl.ds(index * channels, channels), :] = value


def couple(lengths, strength, coupling, messages, local):
    channels = strength.shape[1]
    return pl.pallas_call(
        functools.partial(couple_kernel, local),
        out_shape=[floats(WINDOW * channels, LANES)] * 2,
        in_specs=[SMEM] + [VMEM] * (2 + SHARES),
        out_specs=[VMEM] * 2,
        compiler_params=pltpu.CompilerParams(vmem_limit_bytes=SMALL),
        name="couple",
    )(lengths, strength, coupling, *messages)


def pack_kernel(per_device, local, lengths, after, *refs):
    messages, (basis, cosine, sine, own, other, table) = (
        [ref[...] for ref in refs[:SHARES]],
        refs[SHARES:],
    )
    rows = messages[0].shape[0]
    me = device_id()
    row_table(lengths, table, me, local, lengths.shape[0])
    fill_tables(table, me, per_device, basis, cosine, sine, local // BLOCK)
    arrays = by_row(messages, first_rows(lengths, near(me), local))
    lane = lax.broadcasted_iota(jnp.int32, (1, LANES), 1)
    array = (lane >> 6) * 2 + ((lane >> 3) & 1)
    upper = me >= SHARES
    for part in range(2):
        halves = []
        for half in range(2):
            value = jnp.zeros((rows, LANES), jnp.float32)
            for index in range(SHARES):
                shift = (64 * (index >> 1) + 8 * (index & 1) - 64 * part - 8 * half) % LANES
                moved = pltpu.roll(arrays[index], shift, 1) if shift else arrays[index]
                value = jnp.where(array == index, moved, value)
            halves.append(value)
        own[pl.ds(part * rows, rows), :] = jnp.where(upper, halves[1], halves[0])
        other[pl.ds(part * rows, rows), :] = jnp.where(upper, halves[0], halves[1])


def pack(lengths, after, messages, local, per_device):
    rows = messages[0].shape[0]
    return pl.pallas_call(
        functools.partial(pack_kernel, per_device, local),
        out_shape=table_shapes(local) + [floats(2 * rows, LANES)] * 2,
        in_specs=[SMEM, pl.BlockSpec(memory_space=pl.ANY)] + [VMEM] * SHARES,
        out_specs=[VMEM] * 5,
        scratch_shapes=[pltpu.SMEM((16,), jnp.int32)],
        compiler_params=pltpu.CompilerParams(vmem_limit_bytes=SMALL),
        name="pack",
    )(lengths, after, *messages)


def hand_out_kernel(local, lengths, own, other, *outs):
    channels = outs[0].shape[0]
    firsts = first_rows(lengths, near(device_id()), local)
    begin = row_arrays(least(firsts))
    sums = []
    for index in range(WINDOW):
        at = pl.ds(index * channels, channels)
        sums.append(own[at, :] + other[at, :])
    for first, out in zip(firsts, outs):
        array = row_arrays(first) - begin
        value = sums[0]
        for index in range(1, WINDOW):
            value = jnp.where(array == index, sums[index], value)
        out[...] = value


def hand_out(lengths, own, other, local):
    channels = own.shape[0] // WINDOW
    return pl.pallas_call(
        functools.partial(hand_out_kernel, local),
        out_shape=[floats(channels, LANES)] * SHARES,
        in_specs=[SMEM] + [VMEM] * 2,
        out_specs=[VMEM] * SHARES,
        compiler_params=pltpu.CompilerParams(vmem_limit_bytes=SMALL),
        name="hand_out",
    )(lengths, own, other)


def spectrum_kernel(strength, own, other, poly, gram, out):
    channels = strength.shape[1]
    rate_first = column(strength[0:1, :])
    down = lax.broadcasted_iota(jnp.int32, (8, LANES), 0)
    lane = lax.broadcasted_iota(jnp.int32, (8, LANES), 1)
    match = jnp.where(down == (lane & 7), 1.0, 0.0)[None]
    high = poly[...].astype(jnp.bfloat16)
    low = (poly[...] - high.astype(jnp.float32)).astype(jnp.bfloat16)
    right = jnp.concatenate(
        [
            jnp.concatenate([high, high], axis=1),
            jnp.concatenate([low, jnp.zeros_like(low)], axis=1),
        ],
        axis=0,
    )
    for part in range(2):
        at = pl.ds(2 * part * channels, channels)
        both = own[at, :] + other[at, :]
        at = pl.ds((2 * part + 1) * channels, channels)
        second = own[at, :] + other[at, :]
        first = both - second
        for step in range(GROUP):
            moved = pltpu.roll(second, (LANES - 8 * step) % LANES, 1) if step else second
            first = first - rate_first * (gram[pl.ds(step, 1), :] * moved)
        for index, value in enumerate((first, second)):
            if part:
                value = -value
            rounded = value.astype(jnp.bfloat16).astype(jnp.float32)
            sides = []
            for side in (rounded, value - rounded):
                spread = side[:, None, :] * match
                sides.append(spread.reshape(8 * channels, LANES).astype(jnp.bfloat16))
            product = lax.dot_general(
                jnp.concatenate(sides, axis=1),
                right,
                (((1,), (1,)), ((), ())),
                preferred_element_type=jnp.float32,
            )
            result = product[:, :WAVES] + product[:, WAVES:]
            out[index, :, part] = result.reshape(channels, 8, WAVES)


def spectrum(strength, own, other, poly, gram):
    channels = strength.shape[1]
    return pl.pallas_call(
        spectrum_kernel,
        out_shape=floats(2, channels, 2, 8, WAVES),
        in_specs=[VMEM] * 5,
        out_specs=VMEM,
        compiler_params=pltpu.CompilerParams(vmem_limit_bytes=SMALL),
        name="spectrum",
    )(strength, own, other, poly, gram)


def middle_small(received, strength, lengths, latitude, weights, local, per_device, count):
    coupling, poly, gram, kept = prepare(
        lengths, latitude, weights, received[0], per_device, count, local
    )
    received = [kept] + received[1:]
    part, sent_part = couple(lengths, strength, coupling, received, local)
    other_part = swapped(sent_part, SHARES)
    *tables, own, sent = pack(lengths, part, received, local, per_device)
    other = swapped(sent, SHARES)
    replies = hand_out(lengths, part, other_part, local)
    return replies, tables, (strength, own, other, poly, gram)


def on_device(cot_first, cot_second, strength, lengths, latitude, weights):
    local = cot_first.shape[1]
    count = lax.axis_size(AXES)
    per_device = WAVES // count
    messages = analyse(lengths, strength, cot_second, cot_first, per_device)
    received = [messages[0]] + [swapped(messages[i], i) for i in range(1, SHARES)]
    arguments = (received, strength, lengths, latitude, weights, local, per_device)
    small = count == 2 * SHARES and lengths.shape[0] == GROUP
    if small:
        replies, tables, pieces = middle_small(*arguments, count)
    else:
        replies, grad_target = middle_general(*arguments)
        tables = tables_of(lengths, local, per_device)
    answers = [replies[0]] + [swapped(replies[i], i) for i in range(1, SHARES)]
    grad_state = restore(lengths, answers, cot_second, cot_first, tables)
    if small:
        grad_target = spectrum(*pieces)
    return (grad_state, grad_target)


def solution(mesh):
    return jax.shard_map(
        on_device,
        mesh=mesh,
        in_specs=(
            P("chan", ("groups", "pts", "lev")),
            P("chan", ("groups", "pts", "lev")),
            P(None, ("groups", "chan")),
            P("groups"),
            P("groups"),
            P("groups"),
        ),
        out_specs=(
            P("chan", ("groups", "pts", "lev")),
            P(None, ("groups", "chan"), None, ("pts", "lev"), None),
        ),
        check_vma=False,
    )
```

```python
import functools
import math

import jax
import jax.numpy as jnp
import numpy as np
from jax import lax
from jax.experimental import pallas as pl
from jax.experimental.pallas import tpu as pltpu
from jax.sharding import PartitionSpec as P

MAXLEN = 3072
WAVES = 64
BLOCK = 256
LANES = 128
SHARES = 4
GROUP = WAVES // SHARES
PAD = 64
FULL = 60 * 1024 * 1024
WINDOW = 3
SMALL = 8 * 1024 * 1024
HIGHEST = lax.Precision.HIGHEST
AXES = ("pts", "lev")


def cosine_coefficients():
    nodes = np.cos(np.pi * (np.arange(64) + 0.5) / 64)
    squares = 0.12525 * (nodes + 1.0)
    fitted = np.polynomial.Polynomial.fit(squares, np.cos(2.0 * np.pi * np.sqrt(squares)), 7)
    return [float(value) for value in fitted.convert().coef]


COSINE = cosine_coefficients()


def cos_turns(turns):
    turns = turns - jnp.floor(turns + 0.5)
    square = turns * turns
    value = jnp.full_like(square, COSINE[-1])
    for coefficient in COSINE[-2::-1]:
        value = value * square + coefficient
    return value


def turns_of(wave, point, size):
    inverse = 1.0 / size
    product = wave * point
    whole = jnp.floor(product * inverse + 0.5)
    return (product - whole * size) * inverse


def lane_waves(lane, me, per_device):
    share = (lane >> 4) & 3
    within = lane & (GROUP - 1)
    shift = per_device.bit_length() - 1
    outer = within >> shift
    return per_device * (((me ^ share) & 3) + SHARES * outer) + (within & (per_device - 1))


def device_id():
    return lax.axis_index("pts") * lax.axis_size("lev") + lax.axis_index("lev")


def row_table(lengths, table, me, local, rows):
    begin = me * local
    for slot in range(SHARES):
        table[slot] = 0
        table[SHARES + slot] = MAXLEN
        table[2 * SHARES + slot] = local

    def step(row, carry):
        start, first = carry
        size = lengths[row]
        stop = start + size
        first = first + jnp.where(stop <= begin, 1, 0)

        @pl.when((stop > begin) & (start < begin + local))
        def _():
            table[row & 3] = start - begin
            table[SHARES + (row & 3)] = size
            table[2 * SHARES + row - first] = start - begin

        return stop, first

    _, first = lax.fori_loop(0, rows, step, (jnp.int32(0), jnp.int32(0)))
    table[3 * SHARES] = first


def fill_phases(table, me, per_device, blocks, cosine, sine, sign):
    rows = cosine.shape[1]
    lane = lax.broadcasted_iota(jnp.int32, (rows, LANES), 1)
    begin = BLOCK * lax.broadcasted_iota(jnp.int32, (rows, LANES), 0)
    wave = lane_waves(lane, me, per_device).astype(jnp.float32)
    signs = jnp.where(lane >= PAD, sign, -sign)
    for slot in range(SHARES):
        size = jnp.full((rows, LANES), table[SHARES + slot], jnp.int32).astype(jnp.float32)
        turns = turns_of(wave, (begin - table[slot]).astype(jnp.float32), size)
        cosine[slot] = cos_turns(turns)
        sine[slot] = cos_turns(turns - 0.25) * signs


def basis_of(wave_index, point, size_int, me, per_device):
    wave = lane_waves(wave_index, me, per_device).astype(jnp.float32)
    size = jnp.full(wave.shape, size_int, jnp.int32).astype(jnp.float32)
    turns = turns_of(wave, point.astype(jnp.float32), size)
    value = cos_turns(turns - jnp.where(wave_index >= PAD, 0.25, 0.0))
    high = value.astype(jnp.bfloat16)
    low = (value - high.astype(jnp.float32)).astype(jnp.bfloat16)
    return high, low


def column(row):
    count = row.shape[1]
    down = lax.broadcasted_iota(jnp.int32, (count, count), 0)
    across = lax.broadcasted_iota(jnp.int32, (count, count), 1)
    return jnp.sum(jnp.where(down == across, row, 0.0), axis=1, keepdims=True)


def group_roll(value, step):
    if step == 0:
        return value
    lane = lax.broadcasted_iota(jnp.int32, (1, LANES), 1)
    near = ((lane >> 4) & 3) < SHARES - step
    return jnp.where(
        near,
        pltpu.roll(value, LANES - GROUP * step, 1),
        pltpu.roll(value, GROUP * (SHARES - step), 1),
    )


def first_rows(lengths, devices, local):
    begins = [device * local for device in devices]

    def step(row, carry):
        stop = carry[0] + lengths[row]
        return (stop,) + tuple(
            first + jnp.where(stop <= begin, 1, 0) for first, begin in zip(carry[1:], begins)
        )

    zero = jnp.int32(0)
    return lax.fori_loop(0, lengths.shape[0], step, (zero,) * (1 + len(devices)), unroll=True)[1:]


def near(me):
    return [me ^ share for share in range(SHARES)]


def row_arrays(first):
    lane = lax.broadcasted_iota(jnp.int32, (1, LANES), 1)
    group = (lane >> 4) & 3
    return (first + ((group - first) & 3)) >> 2


def by_row(messages, firsts):
    held = [row_arrays(first) for first in firsts]
    arrays = []
    for index in range(SHARES):
        value = jnp.zeros(messages[0].shape, jnp.float32)
        for array, message in zip(held, messages):
            value = value + jnp.where(array == index, message, 0.0)
        arrays.append(value)
    return arrays


def split_block(begin, blocks):
    within = begin & (BLOCK - 1)
    return jnp.minimum(begin >> 8, blocks - 1), jnp.where(within == 0, BLOCK, within)


def interleaved(message, upper):
    channels = message.shape[0] // 2
    both, second = message[:channels], message[channels:]
    odd = ((lax.broadcasted_iota(jnp.int32, (1, LANES), 1) >> 3) & 1) == 1
    return jnp.where(
        upper,
        jnp.where(odd, second, pltpu.roll(both, LANES - 8, 1)),
        jnp.where(odd, pltpu.roll(second, 8, 1), both),
    )


def load_fields(second, first, fields, sems):
    copies = [
        pltpu.make_async_copy(source, fields.at[index], sems.at[index])
        for index, source in enumerate((second, first))
    ]
    for copy in copies:
        copy.start()
    return copies


def analyse_kernel(per_device, lengths_held, strength_held, second, first, *refs):
    messages, (across, rates, kept, fields, lengths, strength, basis, cosine, sine, lhs, total, table) = (
        refs[:SHARES],
        refs[SHARES:-3],
    )
    sems, length_sem, strength_sem = refs[-3:]
    channels, local = second.shape
    blocks = local // BLOCK
    length_copy = pltpu.make_async_copy(lengths_held, lengths, length_sem)
    length_copy.start()
    strength_copy = pltpu.make_async_copy(strength_held, strength, strength_sem)
    strength_copy.start()
    copies = load_fields(second, first, fields, sems)
    me = device_id()
    length_copy.wait()
    strength_copy.wait()
    row_table(lengths, table, me, local, lengths.shape[0])
    fill_phases(table, me, per_device, blocks, cosine, sine, 1.0)
    wave_index = lax.broadcasted_iota(jnp.int32, (BLOCK, LANES), 1)
    point = lax.broadcasted_iota(jnp.int32, (BLOCK, LANES), 0)
    for slot in range(SHARES):
        high, low = basis_of(wave_index, point, table[SHARES + slot], me, per_device)
        basis[slot, :, :LANES] = high
        basis[slot, :, LANES:] = low
    total[...] = jnp.zeros_like(total)
    lhs[...] = jnp.zeros_like(lhs)
    within = lax.broadcasted_iota(jnp.int32, (1, BLOCK), 1)

    def add_block(block, place, slot, low_end, high_end, buffer):
        keep = (within >= low_end) & (within < high_end)
        for index in range(2):
            piece = jnp.where(keep, fields[index, :, pl.ds(place, BLOCK)], 0.0)
            high = piece.astype(jnp.bfloat16)
            low = (piece - high.astype(jnp.float32)).astype(jnp.bfloat16)
            lhs[buffer, pl.ds(index * PAD, channels), :] = high
            lhs[buffer, pl.ds((2 + index) * PAD, channels), :] = low
        product = jnp.dot(
            lhs[buffer, : 2 * PAD, :], basis[slot], preferred_element_type=jnp.float32
        )
        value = product[:, :LANES] + product[:, LANES:]
        value = value + jnp.dot(
            lhs[buffer, 2 * PAD :, :], basis[slot, :, :LANES], preferred_element_type=jnp.float32
        )
        turned = (
            value * cosine[slot, pl.ds(block, 1), :]
            + pltpu.roll(value, PAD, 1) * sine[slot, pl.ds(block, 1), :]
        )
        total[slot] = total[slot] + turned

    begin_slot = table[3 * SHARES]
    for copy in copies:
        copy.wait()
    for block in range(blocks):
        place = block * BLOCK
        slot = begin_slot
        for later in range(1, SHARES):
            slot = slot + jnp.where(table[2 * SHARES + later] <= place, 1, 0)
        slot = slot & 3
        add_block(
            block, place, slot, 0, table[slot] + table[SHARES + slot] - place, block % lhs.shape[0]
        )
        at = pl.ds(place, BLOCK)
        kept[:, at] = fields[0, :, at] + fields[1, :, at]
    for later in range(1, SHARES):
        block, low_end = split_block(table[2 * SHARES + later], blocks)
        place = pl.multiple_of(block * BLOCK, BLOCK)
        add_block(block, place, (begin_slot + later) & 3, low_end, BLOCK, later)

    rate_first = column(strength[0:1, :])
    rate_second = column(strength[1:2, :])
    rates[...] = jnp.broadcast_to(rate_first, rates.shape)
    lane = lax.broadcasted_iota(jnp.int32, (1, LANES), 1)
    chunk = (lane >> 4) & 3
    pairs = []
    for slot in range(SHARES):
        value_second = total[slot, :channels, :]
        value_first = total[slot, PAD : PAD + channels, :]
        part_second = rate_second * value_second
        pairs.append((rate_first * (value_first + value_second) + part_second, part_second))
    for share in range(SHARES):
        for which in range(2):
            value = jnp.zeros((channels, LANES), jnp.float32)
            for slot in range(SHARES):
                moved = pairs[slot][which]
                if slot != share:
                    moved = pltpu.roll(moved, ((slot - share) * GROUP) % LANES, 1)
                value = jnp.where(chunk == slot, moved, value)
            messages[share][pl.ds(which * channels, channels), :] = value
        across[pl.ds(share * channels, channels), :] = interleaved(
            messages[share][...], me < SHARES
        )


def in_hbm(*values):
    return [pltpu.with_memory_space_constraint(value, pltpu.HBM) for value in values]


def analyse(lengths, strength, second, first, per_device):
    channels, local = second.shape
    blocks = local // BLOCK
    phase_rows = -(-blocks // 8) * 8
    return pl.pallas_call(
        functools.partial(analyse_kernel, per_device),
        out_shape=[pltpu.VMEM((2 * channels, LANES), jnp.float32)] * SHARES
        + [
            pltpu.VMEM((SHARES * channels, LANES), jnp.float32),
            pltpu.VMEM((channels, LANES), jnp.float32),
            pltpu.VMEM((channels, local), jnp.float32),
        ],
        in_specs=[pl.BlockSpec(memory_space=pltpu.HBM)] * 4,
        out_specs=[pl.BlockSpec(memory_space=pltpu.VMEM)] * (SHARES + 3),
        scratch_shapes=[
            pltpu.VMEM((2, channels, local), jnp.float32),
            pltpu.SMEM(lengths.shape, jnp.int32),
            pltpu.VMEM(strength.shape, jnp.float32),
            pltpu.VMEM((SHARES, BLOCK, 2 * LANES), jnp.bfloat16),
            pltpu.VMEM((SHARES, phase_rows, LANES), jnp.float32),
            pltpu.VMEM((SHARES, phase_rows, LANES), jnp.float32),
            pltpu.VMEM((4, 4 * PAD, BLOCK), jnp.bfloat16),
            pltpu.VMEM((SHARES, 2 * PAD, LANES), jnp.float32),
            pltpu.SMEM((16,), jnp.int32),
            pltpu.SemaphoreType.DMA((2,)),
            pltpu.SemaphoreType.DMA,
            pltpu.SemaphoreType.DMA,
        ],
        compiler_params=pltpu.CompilerParams(vmem_limit_bytes=32 * 1024 * 1024),
        name="analyse",
    )(*in_hbm(lengths, strength, second, first))


def restore_kernel(lengths, *refs):
    messages, (kept, basis, cosine, sine, out, held, coeff, ends, table, sems) = (
        refs[:SHARES],
        refs[SHARES:],
    )
    channels, local = kept.shape
    blocks = local // BLOCK
    pieces = sems.shape[0]
    width = local // pieces
    me = device_id()
    row_table(lengths, table, me, local, lengths.shape[0])
    lane = lax.broadcasted_iota(jnp.int32, (1, LANES), 1)
    chunk = (lane >> 4) & 3
    coeff[...] = jnp.zeros_like(coeff)
    for slot in range(SHARES):
        value = jnp.zeros((channels, LANES), jnp.float32)
        for share in range(SHARES):
            moved = messages[share][...]
            if slot != share:
                moved = pltpu.roll(moved, ((share - slot) * GROUP) % LANES, 1)
            value = jnp.where(chunk == share, moved, value)
        coeff[slot, :channels, :] = value
    within = lax.broadcasted_iota(jnp.int32, (1, BLOCK), 1)

    def block_value(block, slot):
        value = coeff[slot]
        turned = (
            value * cosine[slot, pl.ds(block, 1), :]
            + pltpu.roll(value, PAD, 1) * sine[slot, pl.ds(block, 1), :]
        )
        high = turned.astype(jnp.bfloat16)
        low = (turned - high.astype(jnp.float32)).astype(jnp.bfloat16)
        left = jnp.concatenate([high, low], axis=0)
        left = jnp.concatenate([left, left], axis=1)
        product = jnp.dot(left, basis[slot], preferred_element_type=jnp.float32)
        return product[:channels] + product[PAD : PAD + channels]

    begin_slot = table[3 * SHARES]
    splits = []
    for later in range(1, SHARES):
        block, low_end = split_block(table[2 * SHARES + later], blocks)
        splits.append(jnp.where(low_end < BLOCK, block, blocks))
        ends[later] = block_value(block, (begin_slot + later) & 3)
    copies = []
    for block in range(blocks):
        place = block * BLOCK
        slot = begin_slot
        split = jnp.int32(0)
        for later in range(1, SHARES):
            slot = slot + jnp.where(table[2 * SHARES + later] <= place, 1, 0)
            split = jnp.where(splits[later - 1] == block, later, split)
        slot = slot & 3
        end = table[slot] + table[SHARES + slot] - place
        value = jnp.where(within < end, block_value(block, slot), ends[split])
        held[:, pl.ds(place, BLOCK)] = kept[:, pl.ds(place, BLOCK)] - value
        if (place + BLOCK) % width == 0:
            at = pl.ds(place + BLOCK - width, width)
            copies.append(
                pltpu.make_async_copy(held.at[:, at], out.at[:, at], sems.at[len(copies)])
            )
            copies[-1].start()
    for copy in copies:
        copy.wait()


def restore(lengths, messages, kept, tables):
    channels, local = kept.shape
    pieces = math.gcd(local // BLOCK, 6)
    return pl.pallas_call(
        restore_kernel,
        out_shape=jax.ShapeDtypeStruct((channels, local), jnp.float32),
        in_specs=[pl.BlockSpec(memory_space=pltpu.SMEM)]
        + [pl.BlockSpec(memory_space=pltpu.VMEM)] * (SHARES + 4),
        out_specs=pl.BlockSpec(memory_space=pl.ANY),
        scratch_shapes=[
            pltpu.VMEM((channels, local), jnp.float32),
            pltpu.VMEM((SHARES, PAD, LANES), jnp.float32),
            pltpu.VMEM((SHARES, channels, BLOCK), jnp.float32),
            pltpu.SMEM((16,), jnp.int32),
            pltpu.SemaphoreType.DMA((pieces,)),
        ],
        compiler_params=pltpu.CompilerParams(vmem_limit_bytes=32 * 1024 * 1024),
        name="restore",
    )(lengths, *messages, kept, *tables)


def fill_tables(table, me, per_device, basis, cosine, sine, blocks):
    fill_phases(table, me, per_device, blocks, cosine, sine, -1.0)
    wave_index = lax.broadcasted_iota(jnp.int32, (LANES, BLOCK), 0)
    point = lax.broadcasted_iota(jnp.int32, (LANES, BLOCK), 1)
    for slot in range(SHARES):
        high, low = basis_of(wave_index, point, table[SHARES + slot], me, per_device)
        basis[slot, :LANES, :] = high
        basis[slot, LANES:, :] = low


def tables_kernel(per_device, local, lengths, after, basis, cosine, sine, table):
    me = device_id()
    row_table(lengths, table, me, local, lengths.shape[0])
    fill_tables(table, me, per_device, basis, cosine, sine, local // BLOCK)


def table_shapes(local):
    phase_rows = -(-(local // BLOCK) // 8) * 8
    return [
        jax.ShapeDtypeStruct((SHARES, 2 * LANES, BLOCK), jnp.bfloat16),
        jax.ShapeDtypeStruct((SHARES, phase_rows, LANES), jnp.float32),
        jax.ShapeDtypeStruct((SHARES, phase_rows, LANES), jnp.float32),
    ]


def tables_of(lengths, after, local, per_device):
    return pl.pallas_call(
        functools.partial(tables_kernel, per_device, local),
        out_shape=table_shapes(local),
        in_specs=[pl.BlockSpec(memory_space=pltpu.SMEM), pl.BlockSpec(memory_space=pl.ANY)],
        out_specs=[pl.BlockSpec(memory_space=pltpu.VMEM)] * 3,
        scratch_shapes=[pltpu.SMEM((16,), jnp.int32)],
        compiler_params=pltpu.CompilerParams(vmem_limit_bytes=SMALL),
        name="tables",
    )(lengths, after)


def swapped(value, mask):
    count = lax.axis_size(AXES)
    return lax.ppermute(value, AXES, [(i, i ^ mask) for i in range(count)])


def legendre(latitude, waves):
    order = waves.astype(jnp.float32)[None, :]
    sine = jnp.sqrt(1.0 - latitude * latitude)[:, None]
    place = latitude[:, None]
    diagonal = jnp.full((latitude.shape[0], waves.shape[0]), math.sqrt(0.5), jnp.float32)
    previous = jnp.zeros_like(diagonal)
    current = jnp.zeros_like(diagonal)
    degrees = []
    for degree in range(WAVES):
        if degree:
            diagonal = diagonal * (sine * math.sqrt((2.0 * degree + 1.0) / (2.0 * degree)))
        upper = max(4.0 * degree * degree - 1.0, 0.0)
        below = float(degree - 1) ** 2
        factor_upper = jnp.sqrt(upper / jnp.maximum(float(degree * degree) - order * order, 1.0))
        factor_lower = jnp.sqrt(
            jnp.maximum(below - order * order, 0.0) / max(4.0 * below - 1.0, 1.0)
        )
        value = factor_upper * (place * current - factor_lower * previous)
        value = jnp.where(order > degree, 0.0, jnp.where(order == degree, diagonal, value))
        previous, current = current, value
        degrees.append(value)
    return jnp.stack(degrees, axis=-1)


def middle_general(received, strength, lengths, latitude, weights, local, per_device):
    rows = lengths.shape[0]
    count = lax.axis_size(AXES)
    channels = strength.shape[1]
    me = device_id()
    stops = jnp.cumsum(lengths)
    row_ids = jnp.arange(rows, dtype=jnp.int32)
    slots = jnp.arange(SHARES, dtype=jnp.int32)
    picks = []
    for share in range(SHARES):
        first = jnp.sum((stops <= (me ^ share) * local).astype(jnp.int32))
        held = first + ((slots - first) & 3)
        picks.append((held[:, None] == row_ids[None, :]).astype(jnp.float32))
    total = 0.0
    for pick, message in zip(picks, received):
        total = total + jnp.einsum(
            "gj,fcrgm->jfcrm",
            pick,
            message.reshape(2, channels, 2, SHARES, GROUP),
            precision=HIGHEST,
        )
    mask = SHARES
    while mask < count:
        total = total + swapped(total, mask)
        mask *= 2
    outer = jnp.arange(GROUP, dtype=jnp.int32) // per_device
    waves = per_device * ((me & 3) + SHARES * outer) + jnp.arange(GROUP) % per_device
    values = legendre(latitude, waves)
    gram = jnp.einsum("jmn,kmn->mjk", values, values, precision=HIGHEST)
    scale = jnp.where(waves == 0, 1.0, 2.0)
    rate_first = strength[0][:, None, None]
    both, second = total[:, 0], total[:, 1]
    once = jnp.einsum("mjk,kcrm->jcrm", gram, second, precision=HIGHEST)
    first = both - second - rate_first * weights[:, None, None, None] * once
    back = jnp.einsum("mjk,kcrm->jcrm", gram, first + second, precision=HIGHEST)
    back = back * (weights / lengths.astype(jnp.float32))[:, None, None, None] * scale
    replies = [
        jnp.einsum("gj,jcrm->crgm", pick, back, precision=HIGHEST).reshape(channels, LANES)
        for pick in picks
    ]
    spectrum = jnp.stack([first, second])
    begin = (me // SHARES) * per_device
    spectrum = lax.dynamic_slice_in_dim(spectrum, begin, per_device, 4)
    mine = lax.dynamic_slice_in_dim(values, begin, per_device, 1)
    factor = lax.dynamic_slice_in_dim(scale, begin, per_device, 0)
    factor = factor * (float(local * count) ** -0.5)
    result = jnp.einsum("jmn,sjcrm->scrmn", mine, spectrum, precision=HIGHEST)
    result = result * factor[:, None] * jnp.array([1.0, -1.0])[:, None, None]
    return replies, result


def least(values):
    result = values[0]
    for value in values[1:]:
        result = jnp.minimum(result, value)
    return result


def prepare_kernel(
    count, local, lengths, latitude, weights, coupling, poly, gram, pt, square
):
    me = device_id()
    down = lax.broadcasted_iota(jnp.int32, (8, LANES), 0)
    lane = lax.broadcasted_iota(jnp.int32, (8, LANES), 1)
    group = (lane >> 4) & 3
    packed = down >= SHARES
    array = jnp.where(packed, (lane >> 6) * 2 + ((lane >> 3) & 1), down)
    row = SHARES * array + group
    within = lane & (GROUP - 1)
    outer = within >> 3
    order = jnp.where(
        packed, 8 * me + (lane & 7), 8 * ((me & 3) + SHARES * outer) + (lane & 7)
    ).astype(jnp.float32)
    place = jnp.zeros((8, LANES), jnp.float32)
    weight = jnp.zeros((8, LANES), jnp.float32)
    size = jnp.zeros((8, LANES), jnp.int32)
    for index in range(lengths.shape[0]):
        here = row == index
        place = jnp.where(here, latitude[index], place)
        weight = jnp.where(here, weights[index], weight)
        size = jnp.where(here, lengths[index], size)
    doubling = jnp.where(order == 0.0, 1.0, 2.0)
    scale = weight / size.astype(jnp.float32) * doubling
    sine = jnp.sqrt(1.0 - place * place)
    order_square = order * order
    diagonal = jnp.full((8, LANES), math.sqrt(0.5), jnp.float32)
    previous = jnp.zeros((8, LANES), jnp.float32)
    current = previous
    for degree in range(WAVES):
        if degree:
            diagonal = diagonal * (sine * math.sqrt((2.0 * degree + 1.0) / (2.0 * degree)))
        upper = math.sqrt(max(4.0 * degree * degree - 1.0, 0.0))
        below = float(degree - 1) ** 2
        factor_upper = upper * lax.rsqrt(jnp.maximum(float(degree * degree) - order_square, 1.0))
        factor_lower = jnp.sqrt(
            jnp.maximum(below - order_square, 0.0) * (1.0 / max(4.0 * below - 1.0, 1.0))
        )
        value = (factor_upper * place) * current - (factor_upper * factor_lower) * previous
        value = jnp.where(order > degree, 0.0, jnp.where(order == degree, diagonal, value))
        previous, current = current, value
        for index in range(SHARES + 1):
            pt[index, pl.ds(degree, 1), :] = value[index : index + 1, :]
    for step in range(SHARES):
        for source in range(SHARES):
            moved = group_roll(pt[source], step)
            for target in range(SHARES):
                square[target, pl.ds(step * SHARES + source, 1), :] = jnp.sum(
                    pt[target] * moved, axis=0, keepdims=True
                )
    twice = [jnp.zeros((GROUP, LANES), jnp.float32)] * SHARES
    for through in range(SHARES):
        weighted = square[through] * weight[through : through + 1, :]
        for step in range(SHARES):
            moved = group_roll(weighted, step)
            if step:
                moved = jnp.concatenate(
                    [moved[GROUP - SHARES * step :], moved[: GROUP - SHARES * step]], axis=0
                )
            for target in range(SHARES):
                factor = square[target, pl.ds(step * SHARES + through, 1), :]
                twice[target] = twice[target] + factor * moved
    for target in range(SHARES):
        coupling[0, target] = square[target] * scale[target : target + 1, :]
        coupling[1, target] = twice[target] * scale[target : target + 1, :]
    mine = pt[SHARES]
    factor = doubling[SHARES : SHARES + 1, :] * (float(local * count) ** -0.5)
    products = lax.dot_general(
        mine, mine, (((0,), (0,)), ((), ())), precision=HIGHEST, preferred_element_type=jnp.float32
    )
    same = (lax.broadcasted_iota(jnp.int32, (LANES, LANES), 0) & 7) == (
        lax.broadcasted_iota(jnp.int32, (LANES, LANES), 1) & 7
    )
    products = jnp.where(same, products * weight[SHARES : SHARES + 1, :], 0.0)
    turned = jnp.concatenate([mine * factor, jnp.zeros_like(mine)], axis=0).T
    for value, out in ((turned, poly), (products, gram)):
        high = value.astype(jnp.bfloat16)
        low = (value - high.astype(jnp.float32)).astype(jnp.bfloat16)
        out[...] = jnp.concatenate([high, high, low], axis=0)


def three_parts(value):
    rounded = value.astype(jnp.bfloat16).astype(jnp.float32)
    return [rounded, value - rounded, rounded]


SMEM = pl.BlockSpec(memory_space=pltpu.SMEM)
VMEM = pl.BlockSpec(memory_space=pltpu.VMEM)


def floats(*shape):
    return jax.ShapeDtypeStruct(shape, jnp.float32)


def prepare(lengths, latitude, weights, count, local):
    return pl.pallas_call(
        functools.partial(prepare_kernel, count, local),
        out_shape=[
            floats(2, SHARES, GROUP, LANES),
            jax.ShapeDtypeStruct((3 * LANES, LANES), jnp.bfloat16),
            jax.ShapeDtypeStruct((3 * LANES, LANES), jnp.bfloat16),
        ],
        in_specs=[SMEM] * 3,
        out_specs=[VMEM] * 3,
        scratch_shapes=[
            pltpu.VMEM((SHARES + 1, WAVES, LANES), jnp.float32),
            pltpu.VMEM((SHARES, GROUP, LANES), jnp.float32),
        ],
        compiler_params=pltpu.CompilerParams(vmem_limit_bytes=SMALL),
        name="prepare",
    )(lengths, latitude, weights)


def couple_kernel(local, lengths, rates, coupling, *refs):
    messages, (own, other) = [ref[...] for ref in refs[:SHARES]], refs[SHARES:]
    channels = rates.shape[0]
    me = device_id()
    *firsts, far = first_rows(lengths, near(me) + [(me ^ SHARES) & SHARES], local)
    arrays = by_row(messages, firsts)
    sums = [jnp.zeros((channels, LANES), jnp.float32)] * SHARES
    for source in range(SHARES):
        both = arrays[source][:channels]
        second = rates[...] * arrays[source][channels:]
        for step in range(SHARES):
            moved_both = group_roll(both, step)
            moved_second = group_roll(second, step)
            at = pl.ds(step * SHARES + source, 1)
            for target in range(SHARES):
                sums[target] = (
                    sums[target]
                    + coupling[0, target, at, :] * moved_both
                    - coupling[1, target, at, :] * moved_second
                )
    for first, out in ((least(firsts), own), (far, other)):
        begin = row_arrays(first)
        for index in range(WINDOW):
            value = jnp.zeros((channels, LANES), jnp.float32)
            for target in range(SHARES):
                value = jnp.where(begin + index == target, sums[target], value)
            out[pl.ds(index * channels, channels), :] = value


def couple(lengths, rates, coupling, messages, local):
    channels = rates.shape[0]
    return pl.pallas_call(
        functools.partial(couple_kernel, local),
        out_shape=[floats(WINDOW * channels, LANES)] * 2,
        in_specs=[SMEM] + [VMEM] * (2 + SHARES),
        out_specs=[VMEM] * 2,
        compiler_params=pltpu.CompilerParams(vmem_limit_bytes=SMALL),
        name="couple",
    )(lengths, rates, coupling, *messages)


def pack_kernel(local, lengths, after, *refs):
    messages, (across, rows, *chunks) = [ref[...] for ref in refs[:SHARES]], refs[SHARES:]
    channels = messages[0].shape[0] // 2
    me = device_id()
    for share in range(SHARES):
        chunks[share][...] = across[pl.ds(share * channels, channels), :]
    arrays = by_row(
        [interleaved(message, me >= SHARES) for message in messages],
        first_rows(lengths, near(me), local),
    )
    for index in range(SHARES):
        rows[pl.ds(index * channels, channels), :] = arrays[index]


def pack(lengths, after, messages, across, local):
    channels = messages[0].shape[0] // 2
    return pl.pallas_call(
        functools.partial(pack_kernel, local),
        out_shape=[floats(SHARES * channels, LANES)] + [floats(channels, LANES)] * SHARES,
        in_specs=[SMEM, pl.BlockSpec(memory_space=pl.ANY)] + [VMEM] * (SHARES + 1),
        out_specs=[VMEM] * (SHARES + 1),
        compiler_params=pltpu.CompilerParams(vmem_limit_bytes=SMALL),
        name="pack",
    )(lengths, after, *messages, across)


def hand_out_kernel(local, lengths, own, other, *outs):
    channels = outs[0].shape[0]
    firsts = first_rows(lengths, near(device_id()), local)
    begin = row_arrays(least(firsts))
    sums = []
    for index in range(WINDOW):
        at = pl.ds(index * channels, channels)
        sums.append(own[at, :] + other[at, :])
    for first, out in zip(firsts, outs):
        array = row_arrays(first) - begin
        value = sums[0]
        for index in range(1, WINDOW):
            value = jnp.where(array == index, sums[index], value)
        out[...] = value


def hand_out(lengths, own, other, local):
    channels = own.shape[0] // WINDOW
    return pl.pallas_call(
        functools.partial(hand_out_kernel, local),
        out_shape=[floats(channels, LANES)] * SHARES,
        in_specs=[SMEM] + [VMEM] * 2,
        out_specs=[VMEM] * SHARES,
        compiler_params=pltpu.CompilerParams(vmem_limit_bytes=SMALL),
        name="hand_out",
    )(lengths, own, other)


def spectrum_kernel(local, lengths, rates, rows, *refs):
    chunks, (poly, gram, out) = [ref[...] for ref in refs[:SHARES]], refs[SHARES:]
    channels = rates.shape[0]
    far = [device ^ SHARES for device in near(device_id())]
    arrays = by_row(chunks, first_rows(lengths, far, local))
    for index in range(SHARES):
        arrays[index] = arrays[index] + rows[pl.ds(index * channels, channels), :]
    across = lax.broadcasted_iota(jnp.int32, (1, LANES), 1)
    held = (across >> 6) * 2 + ((across >> 3) & 1)

    def by_lane(part, field):
        value = jnp.zeros((channels, LANES), jnp.float32)
        for index in range(SHARES):
            shift = (64 * (index >> 1) + 8 * (index & 1) - 64 * part - 8 * field) % LANES
            moved = pltpu.roll(arrays[index], shift, 1) if shift else arrays[index]
            value = jnp.where(held == index, moved, value)
        return value

    down = lax.broadcasted_iota(jnp.int32, (8, LANES), 0)
    lane = lax.broadcasted_iota(jnp.int32, (8, LANES), 1)
    match = jnp.where(down == (lane & 7), 1.0, 0.0)[None]
    for part in range(2):
        second = by_lane(part, 1)
        left = jnp.concatenate([side.astype(jnp.bfloat16) for side in three_parts(second)], axis=1)
        first = by_lane(part, 0) - second
        first = first - rates[...] * jnp.dot(left, gram[...], preferred_element_type=jnp.float32)
        for index, value in enumerate((first, second)):
            if part:
                value = -value
            high, low, _ = three_parts(value)
            sides = [
                (side[:, None, :] * match).reshape(8 * channels, LANES).astype(jnp.bfloat16)
                for side in (high, low)
            ]
            product = jnp.dot(
                jnp.concatenate(sides + sides[:1], axis=1),
                poly[...],
                preferred_element_type=jnp.float32,
            )
            out[index, :, part] = product[:, :WAVES].reshape(channels, 8, WAVES)


def spectrum(lengths, rates, rows, chunks, poly, gram, local):
    channels = rates.shape[0]
    return pl.pallas_call(
        functools.partial(spectrum_kernel, local),
        out_shape=floats(2, channels, 2, 8, WAVES),
        in_specs=[SMEM] + [VMEM] * (SHARES + 4),
        out_specs=VMEM,
        compiler_params=pltpu.CompilerParams(vmem_limit_bytes=SMALL),
        name="spectrum",
    )(lengths, rates, rows, *chunks, poly, gram)


def middle_small(
    received, across, rates, lengths, latitude, weights, local, per_device, count
):
    across = swapped(across, SHARES)
    coupling, poly, gram = prepare(lengths, latitude, weights, count, local)
    part, sent_part = couple(lengths, rates, coupling, received, local)
    other_part = swapped(sent_part, SHARES)
    tables = tables_of(lengths, part, local, per_device)
    rows, *chunks = pack(lengths, tables[1], received, across, local)
    chunks = [chunks[0]] + [swapped(chunks[i], i) for i in range(1, SHARES)]
    replies = hand_out(lengths, part, other_part, local)
    return replies, tables, (lengths, rates, rows, chunks, poly, gram, local)


def on_device(cot_first, cot_second, strength, lengths, latitude, weights):
    local = cot_first.shape[1]
    count = lax.axis_size(AXES)
    per_device = WAVES // count
    *messages, across, rates, kept = analyse(lengths, strength, cot_second, cot_first, per_device)
    received = [messages[0]] + [swapped(messages[i], i) for i in range(1, SHARES)]
    arguments = (lengths, latitude, weights, local, per_device)
    small = count == 2 * SHARES and lengths.shape[0] == GROUP
    if small:
        replies, tables, pieces = middle_small(received, across, rates, *arguments, count)
    else:
        replies, grad_target = middle_general(received, strength, *arguments)
        tables = tables_of(lengths, replies[0], local, per_device)
    answers = [replies[0]] + [swapped(replies[i], i) for i in range(1, SHARES)]
    grad_state = restore(lengths, answers, kept, tables)
    if small:
        grad_target = spectrum(*pieces)
    return (grad_state, grad_target)


def solution(mesh):
    return jax.shard_map(
        on_device,
        mesh=mesh,
        in_specs=(
            P("chan", ("groups", "pts", "lev")),
            P("chan", ("groups", "pts", "lev")),
            P(None, ("groups", "chan")),
            P("groups"),
            P("groups"),
            P("groups"),
        ),
        out_specs=(
            P("chan", ("groups", "pts", "lev")),
            P(None, ("groups", "chan"), None, ("pts", "lev"), None),
        ),
        check_vma=False,
    )
```

```python
import functools
import math

import jax
import jax.numpy as jnp
import numpy as np
from jax import lax
from jax.experimental import pallas as pl
from jax.experimental.pallas import tpu as pltpu
from jax.sharding import PartitionSpec as P

MAXLEN = 3072
WAVES = 64
BLOCK = 256
LANES = 128
SHARES = 4
GROUP = WAVES // SHARES
ORDER = (0, 2, 3, 1)
PAD = 64
FULL = 60 * 1024 * 1024
WINDOW = 3
SMALL = 8 * 1024 * 1024
HIGHEST = lax.Precision.HIGHEST
AXES = ("pts", "lev")


def cosine_coefficients():
    nodes = np.cos(np.pi * (np.arange(64) + 0.5) / 64)
    squares = 0.12525 * (nodes + 1.0)
    fitted = np.polynomial.Polynomial.fit(squares, np.cos(2.0 * np.pi * np.sqrt(squares)), 7)
    return [float(value) for value in fitted.convert().coef]


COSINE = cosine_coefficients()


def cos_turns(turns):
    turns = turns - jnp.floor(turns + 0.5)
    square = turns * turns
    value = jnp.full_like(square, COSINE[-1])
    for coefficient in COSINE[-2::-1]:
        value = value * square + coefficient
    return value


def turns_of(wave, point, size):
    inverse = 1.0 / size
    product = wave * point
    whole = jnp.floor(product * inverse + 0.5)
    return (product - whole * size) * inverse


def lane_waves(lane, me, per_device):
    share = (lane >> 4) & 3
    within = lane & (GROUP - 1)
    shift = per_device.bit_length() - 1
    outer = within >> shift
    return per_device * (((me ^ share) & 3) + SHARES * outer) + (within & (per_device - 1))


def device_id():
    return lax.axis_index("pts") * lax.axis_size("lev") + lax.axis_index("lev")


def row_table(lengths, table, me, local, rows):
    begin = me * local
    for slot in range(SHARES):
        table[slot] = 0
        table[SHARES + slot] = MAXLEN
        table[2 * SHARES + slot] = local

    def step(row, carry):
        start, first = carry
        size = lengths[row]
        stop = start + size
        first = first + jnp.where(stop <= begin, 1, 0)

        @pl.when((stop > begin) & (start < begin + local))
        def _():
            table[row & 3] = start - begin
            table[SHARES + (row & 3)] = size
            table[2 * SHARES + row - first] = start - begin

        return stop, first

    _, first = lax.fori_loop(0, rows, step, (jnp.int32(0), jnp.int32(0)))
    table[3 * SHARES] = first


def fill_phases(table, me, per_device, blocks, cosine, sine, sign):
    rows = cosine.shape[1]
    lane = lax.broadcasted_iota(jnp.int32, (rows, LANES), 1)
    begin = BLOCK * lax.broadcasted_iota(jnp.int32, (rows, LANES), 0)
    wave = lane_waves(lane, me, per_device).astype(jnp.float32)
    signs = jnp.where(lane >= PAD, sign, -sign)
    for slot in range(SHARES):
        size = jnp.full((rows, LANES), table[SHARES + slot], jnp.int32).astype(jnp.float32)
        turns = turns_of(wave, (begin - table[slot]).astype(jnp.float32), size)
        cosine[slot] = cos_turns(turns)
        sine[slot] = cos_turns(turns - 0.25) * signs


def basis_of(wave_index, point, size_int, me, per_device):
    wave = lane_waves(wave_index, me, per_device).astype(jnp.float32)
    size = jnp.full(wave.shape, size_int, jnp.int32).astype(jnp.float32)
    turns = turns_of(wave, point.astype(jnp.float32), size)
    value = cos_turns(turns - jnp.where(wave_index >= PAD, 0.25, 0.0))
    high = value.astype(jnp.bfloat16)
    low = (value - high.astype(jnp.float32)).astype(jnp.bfloat16)
    return high, low


def column(row):
    count = row.shape[1]
    down = lax.broadcasted_iota(jnp.int32, (count, count), 0)
    across = lax.broadcasted_iota(jnp.int32, (count, count), 1)
    return jnp.sum(jnp.where(down == across, row, 0.0), axis=1, keepdims=True)


def group_roll(value, step):
    if step == 0:
        return value
    lane = lax.broadcasted_iota(jnp.int32, (1, LANES), 1)
    near = ((lane >> 4) & 3) < SHARES - step
    return jnp.where(
        near,
        pltpu.roll(value, LANES - GROUP * step, 1),
        pltpu.roll(value, GROUP * (SHARES - step), 1),
    )


def first_rows(lengths, devices, local):
    begins = [device * local for device in devices]

    def step(row, carry):
        stop = carry[0] + lengths[row]
        return (stop,) + tuple(
            first + jnp.where(stop <= begin, 1, 0) for first, begin in zip(carry[1:], begins)
        )

    zero = jnp.int32(0)
    return lax.fori_loop(0, lengths.shape[0], step, (zero,) * (1 + len(devices)), unroll=True)[1:]


def near(me):
    return [me ^ share for share in ORDER]


def row_arrays(first):
    lane = lax.broadcasted_iota(jnp.int32, (1, LANES), 1)
    group = (lane >> 4) & 3
    return (first + ((group - first) & 3)) >> 2


def by_row(messages, firsts):
    held = [row_arrays(first) for first in firsts]
    arrays = []
    for index in range(SHARES):
        value = jnp.zeros(messages[0].shape, jnp.float32)
        for array, message in zip(held, messages):
            value = value + jnp.where(array == index, message, 0.0)
        arrays.append(value)
    return arrays


def split_block(begin, blocks):
    within = begin & (BLOCK - 1)
    return jnp.minimum(begin >> 8, blocks - 1), jnp.where(within == 0, BLOCK, within)


def interleaved(message, upper):
    channels = message.shape[0] // 2
    both, second = message[:channels], message[channels:]
    odd = ((lax.broadcasted_iota(jnp.int32, (1, LANES), 1) >> 3) & 1) == 1
    return jnp.where(
        upper,
        jnp.where(odd, second, pltpu.roll(both, LANES - 8, 1)),
        jnp.where(odd, pltpu.roll(second, 8, 1), both),
    )


def load_fields(second, first, fields, sems):
    copies = [
        pltpu.make_async_copy(source, fields.at[index], sems.at[index])
        for index, source in enumerate((second, first))
    ]
    for copy in copies:
        copy.start()
    return copies


def analyse_kernel(per_device, lengths_held, strength_held, second, first, *refs):
    messages, (across, rates, kept, fields, lengths, strength, basis, cosine, sine, lhs, total, table) = (
        refs[:SHARES],
        refs[SHARES:-3],
    )
    sems, length_sem, strength_sem = refs[-3:]
    channels, local = second.shape
    blocks = local // BLOCK
    length_copy = pltpu.make_async_copy(lengths_held, lengths, length_sem)
    length_copy.start()
    strength_copy = pltpu.make_async_copy(strength_held, strength, strength_sem)
    strength_copy.start()
    copies = load_fields(second, first, fields, sems)
    me = device_id()
    length_copy.wait()
    strength_copy.wait()
    row_table(lengths, table, me, local, lengths.shape[0])
    fill_phases(table, me, per_device, blocks, cosine, sine, 1.0)
    wave_index = lax.broadcasted_iota(jnp.int32, (BLOCK, LANES), 1)
    point = lax.broadcasted_iota(jnp.int32, (BLOCK, LANES), 0)
    for slot in range(SHARES):
        high, low = basis_of(wave_index, point, table[SHARES + slot], me, per_device)
        basis[slot, :, :LANES] = high
        basis[slot, :, LANES:] = low
    total[...] = jnp.zeros_like(total)
    lhs[...] = jnp.zeros_like(lhs)
    within = lax.broadcasted_iota(jnp.int32, (1, BLOCK), 1)

    def add_block(block, place, slot, low_end, high_end, buffer):
        keep = (within >= low_end) & (within < high_end)
        for index in range(2):
            piece = jnp.where(keep, fields[index, :, pl.ds(place, BLOCK)], 0.0)
            high = piece.astype(jnp.bfloat16)
            low = (piece - high.astype(jnp.float32)).astype(jnp.bfloat16)
            lhs[buffer, pl.ds(index * PAD, channels), :] = high
            lhs[buffer, pl.ds((2 + index) * PAD, channels), :] = low
        product = jnp.dot(
            lhs[buffer, : 2 * PAD, :], basis[slot], preferred_element_type=jnp.float32
        )
        value = product[:, :LANES] + product[:, LANES:]
        value = value + jnp.dot(
            lhs[buffer, 2 * PAD :, :], basis[slot, :, :LANES], preferred_element_type=jnp.float32
        )
        turned = (
            value * cosine[slot, pl.ds(block, 1), :]
            + pltpu.roll(value, PAD, 1) * sine[slot, pl.ds(block, 1), :]
        )
        total[slot] = total[slot] + turned

    begin_slot = table[3 * SHARES]
    for copy in copies:
        copy.wait()
    for block in range(blocks):
        place = block * BLOCK
        slot = begin_slot
        for later in range(1, SHARES):
            slot = slot + jnp.where(table[2 * SHARES + later] <= place, 1, 0)
        slot = slot & 3
        add_block(
            block, place, slot, 0, table[slot] + table[SHARES + slot] - place, block % lhs.shape[0]
        )
        at = pl.ds(place, BLOCK)
        kept[:, at] = fields[0, :, at] + fields[1, :, at]
    for later in range(1, SHARES):
        block, low_end = split_block(table[2 * SHARES + later], blocks)
        place = pl.multiple_of(block * BLOCK, BLOCK)
        add_block(block, place, (begin_slot + later) & 3, low_end, BLOCK, later)

    rate_first = column(strength[0:1, :])
    rate_second = column(strength[1:2, :])
    rates[...] = jnp.broadcast_to(rate_first, rates.shape)
    lane = lax.broadcasted_iota(jnp.int32, (1, LANES), 1)
    chunk = (lane >> 4) & 3
    pairs = []
    for slot in range(SHARES):
        value_second = total[slot, :channels, :]
        value_first = total[slot, PAD : PAD + channels, :]
        part_second = rate_second * value_second
        pairs.append((rate_first * (value_first + value_second) + part_second, part_second))
    for share in range(SHARES):
        for which in range(2):
            value = jnp.zeros((channels, LANES), jnp.float32)
            for slot in range(SHARES):
                moved = pairs[slot][which]
                if slot != share:
                    moved = pltpu.roll(moved, ((slot - share) * GROUP) % LANES, 1)
                value = jnp.where(chunk == slot, moved, value)
            message = messages[ORDER.index(share)]
            message[pl.ds(which * channels, channels), :] = value
        across[pl.ds(share * channels, channels), :] = interleaved(message[...], me < SHARES)


def in_hbm(*values):
    return [pltpu.with_memory_space_constraint(value, pltpu.HBM) for value in values]


def analyse(lengths, strength, second, first, per_device):
    channels, local = second.shape
    blocks = local // BLOCK
    phase_rows = -(-blocks // 8) * 8
    return pl.pallas_call(
        functools.partial(analyse_kernel, per_device),
        out_shape=[pltpu.VMEM((2 * channels, LANES), jnp.float32)] * SHARES
        + [
            pltpu.VMEM((SHARES * channels, LANES), jnp.float32),
            pltpu.VMEM((channels, LANES), jnp.float32),
            pltpu.VMEM((channels, local), jnp.float32),
        ],
        in_specs=[pl.BlockSpec(memory_space=pltpu.HBM)] * 4,
        out_specs=[pl.BlockSpec(memory_space=pltpu.VMEM)] * (SHARES + 3),
        scratch_shapes=[
            pltpu.VMEM((2, channels, local), jnp.float32),
            pltpu.SMEM(lengths.shape, jnp.int32),
            pltpu.VMEM(strength.shape, jnp.float32),
            pltpu.VMEM((SHARES, BLOCK, 2 * LANES), jnp.bfloat16),
            pltpu.VMEM((SHARES, phase_rows, LANES), jnp.float32),
            pltpu.VMEM((SHARES, phase_rows, LANES), jnp.float32),
            pltpu.VMEM((4, 4 * PAD, BLOCK), jnp.bfloat16),
            pltpu.VMEM((SHARES, 2 * PAD, LANES), jnp.float32),
            pltpu.SMEM((16,), jnp.int32),
            pltpu.SemaphoreType.DMA((2,)),
            pltpu.SemaphoreType.DMA,
            pltpu.SemaphoreType.DMA,
        ],
        compiler_params=pltpu.CompilerParams(vmem_limit_bytes=32 * 1024 * 1024),
        name="analyse",
    )(*in_hbm(lengths, strength, second, first))


def restore_kernel(lengths, *refs):
    messages, (kept, basis, cosine, sine, spectra, out, spectra_out, held, coeff, ends, table) = (
        refs[:SHARES],
        refs[SHARES:-2],
    )
    sems, spectra_sem = refs[-2:]
    spectra_copy = pltpu.make_async_copy(spectra, spectra_out, spectra_sem)
    spectra_copy.start()
    channels, local = kept.shape
    blocks = local // BLOCK
    pieces = sems.shape[0]
    width = local // pieces
    me = device_id()
    row_table(lengths, table, me, local, lengths.shape[0])
    lane = lax.broadcasted_iota(jnp.int32, (1, LANES), 1)
    chunk = (lane >> 4) & 3
    coeff[...] = jnp.zeros_like(coeff)
    for slot in range(SHARES):
        value = jnp.zeros((channels, LANES), jnp.float32)
        for share in range(SHARES):
            moved = messages[ORDER.index(share)][...]
            if slot != share:
                moved = pltpu.roll(moved, ((share - slot) * GROUP) % LANES, 1)
            value = jnp.where(chunk == share, moved, value)
        coeff[slot, :channels, :] = value
    within = lax.broadcasted_iota(jnp.int32, (1, BLOCK), 1)

    def block_value(block, slot):
        value = coeff[slot]
        turned = (
            value * cosine[slot, pl.ds(block, 1), :]
            + pltpu.roll(value, PAD, 1) * sine[slot, pl.ds(block, 1), :]
        )
        high = turned.astype(jnp.bfloat16)
        low = (turned - high.astype(jnp.float32)).astype(jnp.bfloat16)
        left = jnp.concatenate([high, low], axis=0)
        left = jnp.concatenate([left, left], axis=1)
        product = jnp.dot(left, basis[slot], preferred_element_type=jnp.float32)
        return product[:channels] + product[PAD : PAD + channels]

    begin_slot = table[3 * SHARES]
    splits = []
    for later in range(1, SHARES):
        block, low_end = split_block(table[2 * SHARES + later], blocks)
        splits.append(jnp.where(low_end < BLOCK, block, blocks))
        ends[later] = block_value(block, (begin_slot + later) & 3)
    copies = []
    for block in range(blocks):
        place = block * BLOCK
        slot = begin_slot
        split = jnp.int32(0)
        for later in range(1, SHARES):
            slot = slot + jnp.where(table[2 * SHARES + later] <= place, 1, 0)
            split = jnp.where(splits[later - 1] == block, later, split)
        slot = slot & 3
        end = table[slot] + table[SHARES + slot] - place
        value = jnp.where(within < end, block_value(block, slot), ends[split])
        held[:, pl.ds(place, BLOCK)] = kept[:, pl.ds(place, BLOCK)] - value
        if (place + BLOCK) % width == 0:
            at = pl.ds(place + BLOCK - width, width)
            copies.append(
                pltpu.make_async_copy(held.at[:, at], out.at[:, at], sems.at[len(copies)])
            )
            copies[-1].start()
    for copy in copies:
        copy.wait()
    spectra_copy.wait()


def restore(lengths, messages, kept, tables, spectra):
    channels, local = kept.shape
    pieces = math.gcd(local // BLOCK, 6)
    return pl.pallas_call(
        restore_kernel,
        out_shape=[
            jax.ShapeDtypeStruct((channels, local), jnp.float32),
            jax.ShapeDtypeStruct(spectra.shape, jnp.float32),
        ],
        in_specs=[pl.BlockSpec(memory_space=pltpu.SMEM)]
        + [pl.BlockSpec(memory_space=pltpu.VMEM)] * (SHARES + 5),
        out_specs=[pl.BlockSpec(memory_space=pl.ANY)] * 2,
        scratch_shapes=[
            pltpu.VMEM((channels, local), jnp.float32),
            pltpu.VMEM((SHARES, PAD, LANES), jnp.float32),
            pltpu.VMEM((SHARES, channels, BLOCK), jnp.float32),
            pltpu.SMEM((16,), jnp.int32),
            pltpu.SemaphoreType.DMA((pieces,)),
            pltpu.SemaphoreType.DMA,
        ],
        compiler_params=pltpu.CompilerParams(vmem_limit_bytes=32 * 1024 * 1024),
        name="restore",
    )(lengths, *messages, kept, *tables, spectra)


def fill_tables(table, me, per_device, basis, cosine, sine, blocks):
    fill_phases(table, me, per_device, blocks, cosine, sine, -1.0)
    wave_index = lax.broadcasted_iota(jnp.int32, (LANES, BLOCK), 0)
    point = lax.broadcasted_iota(jnp.int32, (LANES, BLOCK), 1)
    for slot in range(SHARES):
        high, low = basis_of(wave_index, point, table[SHARES + slot], me, per_device)
        basis[slot, :LANES, :] = high
        basis[slot, LANES:, :] = low


def tables_kernel(per_device, local, lengths, after, basis, cosine, sine, table):
    me = device_id()
    row_table(lengths, table, me, local, lengths.shape[0])
    fill_tables(table, me, per_device, basis, cosine, sine, local // BLOCK)


def table_shapes(local):
    phase_rows = -(-(local // BLOCK) // 8) * 8
    return [
        jax.ShapeDtypeStruct((SHARES, 2 * LANES, BLOCK), jnp.bfloat16),
        jax.ShapeDtypeStruct((SHARES, phase_rows, LANES), jnp.float32),
        jax.ShapeDtypeStruct((SHARES, phase_rows, LANES), jnp.float32),
    ]


def tables_of(lengths, after, local, per_device):
    return pl.pallas_call(
        functools.partial(tables_kernel, per_device, local),
        out_shape=table_shapes(local),
        in_specs=[pl.BlockSpec(memory_space=pltpu.SMEM), pl.BlockSpec(memory_space=pl.ANY)],
        out_specs=[pl.BlockSpec(memory_space=pltpu.VMEM)] * 3,
        scratch_shapes=[pltpu.SMEM((16,), jnp.int32)],
        compiler_params=pltpu.CompilerParams(vmem_limit_bytes=SMALL),
        name="tables",
    )(lengths, after)


def swapped(value, mask):
    count = lax.axis_size(AXES)
    return lax.ppermute(value, AXES, [(i, i ^ mask) for i in range(count)])


def exchanged(values):
    return [swapped(value, share) if share else value for value, share in zip(values, ORDER)]


def legendre(latitude, waves):
    order = waves.astype(jnp.float32)[None, :]
    sine = jnp.sqrt(1.0 - latitude * latitude)[:, None]
    place = latitude[:, None]
    diagonal = jnp.full((latitude.shape[0], waves.shape[0]), math.sqrt(0.5), jnp.float32)
    previous = jnp.zeros_like(diagonal)
    current = jnp.zeros_like(diagonal)
    degrees = []
    for degree in range(WAVES):
        if degree:
            diagonal = diagonal * (sine * math.sqrt((2.0 * degree + 1.0) / (2.0 * degree)))
        upper = max(4.0 * degree * degree - 1.0, 0.0)
        below = float(degree - 1) ** 2
        factor_upper = jnp.sqrt(upper / jnp.maximum(float(degree * degree) - order * order, 1.0))
        factor_lower = jnp.sqrt(
            jnp.maximum(below - order * order, 0.0) / max(4.0 * below - 1.0, 1.0)
        )
        value = factor_upper * (place * current - factor_lower * previous)
        value = jnp.where(order > degree, 0.0, jnp.where(order == degree, diagonal, value))
        previous, current = current, value
        degrees.append(value)
    return jnp.stack(degrees, axis=-1)


def middle_general(received, strength, lengths, latitude, weights, local, per_device):
    rows = lengths.shape[0]
    count = lax.axis_size(AXES)
    channels = strength.shape[1]
    me = device_id()
    stops = jnp.cumsum(lengths)
    row_ids = jnp.arange(rows, dtype=jnp.int32)
    slots = jnp.arange(SHARES, dtype=jnp.int32)
    picks = []
    for share in ORDER:
        first = jnp.sum((stops <= (me ^ share) * local).astype(jnp.int32))
        held = first + ((slots - first) & 3)
        picks.append((held[:, None] == row_ids[None, :]).astype(jnp.float32))
    total = 0.0
    for pick, message in zip(picks, received):
        total = total + jnp.einsum(
            "gj,fcrgm->jfcrm",
            pick,
            message.reshape(2, channels, 2, SHARES, GROUP),
            precision=HIGHEST,
        )
    mask = SHARES
    while mask < count:
        total = total + swapped(total, mask)
        mask *= 2
    outer = jnp.arange(GROUP, dtype=jnp.int32) // per_device
    waves = per_device * ((me & 3) + SHARES * outer) + jnp.arange(GROUP) % per_device
    values = legendre(latitude, waves)
    gram = jnp.einsum("jmn,kmn->mjk", values, values, precision=HIGHEST)
    scale = jnp.where(waves == 0, 1.0, 2.0)
    rate_first = strength[0][:, None, None]
    both, second = total[:, 0], total[:, 1]
    once = jnp.einsum("mjk,kcrm->jcrm", gram, second, precision=HIGHEST)
    first = both - second - rate_first * weights[:, None, None, None] * once
    back = jnp.einsum("mjk,kcrm->jcrm", gram, first + second, precision=HIGHEST)
    back = back * (weights / lengths.astype(jnp.float32))[:, None, None, None] * scale
    replies = [
        jnp.einsum("gj,jcrm->crgm", pick, back, precision=HIGHEST).reshape(channels, LANES)
        for pick in picks
    ]
    spectrum = jnp.stack([first, second])
    begin = (me // SHARES) * per_device
    spectrum = lax.dynamic_slice_in_dim(spectrum, begin, per_device, 4)
    mine = lax.dynamic_slice_in_dim(values, begin, per_device, 1)
    factor = lax.dynamic_slice_in_dim(scale, begin, per_device, 0)
    factor = factor * (float(local * count) ** -0.5)
    result = jnp.einsum("jmn,sjcrm->scrmn", mine, spectrum, precision=HIGHEST)
    result = result * factor[:, None] * jnp.array([1.0, -1.0])[:, None, None]
    return replies, result


def least(values):
    result = values[0]
    for value in values[1:]:
        result = jnp.minimum(result, value)
    return result


def prepare_kernel(
    count, local, lengths, latitude, weights, coupling, poly, gram, pt, square
):
    me = device_id()
    down = lax.broadcasted_iota(jnp.int32, (8, LANES), 0)
    lane = lax.broadcasted_iota(jnp.int32, (8, LANES), 1)
    group = (lane >> 4) & 3
    packed = down >= SHARES
    array = jnp.where(packed, (lane >> 6) * 2 + ((lane >> 3) & 1), down)
    row = SHARES * array + group
    within = lane & (GROUP - 1)
    outer = within >> 3
    order = jnp.where(
        packed, 8 * me + (lane & 7), 8 * ((me & 3) + SHARES * outer) + (lane & 7)
    ).astype(jnp.float32)
    place = jnp.zeros((8, LANES), jnp.float32)
    weight = jnp.zeros((8, LANES), jnp.float32)
    size = jnp.zeros((8, LANES), jnp.int32)
    for index in range(lengths.shape[0]):
        here = row == index
        place = jnp.where(here, latitude[index], place)
        weight = jnp.where(here, weights[index], weight)
        size = jnp.where(here, lengths[index], size)
    doubling = jnp.where(order == 0.0, 1.0, 2.0)
    scale = weight / size.astype(jnp.float32) * doubling
    sine = jnp.sqrt(1.0 - place * place)
    order_square = order * order
    diagonal = jnp.full((8, LANES), math.sqrt(0.5), jnp.float32)
    previous = jnp.zeros((8, LANES), jnp.float32)
    current = previous
    for degree in range(WAVES):
        if degree:
            diagonal = diagonal * (sine * math.sqrt((2.0 * degree + 1.0) / (2.0 * degree)))
        upper = math.sqrt(max(4.0 * degree * degree - 1.0, 0.0))
        below = float(degree - 1) ** 2
        factor_upper = upper * lax.rsqrt(jnp.maximum(float(degree * degree) - order_square, 1.0))
        factor_lower = jnp.sqrt(
            jnp.maximum(below - order_square, 0.0) * (1.0 / max(4.0 * below - 1.0, 1.0))
        )
        value = (factor_upper * place) * current - (factor_upper * factor_lower) * previous
        value = jnp.where(order > degree, 0.0, jnp.where(order == degree, diagonal, value))
        previous, current = current, value
        for index in range(SHARES + 1):
            pt[index, pl.ds(degree, 1), :] = value[index : index + 1, :]
    for step in range(SHARES):
        for source in range(SHARES):
            moved = group_roll(pt[source], step)
            for target in range(SHARES):
                square[target, pl.ds(step * SHARES + source, 1), :] = jnp.sum(
                    pt[target] * moved, axis=0, keepdims=True
                )
    twice = [jnp.zeros((GROUP, LANES), jnp.float32)] * SHARES
    for through in range(SHARES):
        weighted = square[through] * weight[through : through + 1, :]
        for step in range(SHARES):
            moved = group_roll(weighted, step)
            if step:
                moved = jnp.concatenate(
                    [moved[GROUP - SHARES * step :], moved[: GROUP - SHARES * step]], axis=0
                )
            for target in range(SHARES):
                factor = square[target, pl.ds(step * SHARES + through, 1), :]
                twice[target] = twice[target] + factor * moved
    for target in range(SHARES):
        coupling[0, target] = square[target] * scale[target : target + 1, :]
        coupling[1, target] = twice[target] * scale[target : target + 1, :]
    mine = pt[SHARES]
    factor = doubling[SHARES : SHARES + 1, :] * (float(local * count) ** -0.5)
    products = lax.dot_general(
        mine, mine, (((0,), (0,)), ((), ())), precision=HIGHEST, preferred_element_type=jnp.float32
    )
    same = (lax.broadcasted_iota(jnp.int32, (LANES, LANES), 0) & 7) == (
        lax.broadcasted_iota(jnp.int32, (LANES, LANES), 1) & 7
    )
    products = jnp.where(same, products * weight[SHARES : SHARES + 1, :], 0.0)
    turned = jnp.concatenate([mine * factor, jnp.zeros_like(mine)], axis=0).T
    for value, out in ((turned, poly), (products, gram)):
        high = value.astype(jnp.bfloat16)
        low = (value - high.astype(jnp.float32)).astype(jnp.bfloat16)
        out[...] = jnp.concatenate([high, high, low], axis=0)


def three_parts(value):
    rounded = value.astype(jnp.bfloat16).astype(jnp.float32)
    return [rounded, value - rounded, rounded]


SMEM = pl.BlockSpec(memory_space=pltpu.SMEM)
VMEM = pl.BlockSpec(memory_space=pltpu.VMEM)


def floats(*shape):
    return jax.ShapeDtypeStruct(shape, jnp.float32)


def prepare(lengths, latitude, weights, count, local):
    return pl.pallas_call(
        functools.partial(prepare_kernel, count, local),
        out_shape=[
            floats(2, SHARES, GROUP, LANES),
            jax.ShapeDtypeStruct((3 * LANES, LANES), jnp.bfloat16),
            jax.ShapeDtypeStruct((3 * LANES, LANES), jnp.bfloat16),
        ],
        in_specs=[SMEM] * 3,
        out_specs=[VMEM] * 3,
        scratch_shapes=[
            pltpu.VMEM((SHARES + 1, WAVES, LANES), jnp.float32),
            pltpu.VMEM((SHARES, GROUP, LANES), jnp.float32),
        ],
        compiler_params=pltpu.CompilerParams(vmem_limit_bytes=SMALL),
        name="prepare",
    )(lengths, latitude, weights)


def couple_kernel(local, lengths, rates, coupling, *refs):
    messages, (own, other) = [ref[...] for ref in refs[:SHARES]], refs[SHARES:]
    channels = rates.shape[0]
    me = device_id()
    *firsts, far = first_rows(lengths, near(me) + [(me ^ SHARES) & SHARES], local)
    arrays = by_row(messages, firsts)
    sums = [jnp.zeros((channels, LANES), jnp.float32)] * SHARES
    for source in range(SHARES):
        both = arrays[source][:channels]
        second = rates[...] * arrays[source][channels:]
        for step in range(SHARES):
            moved_both = group_roll(both, step)
            moved_second = group_roll(second, step)
            at = pl.ds(step * SHARES + source, 1)
            for target in range(SHARES):
                sums[target] = (
                    sums[target]
                    + coupling[0, target, at, :] * moved_both
                    - coupling[1, target, at, :] * moved_second
                )
    for first, out in ((least(firsts), own), (far, other)):
        begin = row_arrays(first)
        for index in range(WINDOW):
            value = jnp.zeros((channels, LANES), jnp.float32)
            for target in range(SHARES):
                value = jnp.where(begin + index == target, sums[target], value)
            out[pl.ds(index * channels, channels), :] = value


def couple(lengths, rates, coupling, messages, local):
    channels = rates.shape[0]
    return pl.pallas_call(
        functools.partial(couple_kernel, local),
        out_shape=[floats(WINDOW * channels, LANES)] * 2,
        in_specs=[SMEM] + [VMEM] * (2 + SHARES),
        out_specs=[VMEM] * 2,
        compiler_params=pltpu.CompilerParams(vmem_limit_bytes=SMALL),
        name="couple",
    )(lengths, rates, coupling, *messages)


def pack_kernel(local, lengths, after, *refs):
    messages, (across, rows, *chunks) = [ref[...] for ref in refs[:SHARES]], refs[SHARES:]
    channels = messages[0].shape[0] // 2
    me = device_id()
    for share in range(SHARES):
        chunks[ORDER.index(share)][...] = across[pl.ds(share * channels, channels), :]
    arrays = by_row(
        [interleaved(message, me >= SHARES) for message in messages],
        first_rows(lengths, near(me), local),
    )
    for index in range(SHARES):
        rows[pl.ds(index * channels, channels), :] = arrays[index]


def pack(lengths, after, messages, across, local):
    channels = messages[0].shape[0] // 2
    return pl.pallas_call(
        functools.partial(pack_kernel, local),
        out_shape=[floats(SHARES * channels, LANES)] + [floats(channels, LANES)] * SHARES,
        in_specs=[SMEM, pl.BlockSpec(memory_space=pl.ANY)] + [VMEM] * (SHARES + 1),
        out_specs=[VMEM] * (SHARES + 1),
        compiler_params=pltpu.CompilerParams(vmem_limit_bytes=SMALL),
        name="pack",
    )(lengths, after, *messages, across)


def hand_out_kernel(local, lengths, own, other, *outs):
    channels = outs[0].shape[0]
    firsts = first_rows(lengths, near(device_id()), local)
    begin = row_arrays(least(firsts))
    sums = []
    for index in range(WINDOW):
        at = pl.ds(index * channels, channels)
        sums.append(own[at, :] + other[at, :])
    for first, out in zip(firsts, outs):
        array = row_arrays(first) - begin
        value = sums[0]
        for index in range(1, WINDOW):
            value = jnp.where(array == index, sums[index], value)
        out[...] = value


def hand_out(lengths, own, other, local):
    channels = own.shape[0] // WINDOW
    return pl.pallas_call(
        functools.partial(hand_out_kernel, local),
        out_shape=[floats(channels, LANES)] * SHARES,
        in_specs=[SMEM] + [VMEM] * 2,
        out_specs=[VMEM] * SHARES,
        compiler_params=pltpu.CompilerParams(vmem_limit_bytes=SMALL),
        name="hand_out",
    )(lengths, own, other)


def spectrum_kernel(local, lengths, rates, rows, *refs):
    chunks, (poly, gram, out) = [ref[...] for ref in refs[:SHARES]], refs[SHARES:]
    channels = rates.shape[0]
    far = [device ^ SHARES for device in near(device_id())]
    arrays = by_row(chunks, first_rows(lengths, far, local))
    for index in range(SHARES):
        arrays[index] = arrays[index] + rows[pl.ds(index * channels, channels), :]
    across = lax.broadcasted_iota(jnp.int32, (1, LANES), 1)
    held = (across >> 6) * 2 + ((across >> 3) & 1)

    def by_lane(part, field):
        value = jnp.zeros((channels, LANES), jnp.float32)
        for index in range(SHARES):
            shift = (64 * (index >> 1) + 8 * (index & 1) - 64 * part - 8 * field) % LANES
            moved = pltpu.roll(arrays[index], shift, 1) if shift else arrays[index]
            value = jnp.where(held == index, moved, value)
        return value

    down = lax.broadcasted_iota(jnp.int32, (8, LANES), 0)
    lane = lax.broadcasted_iota(jnp.int32, (8, LANES), 1)
    match = jnp.where(down == (lane & 7), 1.0, 0.0)[None]
    for part in range(2):
        second = by_lane(part, 1)
        left = jnp.concatenate([side.astype(jnp.bfloat16) for side in three_parts(second)], axis=1)
        first = by_lane(part, 0) - second
        first = first - rates[...] * jnp.dot(left, gram[...], preferred_element_type=jnp.float32)
        for index, value in enumerate((first, second)):
            if part:
                value = -value
            high, low, _ = three_parts(value)
            sides = [
                (side[:, None, :] * match).reshape(8 * channels, LANES).astype(jnp.bfloat16)
                for side in (high, low)
            ]
            product = jnp.dot(
                jnp.concatenate(sides + sides[:1], axis=1),
                poly[...],
                preferred_element_type=jnp.float32,
            )
            out[index, :, part] = product[:, :WAVES].reshape(channels, 8, WAVES)


def spectrum(lengths, rates, rows, chunks, poly, gram, local):
    channels = rates.shape[0]
    return pl.pallas_call(
        functools.partial(spectrum_kernel, local),
        out_shape=pltpu.VMEM((2, channels, 2, 8, WAVES), jnp.float32),
        in_specs=[SMEM] + [VMEM] * (SHARES + 4),
        out_specs=VMEM,
        compiler_params=pltpu.CompilerParams(vmem_limit_bytes=SMALL),
        name="spectrum",
    )(lengths, rates, rows, *chunks, poly, gram)


def middle_small(
    received, across, rates, lengths, latitude, weights, local, per_device, count
):
    across = swapped(across, SHARES)
    coupling, poly, gram = prepare(lengths, latitude, weights, count, local)
    part, sent_part = couple(lengths, rates, coupling, received, local)
    other_part = swapped(sent_part, SHARES)
    tables = tables_of(lengths, part, local, per_device)
    rows, *chunks = pack(lengths, tables[1], received, across, local)
    chunks = exchanged(chunks)
    replies = hand_out(lengths, part, other_part, local)
    return replies, tables, (lengths, rates, rows, chunks, poly, gram, local)


def on_device(cot_first, cot_second, strength, lengths, latitude, weights):
    local = cot_first.shape[1]
    count = lax.axis_size(AXES)
    per_device = WAVES // count
    *messages, across, rates, kept = analyse(lengths, strength, cot_second, cot_first, per_device)
    received = exchanged(messages)
    arguments = (lengths, latitude, weights, local, per_device)
    small = count == 2 * SHARES and lengths.shape[0] == GROUP
    if small:
        replies, tables, pieces = middle_small(received, across, rates, *arguments, count)
    else:
        replies, grad_target = middle_general(received, strength, *arguments)
        tables = tables_of(lengths, replies[0], local, per_device)
    answers = exchanged(replies)
    if small:
        grad_target = spectrum(*pieces)
    grad_state, grad_target = restore(lengths, answers, kept, tables, grad_target)
    return (grad_state, grad_target)


def solution(mesh):
    return jax.shard_map(
        on_device,
        mesh=mesh,
        in_specs=(
            P("chan", ("groups", "pts", "lev")),
            P("chan", ("groups", "pts", "lev")),
            P(None, ("groups", "chan")),
            P("groups"),
            P("groups"),
            P("groups"),
        ),
        out_specs=(
            P("chan", ("groups", "pts", "lev")),
            P(None, ("groups", "chan"), None, ("pts", "lev"), None),
        ),
        check_vma=False,
    )
```

```python
import functools
import math

import jax
import jax.numpy as jnp
import numpy as np
from jax import lax
from jax.experimental import pallas as pl
from jax.experimental.pallas import tpu as pltpu
from jax.sharding import PartitionSpec as P

MAXLEN = 3072
WAVES = 64
BLOCK = 256
LANES = 128
SHARES = 4
GROUP = WAVES // SHARES
ORDER = (0, 2, 3, 1)
PAD = 64
FULL = 60 * 1024 * 1024
WINDOW = 3
SMALL = 8 * 1024 * 1024
HIGHEST = lax.Precision.HIGHEST
AXES = ("pts", "lev")


def cosine_coefficients():
    nodes = np.cos(np.pi * (np.arange(64) + 0.5) / 64)
    squares = 0.12525 * (nodes + 1.0)
    fitted = np.polynomial.Polynomial.fit(squares, np.cos(2.0 * np.pi * np.sqrt(squares)), 7)
    return [float(value) for value in fitted.convert().coef]


COSINE = cosine_coefficients()


def cos_turns(turns):
    turns = turns - jnp.floor(turns + 0.5)
    square = turns * turns
    value = jnp.full_like(square, COSINE[-1])
    for coefficient in COSINE[-2::-1]:
        value = value * square + coefficient
    return value


def turns_of(wave, point, size):
    inverse = 1.0 / size
    product = wave * point
    whole = jnp.floor(product * inverse + 0.5)
    return (product - whole * size) * inverse


def lane_waves(lane, me, per_device):
    share = (lane >> 4) & 3
    within = lane & (GROUP - 1)
    shift = per_device.bit_length() - 1
    outer = within >> shift
    return per_device * (((me ^ share) & 3) + SHARES * outer) + (within & (per_device - 1))


def device_id():
    return lax.axis_index("pts") * lax.axis_size("lev") + lax.axis_index("lev")


def row_table(lengths, table, me, local, rows):
    begin = me * local
    for slot in range(SHARES):
        table[slot] = 0
        table[SHARES + slot] = MAXLEN
        table[2 * SHARES + slot] = local

    def step(row, carry):
        start, first = carry
        size = lengths[row]
        stop = start + size
        first = first + jnp.where(stop <= begin, 1, 0)

        @pl.when((stop > begin) & (start < begin + local))
        def _():
            table[row & 3] = start - begin
            table[SHARES + (row & 3)] = size
            table[2 * SHARES + row - first] = start - begin

        return stop, first

    _, first = lax.fori_loop(0, rows, step, (jnp.int32(0), jnp.int32(0)))
    table[3 * SHARES] = first


def fill_phases(table, me, per_device, blocks, cosine, sine, sign):
    rows = cosine.shape[1]
    lane = lax.broadcasted_iota(jnp.int32, (rows, LANES), 1)
    begin = BLOCK * lax.broadcasted_iota(jnp.int32, (rows, LANES), 0)
    wave = lane_waves(lane, me, per_device).astype(jnp.float32)
    signs = jnp.where(lane >= PAD, sign, -sign)
    for slot in range(SHARES):
        size = jnp.full((rows, LANES), table[SHARES + slot], jnp.int32).astype(jnp.float32)
        turns = turns_of(wave, (begin - table[slot]).astype(jnp.float32), size)
        cosine[slot] = cos_turns(turns)
        sine[slot] = cos_turns(turns - 0.25) * signs


def basis_of(wave_index, point, size_int, me, per_device):
    wave = lane_waves(wave_index, me, per_device).astype(jnp.float32)
    size = jnp.full(wave.shape, size_int, jnp.int32).astype(jnp.float32)
    turns = turns_of(wave, point.astype(jnp.float32), size)
    value = cos_turns(turns - jnp.where(wave_index >= PAD, 0.25, 0.0))
    high = value.astype(jnp.bfloat16)
    low = (value - high.astype(jnp.float32)).astype(jnp.bfloat16)
    return high, low


def column(row):
    count = row.shape[1]
    down = lax.broadcasted_iota(jnp.int32, (count, count), 0)
    across = lax.broadcasted_iota(jnp.int32, (count, count), 1)
    return jnp.sum(jnp.where(down == across, row, 0.0), axis=1, keepdims=True)


def group_roll(value, step):
    if step == 0:
        return value
    lane = lax.broadcasted_iota(jnp.int32, (1, LANES), 1)
    near = ((lane >> 4) & 3) < SHARES - step
    return jnp.where(
        near,
        pltpu.roll(value, LANES - GROUP * step, 1),
        pltpu.roll(value, GROUP * (SHARES - step), 1),
    )


def first_rows(lengths, devices, local):
    begins = [device * local for device in devices]

    def step(row, carry):
        stop = carry[0] + lengths[row]
        return (stop,) + tuple(
            first + jnp.where(stop <= begin, 1, 0) for first, begin in zip(carry[1:], begins)
        )

    zero = jnp.int32(0)
    return lax.fori_loop(0, lengths.shape[0], step, (zero,) * (1 + len(devices)), unroll=True)[1:]


def near(me):
    return [me ^ share for share in ORDER]


def row_arrays(first):
    lane = lax.broadcasted_iota(jnp.int32, (1, LANES), 1)
    group = (lane >> 4) & 3
    return (first + ((group - first) & 3)) >> 2


def by_row(messages, held):
    arrays = []
    for index in range(SHARES):
        value = jnp.zeros(messages[0].shape, jnp.float32)
        for array, message in zip(held, messages):
            value = value + jnp.where(array == index, message, 0.0)
        arrays.append(value)
    return arrays


def split_block(begin, blocks):
    within = begin & (BLOCK - 1)
    return jnp.minimum(begin >> 8, blocks - 1), jnp.where(within == 0, BLOCK, within)


def interleaved(message, upper):
    channels = message.shape[0] // 2
    both, second = message[:channels], message[channels:]
    odd = ((lax.broadcasted_iota(jnp.int32, (1, LANES), 1) >> 3) & 1) == 1
    return jnp.where(
        upper,
        jnp.where(odd, second, pltpu.roll(both, LANES - 8, 1)),
        jnp.where(odd, pltpu.roll(second, 8, 1), both),
    )


def load_fields(second, first, fields, sems):
    copies = [
        pltpu.make_async_copy(source, fields.at[index], sems.at[index])
        for index, source in enumerate((second, first))
    ]
    for copy in copies:
        copy.start()
    return copies


def analyse_kernel(per_device, lengths_held, strength_held, second, first, *refs):
    messages, (rates, kept, fields, lengths, strength, basis, cosine, sine, lhs, total, table) = (
        refs[:SHARES],
        refs[SHARES:-3],
    )
    sems, length_sem, strength_sem = refs[-3:]
    channels, local = second.shape
    blocks = local // BLOCK
    length_copy = pltpu.make_async_copy(lengths_held, lengths, length_sem)
    length_copy.start()
    strength_copy = pltpu.make_async_copy(strength_held, strength, strength_sem)
    strength_copy.start()
    copies = load_fields(second, first, fields, sems)
    me = device_id()
    length_copy.wait()
    strength_copy.wait()
    row_table(lengths, table, me, local, lengths.shape[0])
    fill_phases(table, me, per_device, blocks, cosine, sine, 1.0)
    wave_index = lax.broadcasted_iota(jnp.int32, (BLOCK, LANES), 1)
    point = lax.broadcasted_iota(jnp.int32, (BLOCK, LANES), 0)
    for slot in range(SHARES):
        high, low = basis_of(wave_index, point, table[SHARES + slot], me, per_device)
        basis[slot, :, :LANES] = high
        basis[slot, :, LANES:] = low
    total[...] = jnp.zeros_like(total)
    lhs[...] = jnp.zeros_like(lhs)
    within = lax.broadcasted_iota(jnp.int32, (1, BLOCK), 1)

    def add_block(block, place, slot, low_end, high_end, buffer):
        keep = (within >= low_end) & (within < high_end)
        for index in range(2):
            piece = jnp.where(keep, fields[index, :, pl.ds(place, BLOCK)], 0.0)
            high = piece.astype(jnp.bfloat16)
            low = (piece - high.astype(jnp.float32)).astype(jnp.bfloat16)
            lhs[buffer, pl.ds(index * PAD, channels), :] = high
            lhs[buffer, pl.ds((2 + index) * PAD, channels), :] = low
        product = jnp.dot(
            lhs[buffer, : 2 * PAD, :], basis[slot], preferred_element_type=jnp.float32
        )
        value = product[:, :LANES] + product[:, LANES:]
        value = value + jnp.dot(
            lhs[buffer, 2 * PAD :, :], basis[slot, :, :LANES], preferred_element_type=jnp.float32
        )
        turned = (
            value * cosine[slot, pl.ds(block, 1), :]
            + pltpu.roll(value, PAD, 1) * sine[slot, pl.ds(block, 1), :]
        )
        total[slot] = total[slot] + turned

    begin_slot = table[3 * SHARES]
    for copy in copies:
        copy.wait()
    for block in range(blocks):
        place = block * BLOCK
        slot = begin_slot
        for later in range(1, SHARES):
            slot = slot + jnp.where(table[2 * SHARES + later] <= place, 1, 0)
        slot = slot & 3
        add_block(
            block, place, slot, 0, table[slot] + table[SHARES + slot] - place, block % lhs.shape[0]
        )
        at = pl.ds(place, BLOCK)
        kept[:, at] = fields[0, :, at] + fields[1, :, at]
    for later in range(1, SHARES):
        block, low_end = split_block(table[2 * SHARES + later], blocks)
        place = pl.multiple_of(block * BLOCK, BLOCK)
        add_block(block, place, (begin_slot + later) & 3, low_end, BLOCK, later)

    rate_first = column(strength[0:1, :])
    rate_second = column(strength[1:2, :])
    rates[...] = jnp.broadcast_to(rate_first, rates.shape)
    lane = lax.broadcasted_iota(jnp.int32, (1, LANES), 1)
    chunk = (lane >> 4) & 3
    pairs = []
    for slot in range(SHARES):
        value_second = total[slot, :channels, :]
        value_first = total[slot, PAD : PAD + channels, :]
        part_second = rate_second * value_second
        pairs.append((rate_first * (value_first + value_second) + part_second, part_second))
    moved = []
    for which in range(2):
        by_shift = {}
        for shift in range(1 - SHARES, SHARES):
            value = jnp.zeros((channels, LANES), jnp.float32)
            for share in range(SHARES):
                if 0 <= share + shift < SHARES:
                    value = jnp.where(chunk == share, pairs[share + shift][which], value)
            by_shift[shift] = pltpu.roll(value, (shift * GROUP) % LANES, 1) if shift else value
        moved.append(by_shift)
    for share in range(SHARES):
        for which in range(2):
            value = moved[which][-share]
            for slot in range(1, SHARES):
                value = jnp.where(chunk == slot, moved[which][slot - share], value)
            message = messages[ORDER.index(share)]
            message[pl.ds(which * channels, channels), :] = value


def in_hbm(*values):
    return [pltpu.with_memory_space_constraint(value, pltpu.HBM) for value in values]


def analyse(lengths, strength, second, first, per_device):
    channels, local = second.shape
    blocks = local // BLOCK
    phase_rows = -(-blocks // 8) * 8
    return pl.pallas_call(
        functools.partial(analyse_kernel, per_device),
        out_shape=[pltpu.VMEM((2 * channels, LANES), jnp.float32)] * SHARES
        + [
            pltpu.VMEM((channels, LANES), jnp.float32),
            pltpu.VMEM((channels, local), jnp.float32),
        ],
        in_specs=[pl.BlockSpec(memory_space=pltpu.HBM)] * 4,
        out_specs=[pl.BlockSpec(memory_space=pltpu.VMEM)] * (SHARES + 2),
        scratch_shapes=[
            pltpu.VMEM((2, channels, local), jnp.float32),
            pltpu.SMEM(lengths.shape, jnp.int32),
            pltpu.VMEM(strength.shape, jnp.float32),
            pltpu.VMEM((SHARES, BLOCK, 2 * LANES), jnp.bfloat16),
            pltpu.VMEM((SHARES, phase_rows, LANES), jnp.float32),
            pltpu.VMEM((SHARES, phase_rows, LANES), jnp.float32),
            pltpu.VMEM((4, 4 * PAD, BLOCK), jnp.bfloat16),
            pltpu.VMEM((SHARES, 2 * PAD, LANES), jnp.float32),
            pltpu.SMEM((16,), jnp.int32),
            pltpu.SemaphoreType.DMA((2,)),
            pltpu.SemaphoreType.DMA,
            pltpu.SemaphoreType.DMA,
        ],
        compiler_params=pltpu.CompilerParams(vmem_limit_bytes=32 * 1024 * 1024),
        name="analyse",
    )(*in_hbm(lengths, strength, second, first))


def restore_kernel(*refs):
    messages, refs = refs[:SHARES], refs[SHARES:]
    kept, bases, cosine, sine, choose, mix, spectra, out, spectra_out, held, coeff = refs[:-2]
    sems, spectra_sem = refs[-2:]
    spectra_copy = pltpu.make_async_copy(spectra, spectra_out, spectra_sem)
    spectra_copy.start()
    channels, local = kept.shape
    blocks = local // BLOCK
    width = local // sems.shape[0]
    lane = lax.broadcasted_iota(jnp.int32, (1, LANES), 1)
    chunk = (lane >> 4) & 3
    coeff[...] = jnp.zeros_like(coeff)
    for slot in range(SHARES):
        value = jnp.zeros((channels, LANES), jnp.float32)
        for share in range(SHARES):
            moved = messages[ORDER.index(share)][...]
            if slot != share:
                moved = pltpu.roll(moved, ((share - slot) * GROUP) % LANES, 1)
            value = jnp.where(chunk == share, moved, value)
        coeff[slot, :channels, :] = value

    def part_value(part):
        value = coeff[0] * choose[pl.ds(SHARES * part, 1), :]
        for slot in range(1, SHARES):
            value = value + coeff[slot] * choose[pl.ds(SHARES * part + slot, 1), :]
        turned = (
            value * cosine[pl.ds(part, 1), :]
            + pltpu.roll(value, PAD, 1) * sine[pl.ds(part, 1), :]
        )
        high = turned.astype(jnp.bfloat16)
        low = (turned - high.astype(jnp.float32)).astype(jnp.bfloat16)
        left = jnp.concatenate([high, low], axis=0)
        left = jnp.concatenate([left, left], axis=1)
        product = jnp.dot(left, bases[part], preferred_element_type=jnp.float32)
        return product[:channels] + product[PAD : PAD + channels]

    ends = [part_value(blocks + index) for index in range(SHARES - 1)]
    copies = []
    for block in range(blocks):
        place = block * BLOCK
        value = part_value(block)
        for index in range(SHARES - 1):
            value = value + ends[index] * mix[pl.ds((SHARES - 1) * block + index, 1), :]
        held[:, pl.ds(place, BLOCK)] = kept[:, pl.ds(place, BLOCK)] - value
        if (place + BLOCK) % width == 0:
            at = pl.ds(place + BLOCK - width, width)
            copies.append(
                pltpu.make_async_copy(held.at[:, at], out.at[:, at], sems.at[len(copies)])
            )
            copies[-1].start()
    for copy in copies:
        copy.wait()
    spectra_copy.wait()


def restore(messages, kept, tables, spectra):
    channels, local = kept.shape
    pieces = math.gcd(local // BLOCK, 6)
    return pl.pallas_call(
        restore_kernel,
        out_shape=[
            jax.ShapeDtypeStruct((channels, local), jnp.float32),
            jax.ShapeDtypeStruct(spectra.shape, jnp.float32),
        ],
        in_specs=[pl.BlockSpec(memory_space=pltpu.VMEM)] * (SHARES + 7),
        out_specs=[pl.BlockSpec(memory_space=pl.ANY)] * 2,
        scratch_shapes=[
            pltpu.VMEM((channels, local), jnp.float32),
            pltpu.VMEM((SHARES, PAD, LANES), jnp.float32),
            pltpu.SemaphoreType.DMA((pieces,)),
            pltpu.SemaphoreType.DMA,
        ],
        compiler_params=pltpu.CompilerParams(vmem_limit_bytes=32 * 1024 * 1024),
        name="restore",
    )(*messages, kept, *tables, spectra)


def fill_tables(table, me, per_device, basis, cosine, sine, blocks):
    fill_phases(table, me, per_device, blocks, cosine, sine, -1.0)
    wave_index = lax.broadcasted_iota(jnp.int32, (LANES, BLOCK), 0)
    point = lax.broadcasted_iota(jnp.int32, (LANES, BLOCK), 1)
    for slot in range(SHARES):
        high, low = basis_of(wave_index, point, table[SHARES + slot], me, per_device)
        basis[slot, :LANES, :] = high
        basis[slot, LANES:, :] = low


def tables_kernel(
    per_device, local, lengths_held, after, bases, cosine, sine, choose, mix, *scratch
):
    basis, cosines, sines, table, lengths, sem = scratch
    blocks = local // BLOCK
    me = device_id()
    copy = pltpu.make_async_copy(lengths_held, lengths, sem)
    copy.start()
    copy.wait()
    row_table(lengths, table, me, local, lengths.shape[0])
    fill_tables(table, me, per_device, basis, cosines, sines, blocks)
    within = lax.broadcasted_iota(jnp.int32, (1, BLOCK), 1)
    begin_slot = table[3 * SHARES]

    def place_part(part, block, slot, low_end, high_end):
        keep = jnp.where((within >= low_end) & (within < high_end), 1.0, 0.0)
        bases[part] = basis[slot] * keep.astype(jnp.bfloat16)
        cosine[pl.ds(part, 1), :] = cosines[slot, pl.ds(block, 1), :]
        sine[pl.ds(part, 1), :] = sines[slot, pl.ds(block, 1), :]
        for other in range(SHARES):
            mark = jnp.where(slot == other, 1.0, 0.0)
            choose[pl.ds(SHARES * part + other, 1), :] = jnp.full((1, LANES), mark)

    for block in range(blocks):
        place = block * BLOCK
        slot = begin_slot
        for later in range(1, SHARES):
            slot = slot + jnp.where(table[2 * SHARES + later] <= place, 1, 0)
        slot = slot & 3
        place_part(block, block, slot, 0, table[slot] + table[SHARES + slot] - place)
    for later in range(1, SHARES):
        block, low_end = split_block(table[2 * SHARES + later], blocks)
        place_part(blocks + later - 1, block, (begin_slot + later) & 3, low_end, BLOCK)
        for other in range(blocks):
            mark = jnp.where(block == other, 1.0, 0.0)
            mix[pl.ds((SHARES - 1) * other + later - 1, 1), :] = jnp.full((1, BLOCK), mark)


def tables_of(lengths, after, local, per_device):
    blocks = local // BLOCK
    parts = blocks + SHARES - 1
    phase_rows = -(-blocks // 8) * 8
    shapes = [
        jax.ShapeDtypeStruct((parts, 2 * LANES, BLOCK), jnp.bfloat16),
        jax.ShapeDtypeStruct((parts, LANES), jnp.float32),
        jax.ShapeDtypeStruct((parts, LANES), jnp.float32),
        jax.ShapeDtypeStruct((SHARES * parts, LANES), jnp.float32),
        jax.ShapeDtypeStruct(((SHARES - 1) * blocks, BLOCK), jnp.float32),
    ]
    return pl.pallas_call(
        functools.partial(tables_kernel, per_device, local),
        out_shape=shapes,
        in_specs=[pl.BlockSpec(memory_space=pltpu.HBM), pl.BlockSpec(memory_space=pl.ANY)],
        out_specs=[pl.BlockSpec(memory_space=pltpu.VMEM)] * len(shapes),
        scratch_shapes=[
            pltpu.VMEM((SHARES, 2 * LANES, BLOCK), jnp.bfloat16),
            pltpu.VMEM((SHARES, phase_rows, LANES), jnp.float32),
            pltpu.VMEM((SHARES, phase_rows, LANES), jnp.float32),
            pltpu.SMEM((16,), jnp.int32),
            pltpu.SMEM(lengths.shape, jnp.int32),
            pltpu.SemaphoreType.DMA,
        ],
        compiler_params=pltpu.CompilerParams(vmem_limit_bytes=SMALL),
        name="tables",
    )(*in_hbm(lengths), after)


def swapped(value, mask):
    count = lax.axis_size(AXES)
    return lax.ppermute(value, AXES, [(i, i ^ mask) for i in range(count)])


def exchanged(values):
    return [swapped(value, share) if share else value for value, share in zip(values, ORDER)]


def legendre(latitude, waves):
    order = waves.astype(jnp.float32)[None, :]
    sine = jnp.sqrt(1.0 - latitude * latitude)[:, None]
    place = latitude[:, None]
    diagonal = jnp.full((latitude.shape[0], waves.shape[0]), math.sqrt(0.5), jnp.float32)
    previous = jnp.zeros_like(diagonal)
    current = jnp.zeros_like(diagonal)
    degrees = []
    for degree in range(WAVES):
        if degree:
            diagonal = diagonal * (sine * math.sqrt((2.0 * degree + 1.0) / (2.0 * degree)))
        upper = max(4.0 * degree * degree - 1.0, 0.0)
        below = float(degree - 1) ** 2
        factor_upper = jnp.sqrt(upper / jnp.maximum(float(degree * degree) - order * order, 1.0))
        factor_lower = jnp.sqrt(
            jnp.maximum(below - order * order, 0.0) / max(4.0 * below - 1.0, 1.0)
        )
        value = factor_upper * (place * current - factor_lower * previous)
        value = jnp.where(order > degree, 0.0, jnp.where(order == degree, diagonal, value))
        previous, current = current, value
        degrees.append(value)
    return jnp.stack(degrees, axis=-1)


def middle_general(received, strength, lengths, latitude, weights, local, per_device):
    rows = lengths.shape[0]
    count = lax.axis_size(AXES)
    channels = strength.shape[1]
    me = device_id()
    stops = jnp.cumsum(lengths)
    row_ids = jnp.arange(rows, dtype=jnp.int32)
    slots = jnp.arange(SHARES, dtype=jnp.int32)
    picks = []
    for share in ORDER:
        first = jnp.sum((stops <= (me ^ share) * local).astype(jnp.int32))
        held = first + ((slots - first) & 3)
        picks.append((held[:, None] == row_ids[None, :]).astype(jnp.float32))
    total = 0.0
    for pick, message in zip(picks, received):
        total = total + jnp.einsum(
            "gj,fcrgm->jfcrm",
            pick,
            message.reshape(2, channels, 2, SHARES, GROUP),
            precision=HIGHEST,
        )
    mask = SHARES
    while mask < count:
        total = total + swapped(total, mask)
        mask *= 2
    outer = jnp.arange(GROUP, dtype=jnp.int32) // per_device
    waves = per_device * ((me & 3) + SHARES * outer) + jnp.arange(GROUP) % per_device
    values = legendre(latitude, waves)
    gram = jnp.einsum("jmn,kmn->mjk", values, values, precision=HIGHEST)
    scale = jnp.where(waves == 0, 1.0, 2.0)
    rate_first = strength[0][:, None, None]
    both, second = total[:, 0], total[:, 1]
    once = jnp.einsum("mjk,kcrm->jcrm", gram, second, precision=HIGHEST)
    first = both - second - rate_first * weights[:, None, None, None] * once
    back = jnp.einsum("mjk,kcrm->jcrm", gram, first + second, precision=HIGHEST)
    back = back * (weights / lengths.astype(jnp.float32))[:, None, None, None] * scale
    replies = [
        jnp.einsum("gj,jcrm->crgm", pick, back, precision=HIGHEST).reshape(channels, LANES)
        for pick in picks
    ]
    spectrum = jnp.stack([first, second])
    begin = (me // SHARES) * per_device
    spectrum = lax.dynamic_slice_in_dim(spectrum, begin, per_device, 4)
    mine = lax.dynamic_slice_in_dim(values, begin, per_device, 1)
    factor = lax.dynamic_slice_in_dim(scale, begin, per_device, 0)
    factor = factor * (float(local * count) ** -0.5)
    result = jnp.einsum("jmn,sjcrm->scrmn", mine, spectrum, precision=HIGHEST)
    result = result * factor[:, None] * jnp.array([1.0, -1.0])[:, None, None]
    return replies, result


def least(values):
    result = values[0]
    for value in values[1:]:
        result = jnp.minimum(result, value)
    return result


def hold_rows(lengths, me, local, held):
    firsts = first_rows(lengths, near(me) + near(me ^ SHARES), local)
    for index, first in enumerate(firsts):
        held[pl.ds(index, 1), :] = row_arrays(first)
    for half in range(2):
        begin = least(firsts[half * SHARES : (half + 1) * SHARES])
        held[pl.ds(2 * SHARES + half, 1), :] = row_arrays(begin)


def prepare_kernel(count, local, lengths_held, latitude_held, weights_held, after, *refs):
    coupling, poly, gram, held, pt, square, lengths, latitude, weights, sems = refs
    copies = [
        pltpu.make_async_copy(source, target, sems.at[index])
        for index, (source, target) in enumerate(
            ((lengths_held, lengths), (latitude_held, latitude), (weights_held, weights))
        )
    ]
    for copy in copies:
        copy.start()
    for copy in copies:
        copy.wait()
    me = device_id()
    hold_rows(lengths, me, local, held)
    down = lax.broadcasted_iota(jnp.int32, (8, LANES), 0)
    lane = lax.broadcasted_iota(jnp.int32, (8, LANES), 1)
    group = (lane >> 4) & 3
    packed = down >= SHARES
    array = jnp.where(packed, (lane >> 6) * 2 + ((lane >> 3) & 1), down)
    row = SHARES * array + group
    within = lane & (GROUP - 1)
    outer = within >> 3
    order = jnp.where(
        packed, 8 * me + (lane & 7), 8 * ((me & 3) + SHARES * outer) + (lane & 7)
    ).astype(jnp.float32)
    place = jnp.zeros((8, LANES), jnp.float32)
    weight = jnp.zeros((8, LANES), jnp.float32)
    size = jnp.zeros((8, LANES), jnp.int32)
    for index in range(lengths.shape[0]):
        here = row == index
        place = jnp.where(here, latitude[index], place)
        weight = jnp.where(here, weights[index], weight)
        size = jnp.where(here, lengths[index], size)
    doubling = jnp.where(order == 0.0, 1.0, 2.0)
    scale = weight / size.astype(jnp.float32) * doubling
    sine = jnp.sqrt(1.0 - place * place)
    order_square = order * order
    diagonal = jnp.full((8, LANES), math.sqrt(0.5), jnp.float32)
    previous = jnp.zeros((8, LANES), jnp.float32)
    current = previous
    for degree in range(WAVES):
        if degree:
            diagonal = diagonal * (sine * math.sqrt((2.0 * degree + 1.0) / (2.0 * degree)))
        upper = math.sqrt(max(4.0 * degree * degree - 1.0, 0.0))
        below = float(degree - 1) ** 2
        factor_upper = upper * lax.rsqrt(jnp.maximum(float(degree * degree) - order_square, 1.0))
        factor_lower = jnp.sqrt(
            jnp.maximum(below - order_square, 0.0) * (1.0 / max(4.0 * below - 1.0, 1.0))
        )
        value = (factor_upper * place) * current - (factor_upper * factor_lower) * previous
        value = jnp.where(order > degree, 0.0, jnp.where(order == degree, diagonal, value))
        previous, current = current, value
        for index in range(SHARES + 1):
            pt[index, pl.ds(degree, 1), :] = value[index : index + 1, :]
    for step in range(SHARES):
        for source in range(SHARES):
            moved = group_roll(pt[source], step)
            for target in range(SHARES):
                square[target, pl.ds(step * SHARES + source, 1), :] = jnp.sum(
                    pt[target] * moved, axis=0, keepdims=True
                )
    twice = [jnp.zeros((GROUP, LANES), jnp.float32)] * SHARES
    for through in range(SHARES):
        weighted = square[through] * weight[through : through + 1, :]
        for step in range(SHARES):
            moved = group_roll(weighted, step)
            if step:
                moved = jnp.concatenate(
                    [moved[GROUP - SHARES * step :], moved[: GROUP - SHARES * step]], axis=0
                )
            for target in range(SHARES):
                factor = square[target, pl.ds(step * SHARES + through, 1), :]
                twice[target] = twice[target] + factor * moved
    for target in range(SHARES):
        coupling[0, target] = square[target] * scale[target : target + 1, :]
        coupling[1, target] = twice[target] * scale[target : target + 1, :]
    mine = pt[SHARES]
    factor = doubling[SHARES : SHARES + 1, :] * (float(local * count) ** -0.5)
    products = lax.dot_general(
        mine, mine, (((0,), (0,)), ((), ())), precision=HIGHEST, preferred_element_type=jnp.float32
    )
    same = (lax.broadcasted_iota(jnp.int32, (LANES, LANES), 0) & 7) == (
        lax.broadcasted_iota(jnp.int32, (LANES, LANES), 1) & 7
    )
    products = jnp.where(same, products * weight[SHARES : SHARES + 1, :], 0.0)
    turned = jnp.concatenate([mine * factor, jnp.zeros_like(mine)], axis=0).T
    for value, out in ((turned, poly), (products, gram)):
        high = value.astype(jnp.bfloat16)
        low = (value - high.astype(jnp.float32)).astype(jnp.bfloat16)
        out[...] = jnp.concatenate([high, high, low], axis=0)


def three_parts(value):
    rounded = value.astype(jnp.bfloat16).astype(jnp.float32)
    return [rounded, value - rounded, rounded]


SMEM = pl.BlockSpec(memory_space=pltpu.SMEM)
VMEM = pl.BlockSpec(memory_space=pltpu.VMEM)


def floats(*shape):
    return jax.ShapeDtypeStruct(shape, jnp.float32)


def prepare(lengths, latitude, weights, after, count, local):
    return pl.pallas_call(
        functools.partial(prepare_kernel, count, local),
        out_shape=[
            floats(2, SHARES, GROUP, LANES),
            jax.ShapeDtypeStruct((3 * LANES, LANES), jnp.bfloat16),
            jax.ShapeDtypeStruct((3 * LANES, LANES), jnp.bfloat16),
            jax.ShapeDtypeStruct((GROUP, LANES), jnp.int32),
        ],
        in_specs=[pl.BlockSpec(memory_space=pltpu.HBM)] * 3 + [pl.BlockSpec(memory_space=pl.ANY)],
        out_specs=[VMEM] * 4,
        scratch_shapes=[
            pltpu.VMEM((SHARES + 1, WAVES, LANES), jnp.float32),
            pltpu.VMEM((SHARES, GROUP, LANES), jnp.float32),
            pltpu.SMEM(lengths.shape, jnp.int32),
            pltpu.SMEM(latitude.shape, jnp.float32),
            pltpu.SMEM(weights.shape, jnp.float32),
            pltpu.SemaphoreType.DMA((3,)),
        ],
        compiler_params=pltpu.CompilerParams(vmem_limit_bytes=SMALL),
        name="prepare",
    )(*in_hbm(lengths, latitude, weights), after)


def fill_window(begin, arrays, out):
    channels = out.shape[0] // WINDOW
    for index in range(WINDOW):
        value = jnp.zeros((channels, LANES), jnp.float32)
        for target in range(SHARES):
            value = jnp.where(begin + index == target, arrays[target], value)
        out[pl.ds(index * channels, channels), :] = value


def couple_kernel(held, rates, coupling, *refs):
    messages, (own, other) = [ref[...] for ref in refs[:SHARES]], refs[SHARES:]
    channels = rates.shape[0]
    arrays = by_row(messages, [held[pl.ds(index, 1), :] for index in range(SHARES)])
    sums = [jnp.zeros((channels, LANES), jnp.float32)] * SHARES
    for source in range(SHARES):
        both = arrays[source][:channels]
        second = rates[...] * arrays[source][channels:]
        for step in range(SHARES):
            moved_both = group_roll(both, step)
            moved_second = group_roll(second, step)
            at = pl.ds(step * SHARES + source, 1)
            for target in range(SHARES):
                sums[target] = (
                    sums[target]
                    + coupling[0, target, at, :] * moved_both
                    - coupling[1, target, at, :] * moved_second
                )
    for half, out in enumerate((own, other)):
        begin = held[pl.ds(2 * SHARES + half, 1), :]
        fill_window(begin, sums, out)


def couple(held, rates, coupling, messages):
    channels = rates.shape[0]
    return pl.pallas_call(
        couple_kernel,
        out_shape=[floats(WINDOW * channels, LANES)] * 2,
        in_specs=[VMEM] * (3 + SHARES),
        out_specs=[VMEM] * 2,
        compiler_params=pltpu.CompilerParams(vmem_limit_bytes=SMALL),
        name="couple",
    )(held, rates, coupling, *messages)


def pack_kernel(held, after, *refs):
    messages, (rows, sent) = [ref[...] for ref in refs[:SHARES]], refs[SHARES:]
    channels = messages[0].shape[0] // 2
    me = device_id()
    places = [held[pl.ds(index, 1), :] for index in range(SHARES)]
    near_half = by_row([interleaved(message, me >= SHARES) for message in messages], places)
    far_half = by_row([interleaved(message, me < SHARES) for message in messages], places)
    for index in range(SHARES):
        rows[pl.ds(index * channels, channels), :] = near_half[index]
    fill_window(held[pl.ds(2 * SHARES, 1), :], far_half, sent)


def pack(held, after, messages):
    channels = messages[0].shape[0] // 2
    return pl.pallas_call(
        pack_kernel,
        out_shape=[floats(SHARES * channels, LANES), floats(WINDOW * channels, LANES)],
        in_specs=[VMEM, pl.BlockSpec(memory_space=pl.ANY)] + [VMEM] * SHARES,
        out_specs=[VMEM] * 2,
        compiler_params=pltpu.CompilerParams(vmem_limit_bytes=SMALL),
        name="pack",
    )(held, after, *messages)


def hand_out_kernel(held, own, other, *outs):
    channels = outs[0].shape[0]
    begin = held[pl.ds(2 * SHARES, 1), :]
    sums = []
    for index in range(WINDOW):
        at = pl.ds(index * channels, channels)
        sums.append(own[at, :] + other[at, :])
    for place, out in enumerate(outs):
        array = held[pl.ds(place, 1), :] - begin
        value = sums[0]
        for index in range(1, WINDOW):
            value = jnp.where(array == index, sums[index], value)
        out[...] = value


def hand_out(held, own, other):
    channels = own.shape[0] // WINDOW
    return pl.pallas_call(
        hand_out_kernel,
        out_shape=[floats(channels, LANES)] * SHARES,
        in_specs=[VMEM] * 3,
        out_specs=[VMEM] * SHARES,
        compiler_params=pltpu.CompilerParams(vmem_limit_bytes=SMALL),
        name="hand_out",
    )(held, own, other)


def spectrum_kernel(held_rows, rates, rows, far, poly, gram, out):
    channels = rates.shape[0]
    begin = held_rows[pl.ds(2 * SHARES + 1, 1), :]
    arrays = []
    for index in range(SHARES):
        value = rows[pl.ds(index * channels, channels), :]
        for place in range(WINDOW):
            piece = far[pl.ds(place * channels, channels), :]
            value = value + jnp.where(begin + place == index, piece, 0.0)
        arrays.append(value)
    across = lax.broadcasted_iota(jnp.int32, (1, LANES), 1)
    held = (across >> 6) * 2 + ((across >> 3) & 1)

    def by_lane(part, field):
        value = jnp.zeros((channels, LANES), jnp.float32)
        for index in range(SHARES):
            shift = (64 * (index >> 1) + 8 * (index & 1) - 64 * part - 8 * field) % LANES
            moved = pltpu.roll(arrays[index], shift, 1) if shift else arrays[index]
            value = jnp.where(held == index, moved, value)
        return value

    down = lax.broadcasted_iota(jnp.int32, (8, LANES), 0)
    lane = lax.broadcasted_iota(jnp.int32, (8, LANES), 1)
    match = jnp.where(down == (lane & 7), 1.0, 0.0)[None]
    for part in range(2):
        second = by_lane(part, 1)
        left = jnp.concatenate([side.astype(jnp.bfloat16) for side in three_parts(second)], axis=1)
        first = by_lane(part, 0) - second
        first = first - rates[...] * jnp.dot(left, gram[...], preferred_element_type=jnp.float32)
        for index, value in enumerate((first, second)):
            if part:
                value = -value
            high, low, _ = three_parts(value)
            sides = [
                (side[:, None, :] * match).reshape(8 * channels, LANES).astype(jnp.bfloat16)
                for side in (high, low)
            ]
            product = jnp.dot(
                jnp.concatenate(sides + sides[:1], axis=1),
                poly[...],
                preferred_element_type=jnp.float32,
            )
            out[index, :, part] = product[:, :WAVES].reshape(channels, 8, WAVES)


def spectrum(held, rates, rows, far, poly, gram):
    channels = rates.shape[0]
    return pl.pallas_call(
        spectrum_kernel,
        out_shape=pltpu.VMEM((2, channels, 2, 8, WAVES), jnp.float32),
        in_specs=[VMEM] * 6,
        out_specs=VMEM,
        compiler_params=pltpu.CompilerParams(vmem_limit_bytes=SMALL),
        name="spectrum",
    )(held, rates, rows, far, poly, gram)


def middle_small(messages, rates, lengths, latitude, weights, local, per_device, count):
    coupling, poly, gram, held = prepare(lengths, latitude, weights, rates, count, local)
    received = exchanged(messages)
    part, sent_part = couple(held, rates, coupling, received)
    other_part = swapped(sent_part, SHARES)
    tables = tables_of(lengths, part, local, per_device)
    rows, sent_rows = pack(held, tables[1], received)
    far = swapped(sent_rows, SHARES)
    replies = hand_out(held, part, other_part)
    return replies, tables, (held, rates, rows, far, poly, gram)


def on_device(cot_first, cot_second, strength, lengths, latitude, weights):
    local = cot_first.shape[1]
    count = lax.axis_size(AXES)
    per_device = WAVES // count
    *messages, rates, kept = analyse(lengths, strength, cot_second, cot_first, per_device)
    arguments = (lengths, latitude, weights, local, per_device)
    small = count == 2 * SHARES and lengths.shape[0] == GROUP
    if small:
        replies, tables, pieces = middle_small(messages, rates, *arguments, count)
    else:
        replies, grad_target = middle_general(exchanged(messages), strength, *arguments)
        tables = tables_of(lengths, replies[0], local, per_device)
    answers = exchanged(replies)
    if small:
        grad_target = spectrum(*pieces)
    grad_state, grad_target = restore(answers, kept, tables, grad_target)
    return (grad_state, grad_target)


def solution(mesh):
    return jax.shard_map(
        on_device,
        mesh=mesh,
        in_specs=(
            P("chan", ("groups", "pts", "lev")),
            P("chan", ("groups", "pts", "lev")),
            P(None, ("groups", "chan")),
            P("groups"),
            P("groups"),
            P("groups"),
        ),
        out_specs=(
            P("chan", ("groups", "pts", "lev")),
            P(None, ("groups", "chan"), None, ("pts", "lev"), None),
        ),
        check_vma=False,
    )
```

```python
import functools
import math

import jax
import jax.numpy as jnp
import numpy as np
from jax import lax
from jax.experimental import pallas as pl
from jax.experimental.pallas import tpu as pltpu
from jax.sharding import PartitionSpec as P

MAXLEN = 3072
WAVES = 64
BLOCK = 256
LANES = 128
SHARES = 4
GROUP = WAVES // SHARES
ORDER = (0, 2, 3, 1)
RETURN = (0, 3, 2, 1)
PAD = 64
FULL = 60 * 1024 * 1024
WINDOW = 3
SMALL = 8 * 1024 * 1024
HIGHEST = lax.Precision.HIGHEST
AXES = ("pts", "lev")


def cosine_coefficients():
    nodes = np.cos(np.pi * (np.arange(64) + 0.5) / 64)
    squares = 0.12525 * (nodes + 1.0)
    fitted = np.polynomial.Polynomial.fit(squares, np.cos(2.0 * np.pi * np.sqrt(squares)), 7)
    return [float(value) for value in fitted.convert().coef]


COSINE = cosine_coefficients()


def cos_turns(turns):
    turns = turns - jnp.floor(turns + 0.5)
    square = turns * turns
    value = jnp.full_like(square, COSINE[-1])
    for coefficient in COSINE[-2::-1]:
        value = value * square + coefficient
    return value


def turns_of(wave, point, size):
    inverse = 1.0 / size
    product = wave * point
    whole = jnp.floor(product * inverse + 0.5)
    return (product - whole * size) * inverse


def lane_waves(lane, me, per_device):
    share = (lane >> 4) & 3
    within = lane & (GROUP - 1)
    shift = per_device.bit_length() - 1
    outer = within >> shift
    return per_device * (((me ^ share) & 3) + SHARES * outer) + (within & (per_device - 1))


def device_id():
    return lax.axis_index("pts") * lax.axis_size("lev") + lax.axis_index("lev")


def row_table(lengths, table, me, local, rows):
    begin = me * local
    for slot in range(SHARES):
        table[slot] = 0
        table[SHARES + slot] = MAXLEN
        table[2 * SHARES + slot] = local

    def step(row, carry):
        start, first = carry
        size = lengths[row]
        stop = start + size
        first = first + jnp.where(stop <= begin, 1, 0)

        @pl.when((stop > begin) & (start < begin + local))
        def _():
            table[row & 3] = start - begin
            table[SHARES + (row & 3)] = size
            table[2 * SHARES + row - first] = start - begin

        return stop, first

    _, first = lax.fori_loop(0, rows, step, (jnp.int32(0), jnp.int32(0)))
    table[3 * SHARES] = first


def fill_phases(table, me, per_device, blocks, cosine, sine, sign):
    rows = cosine.shape[1]
    lane = lax.broadcasted_iota(jnp.int32, (rows, LANES), 1)
    begin = BLOCK * lax.broadcasted_iota(jnp.int32, (rows, LANES), 0)
    wave = lane_waves(lane, me, per_device).astype(jnp.float32)
    signs = jnp.where(lane >= PAD, sign, -sign)
    for slot in range(SHARES):
        size = jnp.full((rows, LANES), table[SHARES + slot], jnp.int32).astype(jnp.float32)
        turns = turns_of(wave, (begin - table[slot]).astype(jnp.float32), size)
        cosine[slot] = cos_turns(turns)
        sine[slot] = cos_turns(turns - 0.25) * signs


def basis_of(wave_index, point, size_int, me, per_device):
    wave = lane_waves(wave_index, me, per_device).astype(jnp.float32)
    size = jnp.full(wave.shape, size_int, jnp.int32).astype(jnp.float32)
    turns = turns_of(wave, point.astype(jnp.float32), size)
    value = cos_turns(turns - jnp.where(wave_index >= PAD, 0.25, 0.0))
    high = value.astype(jnp.bfloat16)
    low = (value - high.astype(jnp.float32)).astype(jnp.bfloat16)
    return high, low


def column(row):
    count = row.shape[1]
    down = lax.broadcasted_iota(jnp.int32, (count, count), 0)
    across = lax.broadcasted_iota(jnp.int32, (count, count), 1)
    return jnp.sum(jnp.where(down == across, row, 0.0), axis=1, keepdims=True)


def group_roll(value, step):
    if step == 0:
        return value
    lane = lax.broadcasted_iota(jnp.int32, (1, LANES), 1)
    near = ((lane >> 4) & 3) < SHARES - step
    return jnp.where(
        near,
        pltpu.roll(value, LANES - GROUP * step, 1),
        pltpu.roll(value, GROUP * (SHARES - step), 1),
    )


def first_rows(lengths, devices, local):
    begins = [device * local for device in devices]

    def step(row, carry):
        stop = carry[0] + lengths[row]
        return (stop,) + tuple(
            first + jnp.where(stop <= begin, 1, 0) for first, begin in zip(carry[1:], begins)
        )

    zero = jnp.int32(0)
    return lax.fori_loop(0, lengths.shape[0], step, (zero,) * (1 + len(devices)), unroll=True)[1:]


def near(me):
    return [me ^ share for share in ORDER]


def row_arrays(first):
    lane = lax.broadcasted_iota(jnp.int32, (1, LANES), 1)
    group = (lane >> 4) & 3
    return (first + ((group - first) & 3)) >> 2


def by_row(messages, held):
    arrays = []
    for index in range(SHARES):
        value = jnp.zeros(messages[0].shape, jnp.float32)
        for array, message in zip(held, messages):
            value = value + jnp.where(array == index, message, 0.0)
        arrays.append(value)
    return arrays


def split_block(begin, blocks):
    within = begin & (BLOCK - 1)
    return jnp.minimum(begin >> 8, blocks - 1), jnp.where(within == 0, BLOCK, within)


def interleaved(message, upper):
    channels = message.shape[0] // 2
    both, second = message[:channels], message[channels:]
    odd = ((lax.broadcasted_iota(jnp.int32, (1, LANES), 1) >> 3) & 1) == 1
    return jnp.where(
        upper,
        jnp.where(odd, second, pltpu.roll(both, LANES - 8, 1)),
        jnp.where(odd, pltpu.roll(second, 8, 1), both),
    )


def padded(value):
    return jnp.pad(value, ((0, -value.shape[0] % 8), (0, 0)))


def load_fields(second, first, fields, sems):
    copies = [
        pltpu.make_async_copy(source, fields.at[index], sems.at[index])
        for index, source in enumerate((second, first))
    ]
    for copy in copies:
        copy.start()
    return copies


def analyse_kernel(per_device, lengths_held, strength_held, second, first, *refs):
    messages, (rates, kept, fields, lengths, strength, basis, cosine, sine, total, table) = (
        refs[:SHARES],
        refs[SHARES:-3],
    )
    sems, length_sem, strength_sem = refs[-3:]
    channels, local = second.shape
    blocks = local // BLOCK
    length_copy = pltpu.make_async_copy(lengths_held, lengths, length_sem)
    length_copy.start()
    strength_copy = pltpu.make_async_copy(strength_held, strength, strength_sem)
    strength_copy.start()
    copies = load_fields(second, first, fields, sems)
    me = device_id()
    length_copy.wait()
    strength_copy.wait()
    row_table(lengths, table, me, local, lengths.shape[0])
    fill_phases(table, me, per_device, blocks, cosine, sine, 1.0)
    wave_index = lax.broadcasted_iota(jnp.int32, (BLOCK, LANES), 1)
    point = lax.broadcasted_iota(jnp.int32, (BLOCK, LANES), 0)
    for slot in range(SHARES):
        high, low = basis_of(wave_index, point, table[SHARES + slot], me, per_device)
        basis[slot, :, :LANES] = high
        basis[slot, :, LANES:] = low
    total[...] = jnp.zeros_like(total)
    within = lax.broadcasted_iota(jnp.int32, (1, BLOCK), 1)

    def add_block(block, place, slot, low_end, high_end):
        keep = (within >= low_end) & (within < high_end)
        highs, lows = [], []
        for index in range(2):
            piece = jnp.where(keep, fields[index, :, pl.ds(place, BLOCK)], 0.0)
            high = piece.astype(jnp.bfloat16).astype(jnp.float32)
            highs.append(padded(high))
            lows.append(padded(piece - high))
        highs, lows = [
            jnp.concatenate(sides, axis=0).astype(jnp.bfloat16) for sides in (highs, lows)
        ]
        product = jnp.dot(highs, basis[slot], preferred_element_type=jnp.float32)
        value = product[:, :LANES] + product[:, LANES:]
        value = value + jnp.dot(
            lows, basis[slot, :, :LANES], preferred_element_type=jnp.float32
        )
        turned = (
            value * cosine[slot, pl.ds(block, 1), :]
            + pltpu.roll(value, PAD, 1) * sine[slot, pl.ds(block, 1), :]
        )
        total[slot] = total[slot] + turned

    begin_slot = table[3 * SHARES]
    for copy in copies:
        copy.wait()
    for block in range(blocks):
        place = block * BLOCK
        slot = begin_slot
        for later in range(1, SHARES):
            slot = slot + jnp.where(table[2 * SHARES + later] <= place, 1, 0)
        slot = slot & 3
        add_block(block, place, slot, 0, table[slot] + table[SHARES + slot] - place)
        at = pl.ds(place, BLOCK)
        kept[:, at] = fields[0, :, at] + fields[1, :, at]
    for later in range(1, SHARES):
        block, low_end = split_block(table[2 * SHARES + later], blocks)
        place = pl.multiple_of(block * BLOCK, BLOCK)
        add_block(block, place, (begin_slot + later) & 3, low_end, BLOCK)

    rate_first = column(strength[0:1, :])
    rate_second = column(strength[1:2, :])
    rates[...] = jnp.broadcast_to(rate_first, rates.shape)
    lane = lax.broadcasted_iota(jnp.int32, (1, LANES), 1)
    chunk = (lane >> 4) & 3
    pairs = []
    for slot in range(SHARES):
        value_second = total[slot, :channels, :]
        value_first = total[slot, total.shape[1] // 2 :, :][:channels]
        part_second = rate_second * value_second
        pairs.append((rate_first * (value_first + value_second) + part_second, part_second))
    moved = []
    for which in range(2):
        by_shift = {}
        for shift in range(1 - SHARES, SHARES):
            value = jnp.zeros((channels, LANES), jnp.float32)
            for share in range(SHARES):
                if 0 <= share + shift < SHARES:
                    value = jnp.where(chunk == share, pairs[share + shift][which], value)
            by_shift[shift] = pltpu.roll(value, (shift * GROUP) % LANES, 1) if shift else value
        moved.append(by_shift)
    for share in range(SHARES):
        for which in range(2):
            value = moved[which][-share]
            for slot in range(1, SHARES):
                value = jnp.where(chunk == slot, moved[which][slot - share], value)
            message = messages[ORDER.index(share)]
            message[pl.ds(which * channels, channels), :] = value


def in_hbm(*values):
    return [pltpu.with_memory_space_constraint(value, pltpu.HBM) for value in values]


def analyse(lengths, strength, second, first, per_device):
    channels, local = second.shape
    blocks = local // BLOCK
    phase_rows = -(-blocks // 8) * 8
    return pl.pallas_call(
        functools.partial(analyse_kernel, per_device),
        out_shape=[pltpu.VMEM((2 * channels, LANES), jnp.float32)] * SHARES
        + [
            pltpu.VMEM((channels, LANES), jnp.float32),
            pltpu.VMEM((channels, local), jnp.float32),
        ],
        in_specs=[pl.BlockSpec(memory_space=pltpu.HBM)] * 4,
        out_specs=[pl.BlockSpec(memory_space=pltpu.VMEM)] * (SHARES + 2),
        scratch_shapes=[
            pltpu.VMEM((2, channels, local), jnp.float32),
            pltpu.SMEM(lengths.shape, jnp.int32),
            pltpu.VMEM(strength.shape, jnp.float32),
            pltpu.VMEM((SHARES, BLOCK, 2 * LANES), jnp.bfloat16),
            pltpu.VMEM((SHARES, phase_rows, LANES), jnp.float32),
            pltpu.VMEM((SHARES, phase_rows, LANES), jnp.float32),
            pltpu.VMEM((SHARES, 2 * (channels + -channels % 8), LANES), jnp.float32),
            pltpu.SMEM((16,), jnp.int32),
            pltpu.SemaphoreType.DMA((2,)),
            pltpu.SemaphoreType.DMA,
            pltpu.SemaphoreType.DMA,
        ],
        compiler_params=pltpu.CompilerParams(vmem_limit_bytes=32 * 1024 * 1024),
        name="analyse",
    )(*in_hbm(lengths, strength, second, first))


def restore_kernel(*refs):
    messages, refs = refs[:SHARES], refs[SHARES:]
    kept, bases, cosine, sine, choose, mix, spectra, out, spectra_out, held, coeff = refs[:-2]
    sems, spectra_sem = refs[-2:]
    spectra_copy = pltpu.make_async_copy(spectra, spectra_out, spectra_sem)
    spectra_copy.start()
    channels, local = kept.shape
    blocks = local // BLOCK
    width = local // sems.shape[0]
    lane = lax.broadcasted_iota(jnp.int32, (1, LANES), 1)
    chunk = (lane >> 4) & 3
    coeff[...] = jnp.zeros_like(coeff)
    for slot in range(SHARES):
        value = jnp.zeros((channels, LANES), jnp.float32)
        for share in range(SHARES):
            moved = messages[RETURN.index(share)][...]
            if slot != share:
                moved = pltpu.roll(moved, ((share - slot) * GROUP) % LANES, 1)
            value = jnp.where(chunk == share, moved, value)
        coeff[slot, :channels, :] = value

    def part_value(part):
        value = coeff[0] * choose[pl.ds(SHARES * part, 1), :]
        for slot in range(1, SHARES):
            value = value + coeff[slot] * choose[pl.ds(SHARES * part + slot, 1), :]
        turned = (
            value * cosine[pl.ds(part, 1), :]
            + pltpu.roll(value, PAD, 1) * sine[pl.ds(part, 1), :]
        )
        high = turned.astype(jnp.bfloat16)
        low = (turned - high.astype(jnp.float32)).astype(jnp.bfloat16)
        left = jnp.concatenate([high, low], axis=0)
        left = jnp.concatenate([left, left], axis=1)
        product = jnp.dot(left, bases[part], preferred_element_type=jnp.float32)
        return product[:channels] + product[PAD : PAD + channels]

    ends = [part_value(blocks + index) for index in range(SHARES - 1)]
    copies = []
    for block in range(blocks):
        place = block * BLOCK
        value = part_value(block)
        for index in range(SHARES - 1):
            value = value + ends[index] * mix[pl.ds((SHARES - 1) * block + index, 1), :]
        held[:, pl.ds(place, BLOCK)] = kept[:, pl.ds(place, BLOCK)] - value
        if (place + BLOCK) % width == 0:
            at = pl.ds(place + BLOCK - width, width)
            copies.append(
                pltpu.make_async_copy(held.at[:, at], out.at[:, at], sems.at[len(copies)])
            )
            copies[-1].start()
    for copy in copies:
        copy.wait()
    spectra_copy.wait()


def restore(messages, kept, tables, spectra):
    channels, local = kept.shape
    pieces = math.gcd(local // BLOCK, 6)
    return pl.pallas_call(
        restore_kernel,
        out_shape=[
            jax.ShapeDtypeStruct((channels, local), jnp.float32),
            jax.ShapeDtypeStruct(spectra.shape, jnp.float32),
        ],
        in_specs=[pl.BlockSpec(memory_space=pltpu.VMEM)] * (SHARES + 7),
        out_specs=[pl.BlockSpec(memory_space=pl.ANY)] * 2,
        scratch_shapes=[
            pltpu.VMEM((channels, local), jnp.float32),
            pltpu.VMEM((SHARES, PAD, LANES), jnp.float32),
            pltpu.SemaphoreType.DMA((pieces,)),
            pltpu.SemaphoreType.DMA,
        ],
        compiler_params=pltpu.CompilerParams(vmem_limit_bytes=32 * 1024 * 1024),
        name="restore",
    )(*messages, kept, *tables, spectra)


def fill_tables(table, me, per_device, basis, cosine, sine, blocks):
    fill_phases(table, me, per_device, blocks, cosine, sine, -1.0)
    wave_index = lax.broadcasted_iota(jnp.int32, (LANES, BLOCK), 0)
    point = lax.broadcasted_iota(jnp.int32, (LANES, BLOCK), 1)
    for slot in range(SHARES):
        high, low = basis_of(wave_index, point, table[SHARES + slot], me, per_device)
        basis[slot, :LANES, :] = high
        basis[slot, LANES:, :] = low


def waves_kernel(per_device, local, lengths_held, after, basis, cosine, sine, table, lengths, sem):
    me = device_id()
    copy = pltpu.make_async_copy(lengths_held, lengths, sem)
    copy.start()
    copy.wait()
    row_table(lengths, table, me, local, lengths.shape[0])
    fill_tables(table, me, per_device, basis, cosine, sine, local // BLOCK)


def waves_of(lengths, after, local, per_device):
    phase_rows = -(-(local // BLOCK) // 8) * 8
    return pl.pallas_call(
        functools.partial(waves_kernel, per_device, local),
        out_shape=[
            jax.ShapeDtypeStruct((SHARES, 2 * LANES, BLOCK), jnp.bfloat16),
            jax.ShapeDtypeStruct((SHARES, phase_rows, LANES), jnp.float32),
            jax.ShapeDtypeStruct((SHARES, phase_rows, LANES), jnp.float32),
        ],
        in_specs=[pl.BlockSpec(memory_space=pltpu.HBM), pl.BlockSpec(memory_space=pl.ANY)],
        out_specs=[pl.BlockSpec(memory_space=pltpu.VMEM)] * 3,
        scratch_shapes=[
            pltpu.SMEM((16,), jnp.int32),
            pltpu.SMEM(lengths.shape, jnp.int32),
            pltpu.SemaphoreType.DMA,
        ],
        compiler_params=pltpu.CompilerParams(vmem_limit_bytes=SMALL),
        name="waves",
    )(*in_hbm(lengths), after)


def tables_kernel(
    local, lengths_held, basis, cosines, sines, bases, cosine, sine, choose, mix, *scratch
):
    table, lengths, sem = scratch
    blocks = local // BLOCK
    me = device_id()
    copy = pltpu.make_async_copy(lengths_held, lengths, sem)
    copy.start()
    copy.wait()
    row_table(lengths, table, me, local, lengths.shape[0])
    within = lax.broadcasted_iota(jnp.int32, (1, BLOCK), 1)
    begin_slot = table[3 * SHARES]

    def place_part(part, block, slot, low_end, high_end):
        keep = jnp.where((within >= low_end) & (within < high_end), 1.0, 0.0)
        bases[part] = basis[slot] * keep.astype(jnp.bfloat16)
        cosine[pl.ds(part, 1), :] = cosines[slot, pl.ds(block, 1), :]
        sine[pl.ds(part, 1), :] = sines[slot, pl.ds(block, 1), :]
        for other in range(SHARES):
            mark = jnp.where(slot == other, 1.0, 0.0)
            choose[pl.ds(SHARES * part + other, 1), :] = jnp.full((1, LANES), mark)

    for block in range(blocks):
        place = block * BLOCK
        slot = begin_slot
        for later in range(1, SHARES):
            slot = slot + jnp.where(table[2 * SHARES + later] <= place, 1, 0)
        slot = slot & 3
        place_part(block, block, slot, 0, table[slot] + table[SHARES + slot] - place)
    for later in range(1, SHARES):
        block, low_end = split_block(table[2 * SHARES + later], blocks)
        place_part(blocks + later - 1, block, (begin_slot + later) & 3, low_end, BLOCK)
        for other in range(blocks):
            mark = jnp.where(block == other, 1.0, 0.0)
            mix[pl.ds((SHARES - 1) * other + later - 1, 1), :] = jnp.full((1, BLOCK), mark)


def tables_of(lengths, waves, local):
    blocks = local // BLOCK
    parts = blocks + SHARES - 1
    shapes = [
        jax.ShapeDtypeStruct((parts, 2 * LANES, BLOCK), jnp.bfloat16),
        jax.ShapeDtypeStruct((parts, LANES), jnp.float32),
        jax.ShapeDtypeStruct((parts, LANES), jnp.float32),
        jax.ShapeDtypeStruct((SHARES * parts, LANES), jnp.float32),
        jax.ShapeDtypeStruct(((SHARES - 1) * blocks, BLOCK), jnp.float32),
    ]
    return pl.pallas_call(
        functools.partial(tables_kernel, local),
        out_shape=shapes,
        in_specs=[pl.BlockSpec(memory_space=pltpu.HBM)] + [pl.BlockSpec(memory_space=pltpu.VMEM)] * 3,
        out_specs=[pl.BlockSpec(memory_space=pltpu.VMEM)] * len(shapes),
        scratch_shapes=[
            pltpu.SMEM((16,), jnp.int32),
            pltpu.SMEM(lengths.shape, jnp.int32),
            pltpu.SemaphoreType.DMA,
        ],
        compiler_params=pltpu.CompilerParams(vmem_limit_bytes=SMALL),
        name="tables",
    )(*in_hbm(lengths), *waves)


def swapped(value, mask):
    count = lax.axis_size(AXES)
    return lax.ppermute(value, AXES, [(i, i ^ mask) for i in range(count)])


def exchanged(values, order):
    return [swapped(value, share) if share else value for value, share in zip(values, order)]


def legendre(latitude, waves):
    order = waves.astype(jnp.float32)[None, :]
    sine = jnp.sqrt(1.0 - latitude * latitude)[:, None]
    place = latitude[:, None]
    diagonal = jnp.full((latitude.shape[0], waves.shape[0]), math.sqrt(0.5), jnp.float32)
    previous = jnp.zeros_like(diagonal)
    current = jnp.zeros_like(diagonal)
    degrees = []
    for degree in range(WAVES):
        if degree:
            diagonal = diagonal * (sine * math.sqrt((2.0 * degree + 1.0) / (2.0 * degree)))
        upper = max(4.0 * degree * degree - 1.0, 0.0)
        below = float(degree - 1) ** 2
        factor_upper = jnp.sqrt(upper / jnp.maximum(float(degree * degree) - order * order, 1.0))
        factor_lower = jnp.sqrt(
            jnp.maximum(below - order * order, 0.0) / max(4.0 * below - 1.0, 1.0)
        )
        value = factor_upper * (place * current - factor_lower * previous)
        value = jnp.where(order > degree, 0.0, jnp.where(order == degree, diagonal, value))
        previous, current = current, value
        degrees.append(value)
    return jnp.stack(degrees, axis=-1)


def middle_general(received, strength, lengths, latitude, weights, local, per_device):
    rows = lengths.shape[0]
    count = lax.axis_size(AXES)
    channels = strength.shape[1]
    me = device_id()
    stops = jnp.cumsum(lengths)
    row_ids = jnp.arange(rows, dtype=jnp.int32)
    slots = jnp.arange(SHARES, dtype=jnp.int32)
    picks = []
    for share in ORDER:
        first = jnp.sum((stops <= (me ^ share) * local).astype(jnp.int32))
        held = first + ((slots - first) & 3)
        picks.append((held[:, None] == row_ids[None, :]).astype(jnp.float32))
    total = 0.0
    for pick, message in zip(picks, received):
        total = total + jnp.einsum(
            "gj,fcrgm->jfcrm",
            pick,
            message.reshape(2, channels, 2, SHARES, GROUP),
            precision=HIGHEST,
        )
    mask = SHARES
    while mask < count:
        total = total + swapped(total, mask)
        mask *= 2
    outer = jnp.arange(GROUP, dtype=jnp.int32) // per_device
    waves = per_device * ((me & 3) + SHARES * outer) + jnp.arange(GROUP) % per_device
    values = legendre(latitude, waves)
    gram = jnp.einsum("jmn,kmn->mjk", values, values, precision=HIGHEST)
    scale = jnp.where(waves == 0, 1.0, 2.0)
    rate_first = strength[0][:, None, None]
    both, second = total[:, 0], total[:, 1]
    once = jnp.einsum("mjk,kcrm->jcrm", gram, second, precision=HIGHEST)
    first = both - second - rate_first * weights[:, None, None, None] * once
    back = jnp.einsum("mjk,kcrm->jcrm", gram, first + second, precision=HIGHEST)
    back = back * (weights / lengths.astype(jnp.float32))[:, None, None, None] * scale
    replies = [
        jnp.einsum("gj,jcrm->crgm", pick, back, precision=HIGHEST).reshape(channels, LANES)
        for pick in picks
    ]
    spectrum = jnp.stack([first, second])
    begin = (me // SHARES) * per_device
    spectrum = lax.dynamic_slice_in_dim(spectrum, begin, per_device, 4)
    mine = lax.dynamic_slice_in_dim(values, begin, per_device, 1)
    factor = lax.dynamic_slice_in_dim(scale, begin, per_device, 0)
    factor = factor * (float(local * count) ** -0.5)
    result = jnp.einsum("jmn,sjcrm->scrmn", mine, spectrum, precision=HIGHEST)
    result = result * factor[:, None] * jnp.array([1.0, -1.0])[:, None, None]
    return replies, result


def least(values):
    result = values[0]
    for value in values[1:]:
        result = jnp.minimum(result, value)
    return result


def hold_rows(lengths, me, local, held):
    firsts = first_rows(lengths, near(me) + near(me ^ SHARES), local)
    for index, first in enumerate(firsts):
        held[pl.ds(index, 1), :] = row_arrays(first)
    for half in range(2):
        begin = least(firsts[half * SHARES : (half + 1) * SHARES])
        held[pl.ds(2 * SHARES + half, 1), :] = row_arrays(begin)


def prepare_kernel(count, local, lengths_held, latitude_held, weights_held, after, *refs):
    coupling, mine, factors, held, pt, square, lengths, latitude, weights, sems = refs
    copies = [
        pltpu.make_async_copy(source, target, sems.at[index])
        for index, (source, target) in enumerate(
            ((lengths_held, lengths), (latitude_held, latitude), (weights_held, weights))
        )
    ]
    for copy in copies:
        copy.start()
    for copy in copies:
        copy.wait()
    me = device_id()
    hold_rows(lengths, me, local, held)
    down = lax.broadcasted_iota(jnp.int32, (8, LANES), 0)
    lane = lax.broadcasted_iota(jnp.int32, (8, LANES), 1)
    group = (lane >> 4) & 3
    packed = down >= SHARES
    array = jnp.where(packed, (lane >> 6) * 2 + ((lane >> 3) & 1), down)
    row = SHARES * array + group
    within = lane & (GROUP - 1)
    outer = within >> 3
    order = jnp.where(
        packed, 8 * me + (lane & 7), 8 * ((me & 3) + SHARES * outer) + (lane & 7)
    ).astype(jnp.float32)
    place = jnp.zeros((8, LANES), jnp.float32)
    weight = jnp.zeros((8, LANES), jnp.float32)
    size = jnp.zeros((8, LANES), jnp.int32)
    for index in range(lengths.shape[0]):
        here = row == index
        place = jnp.where(here, latitude[index], place)
        weight = jnp.where(here, weights[index], weight)
        size = jnp.where(here, lengths[index], size)
    doubling = jnp.where(order == 0.0, 1.0, 2.0)
    scale = weight / size.astype(jnp.float32) * doubling
    sine = jnp.sqrt(1.0 - place * place)
    order_square = order * order
    diagonal = jnp.full((8, LANES), math.sqrt(0.5), jnp.float32)
    previous = jnp.zeros((8, LANES), jnp.float32)
    current = previous
    for degree in range(WAVES):
        if degree:
            diagonal = diagonal * (sine * math.sqrt((2.0 * degree + 1.0) / (2.0 * degree)))
        upper = math.sqrt(max(4.0 * degree * degree - 1.0, 0.0))
        below = float(degree - 1) ** 2
        factor_upper = upper * lax.rsqrt(jnp.maximum(float(degree * degree) - order_square, 1.0))
        factor_lower = jnp.sqrt(
            jnp.maximum(below - order_square, 0.0) * (1.0 / max(4.0 * below - 1.0, 1.0))
        )
        value = (factor_upper * place) * current - (factor_upper * factor_lower) * previous
        value = jnp.where(order > degree, 0.0, jnp.where(order == degree, diagonal, value))
        previous, current = current, value
        for index in range(SHARES + 1):
            pt[index, pl.ds(degree, 1), :] = value[index : index + 1, :]
    for step in range(SHARES):
        for source in range(SHARES):
            moved = group_roll(pt[source], step)
            for target in range(SHARES):
                square[target, pl.ds(step * SHARES + source, 1), :] = jnp.sum(
                    pt[target] * moved, axis=0, keepdims=True
                )
    twice = [jnp.zeros((GROUP, LANES), jnp.float32)] * SHARES
    for through in range(SHARES):
        weighted = square[through] * weight[through : through + 1, :]
        for step in range(SHARES):
            moved = group_roll(weighted, step)
            if step:
                moved = jnp.concatenate(
                    [moved[GROUP - SHARES * step :], moved[: GROUP - SHARES * step]], axis=0
                )
            for target in range(SHARES):
                factor = square[target, pl.ds(step * SHARES + through, 1), :]
                twice[target] = twice[target] + factor * moved
    for target in range(SHARES):
        coupling[0, target] = square[target] * scale[target : target + 1, :]
        coupling[1, target] = twice[target] * scale[target : target + 1, :]
    mine[...] = pt[SHARES]
    factors[0:1, :] = weight[SHARES : SHARES + 1, :]
    factors[1:2, :] = doubling[SHARES : SHARES + 1, :] * (float(local * count) ** -0.5)


def spectral_factors(mine, factors, poly, gram):
    products = lax.dot_general(
        mine, mine, (((0,), (0,)), ((), ())), precision=HIGHEST, preferred_element_type=jnp.float32
    )
    same = (lax.broadcasted_iota(jnp.int32, (LANES, LANES), 0) & 7) == (
        lax.broadcasted_iota(jnp.int32, (LANES, LANES), 1) & 7
    )
    products = jnp.where(same, products * factors[0:1, :], 0.0)
    turned = jnp.concatenate([mine * factors[1:2, :], jnp.zeros_like(mine)], axis=0).T
    for value, out in ((turned, poly), (products, gram)):
        high = value.astype(jnp.bfloat16)
        low = (value - high.astype(jnp.float32)).astype(jnp.bfloat16)
        out[...] = jnp.concatenate([high, high, low], axis=0)


def three_parts(value):
    rounded = value.astype(jnp.bfloat16).astype(jnp.float32)
    return [rounded, value - rounded, rounded]


SMEM = pl.BlockSpec(memory_space=pltpu.SMEM)
VMEM = pl.BlockSpec(memory_space=pltpu.VMEM)


def floats(*shape):
    return jax.ShapeDtypeStruct(shape, jnp.float32)


def prepare(lengths, latitude, weights, after, count, local):
    return pl.pallas_call(
        functools.partial(prepare_kernel, count, local),
        out_shape=[
            floats(2, SHARES, GROUP, LANES),
            floats(WAVES, LANES),
            floats(8, LANES),
            jax.ShapeDtypeStruct((GROUP, LANES), jnp.int32),
        ],
        in_specs=[pl.BlockSpec(memory_space=pltpu.HBM)] * 3 + [pl.BlockSpec(memory_space=pl.ANY)],
        out_specs=[VMEM] * 4,
        scratch_shapes=[
            pltpu.VMEM((SHARES + 1, WAVES, LANES), jnp.float32),
            pltpu.VMEM((SHARES, GROUP, LANES), jnp.float32),
            pltpu.SMEM(lengths.shape, jnp.int32),
            pltpu.SMEM(latitude.shape, jnp.float32),
            pltpu.SMEM(weights.shape, jnp.float32),
            pltpu.SemaphoreType.DMA((3,)),
        ],
        compiler_params=pltpu.CompilerParams(vmem_limit_bytes=SMALL),
        name="prepare",
    )(*in_hbm(lengths, latitude, weights), after)


def fill_window(begin, arrays, out):
    channels = out.shape[0] // WINDOW
    for index in range(WINDOW):
        value = jnp.zeros((channels, LANES), jnp.float32)
        for target in range(SHARES):
            value = jnp.where(begin + index == target, arrays[target], value)
        out[pl.ds(index * channels, channels), :] = value


def couple_kernel(held, rates, coupling, *refs):
    messages, (own, other) = [ref[...] for ref in refs[:SHARES]], refs[SHARES:]
    channels = rates.shape[0]
    arrays = by_row(messages, [held[pl.ds(index, 1), :] for index in range(SHARES)])
    sums = [jnp.zeros((channels, LANES), jnp.float32)] * SHARES
    for source in range(SHARES):
        both = arrays[source][:channels]
        second = rates[...] * arrays[source][channels:]
        for step in range(SHARES):
            moved_both = group_roll(both, step)
            moved_second = group_roll(second, step)
            at = pl.ds(step * SHARES + source, 1)
            for target in range(SHARES):
                sums[target] = (
                    sums[target]
                    + coupling[0, target, at, :] * moved_both
                    - coupling[1, target, at, :] * moved_second
                )
    for half, out in enumerate((own, other)):
        begin = held[pl.ds(2 * SHARES + half, 1), :]
        fill_window(begin, sums, out)


def couple(held, rates, coupling, messages):
    channels = rates.shape[0]
    return pl.pallas_call(
        couple_kernel,
        out_shape=[floats(WINDOW * channels, LANES)] * 2,
        in_specs=[VMEM] * (3 + SHARES),
        out_specs=[VMEM] * 2,
        compiler_params=pltpu.CompilerParams(vmem_limit_bytes=SMALL),
        name="couple",
    )(held, rates, coupling, *messages)


def pack_kernel(held, mine, factors, after, *refs):
    messages, (rows, sent, poly, gram) = [ref[...] for ref in refs[:SHARES]], refs[SHARES:]
    channels = messages[0].shape[0] // 2
    me = device_id()
    places = [held[pl.ds(index, 1), :] for index in range(SHARES)]
    near_half = by_row([interleaved(message, me >= SHARES) for message in messages], places)
    far_half = by_row([interleaved(message, me < SHARES) for message in messages], places)
    for index in range(SHARES):
        rows[pl.ds(index * channels, channels), :] = near_half[index]
    fill_window(held[pl.ds(2 * SHARES, 1), :], far_half, sent)
    spectral_factors(mine[...], factors[...], poly, gram)


def pack(held, mine, factors, after, messages):
    channels = messages[0].shape[0] // 2
    return pl.pallas_call(
        pack_kernel,
        out_shape=[floats(SHARES * channels, LANES), floats(WINDOW * channels, LANES)]
        + [jax.ShapeDtypeStruct((3 * LANES, LANES), jnp.bfloat16)] * 2,
        in_specs=[VMEM] * 3 + [pl.BlockSpec(memory_space=pl.ANY)] + [VMEM] * SHARES,
        out_specs=[VMEM] * 4,
        compiler_params=pltpu.CompilerParams(vmem_limit_bytes=SMALL),
        name="pack",
    )(held, mine, factors, after, *messages)


def hand_out_kernel(held, own, other, *outs):
    channels = outs[0].shape[0]
    begin = held[pl.ds(2 * SHARES, 1), :]
    sums = []
    for index in range(WINDOW):
        at = pl.ds(index * channels, channels)
        sums.append(own[at, :] + other[at, :])
    for share, out in zip(RETURN, outs):
        array = held[pl.ds(ORDER.index(share), 1), :] - begin
        value = sums[0]
        for index in range(1, WINDOW):
            value = jnp.where(array == index, sums[index], value)
        out[...] = value


def hand_out(held, own, other):
    channels = own.shape[0] // WINDOW
    return pl.pallas_call(
        hand_out_kernel,
        out_shape=[floats(channels, LANES)] * SHARES,
        in_specs=[VMEM] * 3,
        out_specs=[VMEM] * SHARES,
        compiler_params=pltpu.CompilerParams(vmem_limit_bytes=SMALL),
        name="hand_out",
    )(held, own, other)


def spectrum_kernel(held_rows, rates, rows, far, poly, gram, out):
    channels = rates.shape[0]
    begin = held_rows[pl.ds(2 * SHARES + 1, 1), :]
    arrays = []
    for index in range(SHARES):
        value = rows[pl.ds(index * channels, channels), :]
        for place in range(WINDOW):
            piece = far[pl.ds(place * channels, channels), :]
            value = value + jnp.where(begin + place == index, piece, 0.0)
        arrays.append(value)
    across = lax.broadcasted_iota(jnp.int32, (1, LANES), 1)
    held = (across >> 6) * 2 + ((across >> 3) & 1)

    def by_lane(part, field):
        value = jnp.zeros((channels, LANES), jnp.float32)
        for index in range(SHARES):
            shift = (64 * (index >> 1) + 8 * (index & 1) - 64 * part - 8 * field) % LANES
            moved = pltpu.roll(arrays[index], shift, 1) if shift else arrays[index]
            value = jnp.where(held == index, moved, value)
        return value

    down = lax.broadcasted_iota(jnp.int32, (8, LANES), 0)
    lane = lax.broadcasted_iota(jnp.int32, (8, LANES), 1)
    match = jnp.where(down == (lane & 7), 1.0, 0.0)[None]
    for part in range(2):
        second = by_lane(part, 1)
        left = jnp.concatenate([side.astype(jnp.bfloat16) for side in three_parts(second)], axis=1)
        first = by_lane(part, 0) - second
        first = first - rates[...] * jnp.dot(left, gram[...], preferred_element_type=jnp.float32)
        for index, value in enumerate((first, second)):
            if part:
                value = -value
            high, low, _ = three_parts(value)
            sides = [
                (side[:, None, :] * match).reshape(8 * channels, LANES).astype(jnp.bfloat16)
                for side in (high, low)
            ]
            product = jnp.dot(
                jnp.concatenate(sides + sides[:1], axis=1),
                poly[...],
                preferred_element_type=jnp.float32,
            )
            out[index, :, part] = product[:, :WAVES].reshape(channels, 8, WAVES)


def spectrum(held, rates, rows, far, poly, gram):
    channels = rates.shape[0]
    return pl.pallas_call(
        spectrum_kernel,
        out_shape=pltpu.VMEM((2, channels, 2, 8, WAVES), jnp.float32),
        in_specs=[VMEM] * 6,
        out_specs=VMEM,
        compiler_params=pltpu.CompilerParams(vmem_limit_bytes=SMALL),
        name="spectrum",
    )(held, rates, rows, far, poly, gram)


def middle_small(messages, rates, lengths, latitude, weights, local, per_device, count):
    coupling, mine, factors, held = prepare(lengths, latitude, weights, rates, count, local)
    received = exchanged(messages, ORDER)
    part, sent_part = couple(held, rates, coupling, received)
    other_part = swapped(sent_part, SHARES)
    waves = waves_of(lengths, part, local, per_device)
    rows, sent_rows, poly, gram = pack(held, mine, factors, waves[1], received)
    tables = tables_of(lengths, waves, local)
    far = swapped(sent_rows, SHARES)
    replies = hand_out(held, part, other_part)
    return replies, tables, (held, rates, rows, far, poly, gram)


def on_device(cot_first, cot_second, strength, lengths, latitude, weights):
    local = cot_first.shape[1]
    count = lax.axis_size(AXES)
    per_device = WAVES // count
    *messages, rates, kept = analyse(lengths, strength, cot_second, cot_first, per_device)
    arguments = (lengths, latitude, weights, local, per_device)
    small = count == 2 * SHARES and lengths.shape[0] == GROUP
    if small:
        replies, tables, pieces = middle_small(messages, rates, *arguments, count)
    else:
        replies, grad_target = middle_general(exchanged(messages, ORDER), strength, *arguments)
        replies = [replies[ORDER.index(share)] for share in RETURN]
        tables = tables_of(lengths, waves_of(lengths, replies[0], local, per_device), local)
    answers = exchanged(replies, RETURN)
    if small:
        grad_target = spectrum(*pieces)
    grad_state, grad_target = restore(answers, kept, tables, grad_target)
    return (grad_state, grad_target)


def solution(mesh):
    return jax.shard_map(
        on_device,
        mesh=mesh,
        in_specs=(
            P("chan", ("groups", "pts", "lev")),
            P("chan", ("groups", "pts", "lev")),
            P(None, ("groups", "chan")),
            P("groups"),
            P("groups"),
            P("groups"),
        ),
        out_specs=(
            P("chan", ("groups", "pts", "lev")),
            P(None, ("groups", "chan"), None, ("pts", "lev"), None),
        ),
        check_vma=False,
    )
```

```python
import functools
import math

import jax
import jax.numpy as jnp
import numpy as np
from jax import lax
from jax.experimental import pallas as pl
from jax.experimental.pallas import tpu as pltpu
from jax.sharding import PartitionSpec as P

MAXLEN = 3072
WAVES = 64
BLOCK = 256
LANES = 128
SHARES = 4
GROUP = WAVES // SHARES
ORDER = (0, 2, 3, 1)
RETURN = (0, 3, 2, 1)
PAD = 64
FULL = 60 * 1024 * 1024
WINDOW = 3
SMALL = 8 * 1024 * 1024
HIGHEST = lax.Precision.HIGHEST
AXES = ("pts", "lev")


def cosine_coefficients():
    nodes = np.cos(np.pi * (np.arange(64) + 0.5) / 64)
    squares = 0.12525 * (nodes + 1.0)
    fitted = np.polynomial.Polynomial.fit(squares, np.cos(2.0 * np.pi * np.sqrt(squares)), 7)
    return [float(value) for value in fitted.convert().coef]


COSINE = cosine_coefficients()


def cos_turns(turns):
    turns = turns - jnp.floor(turns + 0.5)
    square = turns * turns
    value = jnp.full_like(square, COSINE[-1])
    for coefficient in COSINE[-2::-1]:
        value = value * square + coefficient
    return value


def turns_of(wave, point, size):
    inverse = 1.0 / size
    product = wave * point
    whole = jnp.floor(product * inverse + 0.5)
    return (product - whole * size) * inverse


def lane_waves(lane, me, per_device):
    share = (lane >> 4) & 3
    within = lane & (GROUP - 1)
    shift = per_device.bit_length() - 1
    outer = within >> shift
    return per_device * (((me ^ share) & 3) + SHARES * outer) + (within & (per_device - 1))


def device_id():
    return lax.axis_index("pts") * lax.axis_size("lev") + lax.axis_index("lev")


def row_table(lengths, table, me, local, rows):
    begin = me * local
    for slot in range(SHARES):
        table[slot] = 0
        table[SHARES + slot] = MAXLEN
        table[2 * SHARES + slot] = local

    def step(row, carry):
        start, first = carry
        size = lengths[row]
        stop = start + size
        first = first + jnp.where(stop <= begin, 1, 0)

        @pl.when((stop > begin) & (start < begin + local))
        def _():
            table[row & 3] = start - begin
            table[SHARES + (row & 3)] = size
            table[2 * SHARES + row - first] = start - begin

        return stop, first

    _, first = lax.fori_loop(0, rows, step, (jnp.int32(0), jnp.int32(0)))
    table[3 * SHARES] = first


def fill_phases(table, me, per_device, blocks, cosine, sine, sign):
    rows = cosine.shape[1]
    lane = lax.broadcasted_iota(jnp.int32, (rows, LANES), 1)
    begin = BLOCK * lax.broadcasted_iota(jnp.int32, (rows, LANES), 0)
    wave = lane_waves(lane, me, per_device).astype(jnp.float32)
    signs = jnp.where(lane >= PAD, sign, -sign)
    for slot in range(SHARES):
        size = jnp.full((rows, LANES), table[SHARES + slot], jnp.int32).astype(jnp.float32)
        turns = turns_of(wave, (begin - table[slot]).astype(jnp.float32), size)
        cosine[slot] = cos_turns(turns)
        sine[slot] = cos_turns(turns - 0.25) * signs


def basis_of(wave_index, point, size_int, me, per_device):
    wave = lane_waves(wave_index, me, per_device).astype(jnp.float32)
    size = jnp.full(wave.shape, size_int, jnp.int32).astype(jnp.float32)
    turns = turns_of(wave, point.astype(jnp.float32), size)
    value = cos_turns(turns - jnp.where(wave_index >= PAD, 0.25, 0.0))
    high = value.astype(jnp.bfloat16)
    low = (value - high.astype(jnp.float32)).astype(jnp.bfloat16)
    return high, low


def column(row):
    count = row.shape[1]
    down = lax.broadcasted_iota(jnp.int32, (count, count), 0)
    across = lax.broadcasted_iota(jnp.int32, (count, count), 1)
    return jnp.sum(jnp.where(down == across, row, 0.0), axis=1, keepdims=True)


def group_roll(value, step):
    if step == 0:
        return value
    lane = lax.broadcasted_iota(jnp.int32, (1, LANES), 1)
    near = ((lane >> 4) & 3) < SHARES - step
    return jnp.where(
        near,
        pltpu.roll(value, LANES - GROUP * step, 1),
        pltpu.roll(value, GROUP * (SHARES - step), 1),
    )


def first_rows(lengths, devices, local):
    begins = [device * local for device in devices]

    def step(row, carry):
        stop = carry[0] + lengths[row]
        return (stop,) + tuple(
            first + jnp.where(stop <= begin, 1, 0) for first, begin in zip(carry[1:], begins)
        )

    zero = jnp.int32(0)
    return lax.fori_loop(0, lengths.shape[0], step, (zero,) * (1 + len(devices)), unroll=True)[1:]


def near(me):
    return [me ^ share for share in ORDER]


def row_arrays(first):
    lane = lax.broadcasted_iota(jnp.int32, (1, LANES), 1)
    group = (lane >> 4) & 3
    return (first + ((group - first) & 3)) >> 2


def by_row(messages, held):
    arrays = []
    for index in range(SHARES):
        value = jnp.zeros(messages[0].shape, jnp.float32)
        for array, message in zip(held, messages):
            value = value + jnp.where(array == index, message, 0.0)
        arrays.append(value)
    return arrays


def split_block(begin, blocks):
    within = begin & (BLOCK - 1)
    return jnp.minimum(begin >> 8, blocks - 1), jnp.where(within == 0, BLOCK, within)


def interleaved(message, upper):
    channels = message.shape[0] // 2
    both, second = message[:channels], message[channels:]
    odd = ((lax.broadcasted_iota(jnp.int32, (1, LANES), 1) >> 3) & 1) == 1
    return jnp.where(
        upper,
        jnp.where(odd, second, pltpu.roll(both, LANES - 8, 1)),
        jnp.where(odd, pltpu.roll(second, 8, 1), both),
    )


def padded(value):
    return jnp.pad(value, ((0, -value.shape[0] % 8), (0, 0)))


def load_fields(second, first, fields, sems):
    copies = [
        pltpu.make_async_copy(source, fields.at[index], sems.at[index])
        for index, source in enumerate((second, first))
    ]
    for copy in copies:
        copy.start()
    return copies


def analyse_kernel(per_device, lengths_held, strength_held, second, first, *refs):
    messages, (rates, kept, fields, lengths, strength, basis, cosine, sine, total, table) = (
        refs[:SHARES],
        refs[SHARES:-3],
    )
    sems, length_sem, strength_sem = refs[-3:]
    channels, local = second.shape
    blocks = local // BLOCK
    length_copy = pltpu.make_async_copy(lengths_held, lengths, length_sem)
    length_copy.start()
    strength_copy = pltpu.make_async_copy(strength_held, strength, strength_sem)
    strength_copy.start()
    copies = load_fields(second, first, fields, sems)
    me = device_id()
    length_copy.wait()
    strength_copy.wait()
    row_table(lengths, table, me, local, lengths.shape[0])
    fill_phases(table, me, per_device, blocks, cosine, sine, 1.0)
    wave_index = lax.broadcasted_iota(jnp.int32, (BLOCK, LANES), 1)
    point = lax.broadcasted_iota(jnp.int32, (BLOCK, LANES), 0)
    for slot in range(SHARES):
        high, low = basis_of(wave_index, point, table[SHARES + slot], me, per_device)
        basis[slot, :, :LANES] = high
        basis[slot, :, LANES:] = low
    total[...] = jnp.zeros_like(total)
    within = lax.broadcasted_iota(jnp.int32, (1, BLOCK), 1)

    def add_block(block, place, slot, low_end, high_end):
        keep = (within >= low_end) & (within < high_end)
        highs, lows = [], []
        for index in range(2):
            piece = jnp.where(keep, fields[index, :, pl.ds(place, BLOCK)], 0.0)
            high = piece.astype(jnp.bfloat16).astype(jnp.float32)
            highs.append(padded(high))
            lows.append(padded(piece - high))
        highs, lows = [
            jnp.concatenate(sides, axis=0).astype(jnp.bfloat16) for sides in (highs, lows)
        ]
        product = jnp.dot(highs, basis[slot], preferred_element_type=jnp.float32)
        value = product[:, :LANES] + product[:, LANES:]
        value = value + jnp.dot(
            lows, basis[slot, :, :LANES], preferred_element_type=jnp.float32
        )
        turned = (
            value * cosine[slot, pl.ds(block, 1), :]
            + pltpu.roll(value, PAD, 1) * sine[slot, pl.ds(block, 1), :]
        )
        total[slot] = total[slot] + turned

    begin_slot = table[3 * SHARES]
    for copy in copies:
        copy.wait()
    for block in range(blocks):
        place = block * BLOCK
        slot = begin_slot
        for later in range(1, SHARES):
            slot = slot + jnp.where(table[2 * SHARES + later] <= place, 1, 0)
        slot = slot & 3
        add_block(block, place, slot, 0, table[slot] + table[SHARES + slot] - place)
        at = pl.ds(place, BLOCK)
        kept[:, at] = fields[0, :, at] + fields[1, :, at]
    for later in range(1, SHARES):
        block, low_end = split_block(table[2 * SHARES + later], blocks)
        place = pl.multiple_of(block * BLOCK, BLOCK)
        add_block(block, place, (begin_slot + later) & 3, low_end, BLOCK)

    rate_first = column(strength[0:1, :])
    rate_second = column(strength[1:2, :])
    rates[...] = jnp.broadcast_to(rate_first, rates.shape)
    lane = lax.broadcasted_iota(jnp.int32, (1, LANES), 1)
    chunk = (lane >> 4) & 3
    pairs = []
    for slot in range(SHARES):
        value_second = total[slot, :channels, :]
        value_first = total[slot, total.shape[1] // 2 :, :][:channels]
        part_second = rate_second * value_second
        pairs.append((rate_first * (value_first + value_second) + part_second, part_second))
    moved = []
    for which in range(2):
        by_shift = {}
        for shift in range(1 - SHARES, SHARES):
            value = jnp.zeros((channels, LANES), jnp.float32)
            for share in range(SHARES):
                if 0 <= share + shift < SHARES:
                    value = jnp.where(chunk == share, pairs[share + shift][which], value)
            by_shift[shift] = pltpu.roll(value, (shift * GROUP) % LANES, 1) if shift else value
        moved.append(by_shift)
    for share in range(SHARES):
        for which in range(2):
            value = moved[which][-share]
            for slot in range(1, SHARES):
                value = jnp.where(chunk == slot, moved[which][slot - share], value)
            message = messages[ORDER.index(share)]
            message[pl.ds(which * channels, channels), :] = value


def in_hbm(*values):
    return [pltpu.with_memory_space_constraint(value, pltpu.HBM) for value in values]


def analyse(lengths, strength, second, first, per_device):
    channels, local = second.shape
    blocks = local // BLOCK
    phase_rows = -(-blocks // 8) * 8
    return pl.pallas_call(
        functools.partial(analyse_kernel, per_device),
        out_shape=[pltpu.VMEM((2 * channels, LANES), jnp.float32)] * SHARES
        + [
            pltpu.VMEM((channels, LANES), jnp.float32),
            pltpu.VMEM((channels, local), jnp.float32),
        ],
        in_specs=[pl.BlockSpec(memory_space=pltpu.HBM)] * 4,
        out_specs=[pl.BlockSpec(memory_space=pltpu.VMEM)] * (SHARES + 2),
        scratch_shapes=[
            pltpu.VMEM((2, channels, local), jnp.float32),
            pltpu.SMEM(lengths.shape, jnp.int32),
            pltpu.VMEM(strength.shape, jnp.float32),
            pltpu.VMEM((SHARES, BLOCK, 2 * LANES), jnp.bfloat16),
            pltpu.VMEM((SHARES, phase_rows, LANES), jnp.float32),
            pltpu.VMEM((SHARES, phase_rows, LANES), jnp.float32),
            pltpu.VMEM((SHARES, 2 * (channels + -channels % 8), LANES), jnp.float32),
            pltpu.SMEM((16,), jnp.int32),
            pltpu.SemaphoreType.DMA((2,)),
            pltpu.SemaphoreType.DMA,
            pltpu.SemaphoreType.DMA,
        ],
        compiler_params=pltpu.CompilerParams(vmem_limit_bytes=32 * 1024 * 1024),
        name="analyse",
    )(*in_hbm(lengths, strength, second, first))


def restore_kernel(*refs):
    messages, refs = refs[:SHARES], refs[SHARES:]
    kept, bases, cosine, sine, choose, mix, spectra, out, spectra_out, held, coeff = refs[:-2]
    sems, spectra_sem = refs[-2:]
    spectra_copy = pltpu.make_async_copy(spectra, spectra_out, spectra_sem)
    spectra_copy.start()
    channels, local = kept.shape
    blocks = local // BLOCK
    width = local // sems.shape[0]
    lane = lax.broadcasted_iota(jnp.int32, (1, LANES), 1)
    chunk = (lane >> 4) & 3
    coeff[...] = jnp.zeros_like(coeff)
    for slot in range(SHARES):
        value = jnp.zeros((channels, LANES), jnp.float32)
        for share in range(SHARES):
            moved = messages[RETURN.index(share)][...]
            if slot != share:
                moved = pltpu.roll(moved, ((share - slot) * GROUP) % LANES, 1)
            value = jnp.where(chunk == share, moved, value)
        coeff[slot, :channels, :] = value

    def part_value(part):
        value = coeff[0] * choose[pl.ds(SHARES * part, 1), :]
        for slot in range(1, SHARES):
            value = value + coeff[slot] * choose[pl.ds(SHARES * part + slot, 1), :]
        turned = (
            value * cosine[pl.ds(part, 1), :]
            + pltpu.roll(value, PAD, 1) * sine[pl.ds(part, 1), :]
        )
        high = turned.astype(jnp.bfloat16)
        low = (turned - high.astype(jnp.float32)).astype(jnp.bfloat16)
        left = jnp.concatenate([high, low], axis=0)
        left = jnp.concatenate([left, left], axis=1)
        product = jnp.dot(left, bases[part], preferred_element_type=jnp.float32)
        return product[:channels] + product[PAD : PAD + channels]

    ends = [part_value(blocks + index) for index in range(SHARES - 1)]
    copies = []
    for block in range(blocks):
        place = block * BLOCK
        value = part_value(block)
        for index in range(SHARES - 1):
            value = value + ends[index] * mix[pl.ds((SHARES - 1) * block + index, 1), :]
        held[:, pl.ds(place, BLOCK)] = kept[:, pl.ds(place, BLOCK)] - value
        if (place + BLOCK) % width == 0:
            at = pl.ds(place + BLOCK - width, width)
            copies.append(
                pltpu.make_async_copy(held.at[:, at], out.at[:, at], sems.at[len(copies)])
            )
            copies[-1].start()
    for copy in copies:
        copy.wait()
    spectra_copy.wait()


def restore(messages, kept, tables, spectra):
    channels, local = kept.shape
    pieces = math.gcd(local // BLOCK, 6)
    return pl.pallas_call(
        restore_kernel,
        out_shape=[
            jax.ShapeDtypeStruct((channels, local), jnp.float32),
            jax.ShapeDtypeStruct(spectra.shape, jnp.float32),
        ],
        in_specs=[pl.BlockSpec(memory_space=pltpu.VMEM)] * (SHARES + 7),
        out_specs=[pl.BlockSpec(memory_space=pl.ANY)] * 2,
        scratch_shapes=[
            pltpu.VMEM((channels, local), jnp.float32),
            pltpu.VMEM((SHARES, PAD, LANES), jnp.float32),
            pltpu.SemaphoreType.DMA((pieces,)),
            pltpu.SemaphoreType.DMA,
        ],
        compiler_params=pltpu.CompilerParams(vmem_limit_bytes=32 * 1024 * 1024),
        name="restore",
    )(*messages, kept, *tables, spectra)


def fill_tables(table, me, per_device, basis, cosine, sine, blocks):
    fill_phases(table, me, per_device, blocks, cosine, sine, -1.0)
    wave_index = lax.broadcasted_iota(jnp.int32, (LANES, BLOCK), 0)
    point = lax.broadcasted_iota(jnp.int32, (LANES, BLOCK), 1)
    for slot in range(SHARES):
        high, low = basis_of(wave_index, point, table[SHARES + slot], me, per_device)
        basis[slot, :LANES, :] = high
        basis[slot, LANES:, :] = low


def waves_kernel(per_device, local, lengths_held, after, basis, cosine, sine, table, lengths, sem):
    me = device_id()
    copy = pltpu.make_async_copy(lengths_held, lengths, sem)
    copy.start()
    copy.wait()
    row_table(lengths, table, me, local, lengths.shape[0])
    fill_tables(table, me, per_device, basis, cosine, sine, local // BLOCK)


def waves_of(lengths, after, local, per_device):
    phase_rows = -(-(local // BLOCK) // 8) * 8
    return pl.pallas_call(
        functools.partial(waves_kernel, per_device, local),
        out_shape=[
            jax.ShapeDtypeStruct((SHARES, 2 * LANES, BLOCK), jnp.bfloat16),
            jax.ShapeDtypeStruct((SHARES, phase_rows, LANES), jnp.float32),
            jax.ShapeDtypeStruct((SHARES, phase_rows, LANES), jnp.float32),
        ],
        in_specs=[pl.BlockSpec(memory_space=pltpu.HBM), pl.BlockSpec(memory_space=pl.ANY)],
        out_specs=[pl.BlockSpec(memory_space=pltpu.VMEM)] * 3,
        scratch_shapes=[
            pltpu.SMEM((16,), jnp.int32),
            pltpu.SMEM(lengths.shape, jnp.int32),
            pltpu.SemaphoreType.DMA,
        ],
        compiler_params=pltpu.CompilerParams(vmem_limit_bytes=SMALL),
        name="waves",
    )(*in_hbm(lengths), after)


def tables_kernel(
    local, lengths_held, basis, cosines, sines, bases, cosine, sine, choose, mix, *scratch
):
    table, lengths, sem = scratch
    blocks = local // BLOCK
    me = device_id()
    copy = pltpu.make_async_copy(lengths_held, lengths, sem)
    copy.start()
    copy.wait()
    row_table(lengths, table, me, local, lengths.shape[0])
    within = lax.broadcasted_iota(jnp.int32, (1, BLOCK), 1)
    begin_slot = table[3 * SHARES]

    def place_part(part, block, slot, low_end, high_end):
        keep = jnp.where((within >= low_end) & (within < high_end), 1.0, 0.0)
        bases[part] = basis[slot] * keep.astype(jnp.bfloat16)
        cosine[pl.ds(part, 1), :] = cosines[slot, pl.ds(block, 1), :]
        sine[pl.ds(part, 1), :] = sines[slot, pl.ds(block, 1), :]
        for other in range(SHARES):
            mark = jnp.where(slot == other, 1.0, 0.0)
            choose[pl.ds(SHARES * part + other, 1), :] = jnp.full((1, LANES), mark)

    for block in range(blocks):
        place = block * BLOCK
        slot = begin_slot
        for later in range(1, SHARES):
            slot = slot + jnp.where(table[2 * SHARES + later] <= place, 1, 0)
        slot = slot & 3
        place_part(block, block, slot, 0, table[slot] + table[SHARES + slot] - place)
    for later in range(1, SHARES):
        block, low_end = split_block(table[2 * SHARES + later], blocks)
        place_part(blocks + later - 1, block, (begin_slot + later) & 3, low_end, BLOCK)
        for other in range(blocks):
            mark = jnp.where(block == other, 1.0, 0.0)
            mix[pl.ds((SHARES - 1) * other + later - 1, 1), :] = jnp.full((1, BLOCK), mark)


def tables_of(lengths, waves, local):
    blocks = local // BLOCK
    parts = blocks + SHARES - 1
    shapes = [
        jax.ShapeDtypeStruct((parts, 2 * LANES, BLOCK), jnp.bfloat16),
        jax.ShapeDtypeStruct((parts, LANES), jnp.float32),
        jax.ShapeDtypeStruct((parts, LANES), jnp.float32),
        jax.ShapeDtypeStruct((SHARES * parts, LANES), jnp.float32),
        jax.ShapeDtypeStruct(((SHARES - 1) * blocks, BLOCK), jnp.float32),
    ]
    return pl.pallas_call(
        functools.partial(tables_kernel, local),
        out_shape=shapes,
        in_specs=[pl.BlockSpec(memory_space=pltpu.HBM)] + [pl.BlockSpec(memory_space=pltpu.VMEM)] * 3,
        out_specs=[pl.BlockSpec(memory_space=pltpu.VMEM)] * len(shapes),
        scratch_shapes=[
            pltpu.SMEM((16,), jnp.int32),
            pltpu.SMEM(lengths.shape, jnp.int32),
            pltpu.SemaphoreType.DMA,
        ],
        compiler_params=pltpu.CompilerParams(vmem_limit_bytes=SMALL),
        name="tables",
    )(*in_hbm(lengths), *waves)


def swapped(value, mask):
    count = lax.axis_size(AXES)
    return lax.ppermute(value, AXES, [(i, i ^ mask) for i in range(count)])


def exchanged(values, order):
    return [swapped(value, share) if share else value for value, share in zip(values, order)]


def legendre(latitude, waves):
    order = waves.astype(jnp.float32)[None, :]
    sine = jnp.sqrt(1.0 - latitude * latitude)[:, None]
    place = latitude[:, None]
    diagonal = jnp.full((latitude.shape[0], waves.shape[0]), math.sqrt(0.5), jnp.float32)
    previous = jnp.zeros_like(diagonal)
    current = jnp.zeros_like(diagonal)
    degrees = []
    for degree in range(WAVES):
        if degree:
            diagonal = diagonal * (sine * math.sqrt((2.0 * degree + 1.0) / (2.0 * degree)))
        upper = max(4.0 * degree * degree - 1.0, 0.0)
        below = float(degree - 1) ** 2
        factor_upper = jnp.sqrt(upper / jnp.maximum(float(degree * degree) - order * order, 1.0))
        factor_lower = jnp.sqrt(
            jnp.maximum(below - order * order, 0.0) / max(4.0 * below - 1.0, 1.0)
        )
        value = factor_upper * (place * current - factor_lower * previous)
        value = jnp.where(order > degree, 0.0, jnp.where(order == degree, diagonal, value))
        previous, current = current, value
        degrees.append(value)
    return jnp.stack(degrees, axis=-1)


def middle_general(received, strength, lengths, latitude, weights, local, per_device):
    rows = lengths.shape[0]
    count = lax.axis_size(AXES)
    channels = strength.shape[1]
    me = device_id()
    stops = jnp.cumsum(lengths)
    row_ids = jnp.arange(rows, dtype=jnp.int32)
    slots = jnp.arange(SHARES, dtype=jnp.int32)
    picks = []
    for share in ORDER:
        first = jnp.sum((stops <= (me ^ share) * local).astype(jnp.int32))
        held = first + ((slots - first) & 3)
        picks.append((held[:, None] == row_ids[None, :]).astype(jnp.float32))
    total = 0.0
    for pick, message in zip(picks, received):
        total = total + jnp.einsum(
            "gj,fcrgm->jfcrm",
            pick,
            message.reshape(2, channels, 2, SHARES, GROUP),
            precision=HIGHEST,
        )
    mask = SHARES
    while mask < count:
        total = total + swapped(total, mask)
        mask *= 2
    outer = jnp.arange(GROUP, dtype=jnp.int32) // per_device
    waves = per_device * ((me & 3) + SHARES * outer) + jnp.arange(GROUP) % per_device
    values = legendre(latitude, waves)
    gram = jnp.einsum("jmn,kmn->mjk", values, values, precision=HIGHEST)
    scale = jnp.where(waves == 0, 1.0, 2.0)
    rate_first = strength[0][:, None, None]
    both, second = total[:, 0], total[:, 1]
    once = jnp.einsum("mjk,kcrm->jcrm", gram, second, precision=HIGHEST)
    first = both - second - rate_first * weights[:, None, None, None] * once
    back = jnp.einsum("mjk,kcrm->jcrm", gram, first + second, precision=HIGHEST)
    back = back * (weights / lengths.astype(jnp.float32))[:, None, None, None] * scale
    replies = [
        jnp.einsum("gj,jcrm->crgm", pick, back, precision=HIGHEST).reshape(channels, LANES)
        for pick in picks
    ]
    spectrum = jnp.stack([first, second])
    begin = (me // SHARES) * per_device
    spectrum = lax.dynamic_slice_in_dim(spectrum, begin, per_device, 4)
    mine = lax.dynamic_slice_in_dim(values, begin, per_device, 1)
    factor = lax.dynamic_slice_in_dim(scale, begin, per_device, 0)
    factor = factor * (float(local * count) ** -0.5)
    result = jnp.einsum("jmn,sjcrm->scrmn", mine, spectrum, precision=HIGHEST)
    result = result * factor[:, None] * jnp.array([1.0, -1.0])[:, None, None]
    return replies, result


def least(values):
    result = values[0]
    for value in values[1:]:
        result = jnp.minimum(result, value)
    return result


def hold_rows(lengths, me, local, held):
    firsts = first_rows(lengths, near(me) + near(me ^ SHARES), local)
    for index, first in enumerate(firsts):
        held[pl.ds(index, 1), :] = row_arrays(first)
    for half in range(2):
        begin = least(firsts[half * SHARES : (half + 1) * SHARES])
        held[pl.ds(2 * SHARES + half, 1), :] = row_arrays(begin)


def prepare_kernel(count, local, lengths_held, latitude_held, weights_held, after, *refs):
    coupling, mine, factors, held, pt, square, lengths, latitude, weights, sems = refs
    copies = [
        pltpu.make_async_copy(source, target, sems.at[index])
        for index, (source, target) in enumerate(
            ((lengths_held, lengths), (latitude_held, latitude), (weights_held, weights))
        )
    ]
    for copy in copies:
        copy.start()
    for copy in copies:
        copy.wait()
    me = device_id()
    hold_rows(lengths, me, local, held)
    down = lax.broadcasted_iota(jnp.int32, (8, LANES), 0)
    lane = lax.broadcasted_iota(jnp.int32, (8, LANES), 1)
    group = (lane >> 4) & 3
    packed = down >= SHARES
    array = jnp.where(packed, (lane >> 6) * 2 + ((lane >> 3) & 1), down)
    row = SHARES * array + group
    within = lane & (GROUP - 1)
    outer = within >> 3
    order = jnp.where(
        packed, 8 * me + (lane & 7), 8 * ((me & 3) + SHARES * outer) + (lane & 7)
    ).astype(jnp.float32)
    place = jnp.zeros((8, LANES), jnp.float32)
    weight = jnp.zeros((8, LANES), jnp.float32)
    size = jnp.zeros((8, LANES), jnp.int32)
    for index in range(lengths.shape[0]):
        here = row == index
        place = jnp.where(here, latitude[index], place)
        weight = jnp.where(here, weights[index], weight)
        size = jnp.where(here, lengths[index], size)
    doubling = jnp.where(order == 0.0, 1.0, 2.0)
    scale = weight / size.astype(jnp.float32) * doubling
    sine = jnp.sqrt(1.0 - place * place)
    order_square = order * order
    diagonal = jnp.full((8, LANES), math.sqrt(0.5), jnp.float32)
    previous = jnp.zeros((8, LANES), jnp.float32)
    current = previous
    for degree in range(WAVES):
        if degree:
            diagonal = diagonal * (sine * math.sqrt((2.0 * degree + 1.0) / (2.0 * degree)))
        upper = math.sqrt(max(4.0 * degree * degree - 1.0, 0.0))
        below = float(degree - 1) ** 2
        factor_upper = upper * lax.rsqrt(jnp.maximum(float(degree * degree) - order_square, 1.0))
        factor_lower = jnp.sqrt(
            jnp.maximum(below - order_square, 0.0) * (1.0 / max(4.0 * below - 1.0, 1.0))
        )
        value = (factor_upper * place) * current - (factor_upper * factor_lower) * previous
        value = jnp.where(order > degree, 0.0, jnp.where(order == degree, diagonal, value))
        previous, current = current, value
        for index in range(SHARES + 1):
            pt[index, pl.ds(degree, 1), :] = value[index : index + 1, :]
    for step in range(SHARES):
        for source in range(SHARES):
            moved = group_roll(pt[source], step)
            for target in range(SHARES):
                square[target, pl.ds(step * SHARES + source, 1), :] = jnp.sum(
                    pt[target] * moved, axis=0, keepdims=True
                )
    twice = [jnp.zeros((GROUP, LANES), jnp.float32)] * SHARES
    for through in range(SHARES):
        weighted = square[through] * weight[through : through + 1, :]
        for step in range(SHARES):
            moved = group_roll(weighted, step)
            if step:
                moved = jnp.concatenate(
                    [moved[GROUP - SHARES * step :], moved[: GROUP - SHARES * step]], axis=0
                )
            for target in range(SHARES):
                factor = square[target, pl.ds(step * SHARES + through, 1), :]
                twice[target] = twice[target] + factor * moved
    for target in range(SHARES):
        coupling[0, target] = square[target] * scale[target : target + 1, :]
        coupling[1, target] = twice[target] * scale[target : target + 1, :]
    mine[...] = pt[SHARES]
    factors[0:1, :] = weight[SHARES : SHARES + 1, :]
    factors[1:2, :] = doubling[SHARES : SHARES + 1, :] * (float(local * count) ** -0.5)


def spectral_factors(mine, factors, poly, gram):
    products = lax.dot_general(
        mine, mine, (((0,), (0,)), ((), ())), precision=HIGHEST, preferred_element_type=jnp.float32
    )
    same = (lax.broadcasted_iota(jnp.int32, (LANES, LANES), 0) & 7) == (
        lax.broadcasted_iota(jnp.int32, (LANES, LANES), 1) & 7
    )
    products = jnp.where(same, products * factors[0:1, :], 0.0)
    turned = jnp.concatenate([mine * factors[1:2, :], jnp.zeros_like(mine)], axis=0).T
    for value, out in ((turned, poly), (products, gram)):
        high = value.astype(jnp.bfloat16)
        low = (value - high.astype(jnp.float32)).astype(jnp.bfloat16)
        out[...] = jnp.concatenate([high, high, low], axis=0)


def three_parts(value):
    rounded = value.astype(jnp.bfloat16).astype(jnp.float32)
    return [rounded, value - rounded, rounded]


SMEM = pl.BlockSpec(memory_space=pltpu.SMEM)
VMEM = pl.BlockSpec(memory_space=pltpu.VMEM)


def floats(*shape):
    return jax.ShapeDtypeStruct(shape, jnp.float32)


def prepare(lengths, latitude, weights, after, count, local):
    return pl.pallas_call(
        functools.partial(prepare_kernel, count, local),
        out_shape=[
            floats(2, SHARES, GROUP, LANES),
            floats(WAVES, LANES),
            floats(8, LANES),
            jax.ShapeDtypeStruct((GROUP, LANES), jnp.int32),
        ],
        in_specs=[pl.BlockSpec(memory_space=pltpu.HBM)] * 3 + [pl.BlockSpec(memory_space=pl.ANY)],
        out_specs=[VMEM] * 4,
        scratch_shapes=[
            pltpu.VMEM((SHARES + 1, WAVES, LANES), jnp.float32),
            pltpu.VMEM((SHARES, GROUP, LANES), jnp.float32),
            pltpu.SMEM(lengths.shape, jnp.int32),
            pltpu.SMEM(latitude.shape, jnp.float32),
            pltpu.SMEM(weights.shape, jnp.float32),
            pltpu.SemaphoreType.DMA((3,)),
        ],
        compiler_params=pltpu.CompilerParams(vmem_limit_bytes=SMALL),
        name="prepare",
    )(*in_hbm(lengths, latitude, weights), after)


def fill_window(begin, arrays, out):
    channels = out.shape[0] // WINDOW
    for index in range(WINDOW):
        value = jnp.zeros((channels, LANES), jnp.float32)
        for target in range(SHARES):
            value = jnp.where(begin + index == target, arrays[target], value)
        out[pl.ds(index * channels, channels), :] = value


def couple_kernel(held, rates, coupling, *refs):
    messages, (own, other) = [ref[...] for ref in refs[:SHARES]], refs[SHARES:]
    channels = rates.shape[0]
    arrays = by_row(messages, [held[pl.ds(index, 1), :] for index in range(SHARES)])
    sums = [jnp.zeros((channels, LANES), jnp.float32)] * SHARES
    for source in range(SHARES):
        both = arrays[source][:channels]
        second = rates[...] * arrays[source][channels:]
        for step in range(SHARES):
            moved_both = group_roll(both, step)
            moved_second = group_roll(second, step)
            at = pl.ds(step * SHARES + source, 1)
            for target in range(SHARES):
                sums[target] = (
                    sums[target]
                    + coupling[0, target, at, :] * moved_both
                    - coupling[1, target, at, :] * moved_second
                )
    for half, out in enumerate((own, other)):
        begin = held[pl.ds(2 * SHARES + half, 1), :]
        fill_window(begin, sums, out)


def couple(held, rates, coupling, messages):
    channels = rates.shape[0]
    return pl.pallas_call(
        couple_kernel,
        out_shape=[floats(WINDOW * channels, LANES)] * 2,
        in_specs=[VMEM] * (3 + SHARES),
        out_specs=[VMEM] * 2,
        compiler_params=pltpu.CompilerParams(vmem_limit_bytes=SMALL),
        name="couple",
    )(held, rates, coupling, *messages)


def pack_kernel(held, mine, factors, after, *refs):
    messages, (rows, sent, poly, gram) = [ref[...] for ref in refs[:SHARES]], refs[SHARES:]
    channels = messages[0].shape[0] // 2
    me = device_id()
    places = [held[pl.ds(index, 1), :] for index in range(SHARES)]
    near_half = by_row([interleaved(message, me >= SHARES) for message in messages], places)
    far_half = by_row([interleaved(message, me < SHARES) for message in messages], places)
    for index in range(SHARES):
        rows[pl.ds(index * channels, channels), :] = near_half[index]
    fill_window(held[pl.ds(2 * SHARES, 1), :], far_half, sent)
    spectral_factors(mine[...], factors[...], poly, gram)


def pack(held, mine, factors, after, messages):
    channels = messages[0].shape[0] // 2
    return pl.pallas_call(
        pack_kernel,
        out_shape=[floats(SHARES * channels, LANES), floats(WINDOW * channels, LANES)]
        + [jax.ShapeDtypeStruct((3 * LANES, LANES), jnp.bfloat16)] * 2,
        in_specs=[VMEM] * 3 + [pl.BlockSpec(memory_space=pl.ANY)] + [VMEM] * SHARES,
        out_specs=[VMEM] * 4,
        compiler_params=pltpu.CompilerParams(vmem_limit_bytes=SMALL),
        name="pack",
    )(held, mine, factors, after, *messages)


def hand_out_kernel(held, own, other, after, *outs):
    channels = outs[0].shape[0]
    begin = held[pl.ds(2 * SHARES, 1), :]
    sums = []
    for index in range(WINDOW):
        at = pl.ds(index * channels, channels)
        sums.append(own[at, :] + other[at, :])
    for share, out in zip(RETURN, outs):
        array = held[pl.ds(ORDER.index(share), 1), :] - begin
        value = sums[0]
        for index in range(1, WINDOW):
            value = jnp.where(array == index, sums[index], value)
        out[...] = value


def hand_out(held, own, other, after):
    channels = own.shape[0] // WINDOW
    return pl.pallas_call(
        hand_out_kernel,
        out_shape=[floats(channels, LANES)] * SHARES,
        in_specs=[VMEM] * 3 + [pl.BlockSpec(memory_space=pl.ANY)],
        out_specs=[VMEM] * SHARES,
        compiler_params=pltpu.CompilerParams(vmem_limit_bytes=SMALL),
        name="hand_out",
    )(held, own, other, after)


def spectrum_kernel(held_rows, rates, rows, far, poly, gram, out):
    channels = rates.shape[0]
    begin = held_rows[pl.ds(2 * SHARES + 1, 1), :]
    arrays = []
    for index in range(SHARES):
        value = rows[pl.ds(index * channels, channels), :]
        for place in range(WINDOW):
            piece = far[pl.ds(place * channels, channels), :]
            value = value + jnp.where(begin + place == index, piece, 0.0)
        arrays.append(value)
    across = lax.broadcasted_iota(jnp.int32, (1, LANES), 1)
    held = (across >> 6) * 2 + ((across >> 3) & 1)

    def by_lane(part, field):
        value = jnp.zeros((channels, LANES), jnp.float32)
        for index in range(SHARES):
            shift = (64 * (index >> 1) + 8 * (index & 1) - 64 * part - 8 * field) % LANES
            moved = pltpu.roll(arrays[index], shift, 1) if shift else arrays[index]
            value = jnp.where(held == index, moved, value)
        return value

    down = lax.broadcasted_iota(jnp.int32, (8, LANES), 0)
    lane = lax.broadcasted_iota(jnp.int32, (8, LANES), 1)
    match = jnp.where(down == (lane & 7), 1.0, 0.0)[None]
    for part in range(2):
        second = by_lane(part, 1)
        left = jnp.concatenate([side.astype(jnp.bfloat16) for side in three_parts(second)], axis=1)
        first = by_lane(part, 0) - second
        first = first - rates[...] * jnp.dot(left, gram[...], preferred_element_type=jnp.float32)
        for index, value in enumerate((first, second)):
            if part:
                value = -value
            high, low, _ = three_parts(value)
            sides = [
                (side[:, None, :] * match).reshape(8 * channels, LANES).astype(jnp.bfloat16)
                for side in (high, low)
            ]
            product = jnp.dot(
                jnp.concatenate(sides + sides[:1], axis=1),
                poly[...],
                preferred_element_type=jnp.float32,
            )
            out[index, :, part] = product[:, :WAVES].reshape(channels, 8, WAVES)


def spectrum(held, rates, rows, far, poly, gram):
    channels = rates.shape[0]
    return pl.pallas_call(
        spectrum_kernel,
        out_shape=pltpu.VMEM((2, channels, 2, 8, WAVES), jnp.float32),
        in_specs=[VMEM] * 6,
        out_specs=VMEM,
        compiler_params=pltpu.CompilerParams(vmem_limit_bytes=SMALL),
        name="spectrum",
    )(held, rates, rows, far, poly, gram)


def middle_small(messages, rates, lengths, latitude, weights, local, per_device, count):
    coupling, mine, factors, held = prepare(lengths, latitude, weights, rates, count, local)
    received = exchanged(messages, ORDER)
    part, sent_part = couple(held, rates, coupling, received)
    other_part = swapped(sent_part, SHARES)
    waves = waves_of(lengths, part, local, per_device)
    rows, sent_rows, poly, gram = pack(held, mine, factors, waves[1], received)
    tables = tables_of(lengths, waves, local)
    far = swapped(sent_rows, SHARES)
    replies = hand_out(held, part, other_part, tables[1])
    return replies, tables, (held, rates, rows, far, poly, gram)


def on_device(cot_first, cot_second, strength, lengths, latitude, weights):
    local = cot_first.shape[1]
    count = lax.axis_size(AXES)
    per_device = WAVES // count
    *messages, rates, kept = analyse(lengths, strength, cot_second, cot_first, per_device)
    arguments = (lengths, latitude, weights, local, per_device)
    small = count == 2 * SHARES and lengths.shape[0] == GROUP
    if small:
        replies, tables, pieces = middle_small(messages, rates, *arguments, count)
    else:
        replies, grad_target = middle_general(exchanged(messages, ORDER), strength, *arguments)
        replies = [replies[ORDER.index(share)] for share in RETURN]
        tables = tables_of(lengths, waves_of(lengths, replies[0], local, per_device), local)
    answers = exchanged(replies, RETURN)
    if small:
        grad_target = spectrum(*pieces)
    grad_state, grad_target = restore(answers, kept, tables, grad_target)
    return (grad_state, grad_target)


def solution(mesh):
    return jax.shard_map(
        on_device,
        mesh=mesh,
        in_specs=(
            P("chan", ("groups", "pts", "lev")),
            P("chan", ("groups", "pts", "lev")),
            P(None, ("groups", "chan")),
            P("groups"),
            P("groups"),
            P("groups"),
        ),
        out_specs=(
            P("chan", ("groups", "pts", "lev")),
            P(None, ("groups", "chan"), None, ("pts", "lev"), None),
        ),
        check_vma=False,
    )
```

```python
import functools
import math

import jax
import jax.numpy as jnp
import numpy as np
from jax import lax
from jax.experimental import pallas as pl
from jax.experimental.pallas import tpu as pltpu
from jax.sharding import PartitionSpec as P

MAXLEN = 3072
WAVES = 64
BLOCK = 256
LANES = 128
SHARES = 4
GROUP = WAVES // SHARES
ORDER = (0, 2, 3, 1)
RETURN = (0, 3, 2, 1)
PAD = 64
FULL = 60 * 1024 * 1024
WINDOW = 3
SMALL = 8 * 1024 * 1024
HIGHEST = lax.Precision.HIGHEST
AXES = ("pts", "lev")


def cosine_coefficients():
    nodes = np.cos(np.pi * (np.arange(64) + 0.5) / 64)
    squares = 0.12525 * (nodes + 1.0)
    fitted = np.polynomial.Polynomial.fit(squares, np.cos(2.0 * np.pi * np.sqrt(squares)), 7)
    return [float(value) for value in fitted.convert().coef]


COSINE = cosine_coefficients()


def cos_turns(turns):
    turns = turns - jnp.floor(turns + 0.5)
    square = turns * turns
    value = jnp.full_like(square, COSINE[-1])
    for coefficient in COSINE[-2::-1]:
        value = value * square + coefficient
    return value


def turns_of(wave, point, size):
    inverse = 1.0 / size
    product = wave * point
    whole = jnp.floor(product * inverse + 0.5)
    return (product - whole * size) * inverse


def lane_waves(lane, me, per_device):
    share = (lane >> 4) & 3
    within = lane & (GROUP - 1)
    shift = per_device.bit_length() - 1
    outer = within >> shift
    return per_device * (((me ^ share) & 3) + SHARES * outer) + (within & (per_device - 1))


def device_id():
    return lax.axis_index("pts") * lax.axis_size("lev") + lax.axis_index("lev")


def row_table(lengths, table, me, local, rows):
    begin = me * local
    for slot in range(SHARES):
        table[slot] = 0
        table[SHARES + slot] = MAXLEN
        table[2 * SHARES + slot] = local

    def step(row, carry):
        start, first = carry
        size = lengths[row]
        stop = start + size
        first = first + jnp.where(stop <= begin, 1, 0)

        @pl.when((stop > begin) & (start < begin + local))
        def _():
            table[row & 3] = start - begin
            table[SHARES + (row & 3)] = size
            table[2 * SHARES + row - first] = start - begin

        return stop, first

    _, first = lax.fori_loop(0, rows, step, (jnp.int32(0), jnp.int32(0)))
    table[3 * SHARES] = first


def fill_phases(table, me, per_device, blocks, cosine, sine, sign):
    rows = cosine.shape[1]
    lane = lax.broadcasted_iota(jnp.int32, (rows, LANES), 1)
    begin = BLOCK * lax.broadcasted_iota(jnp.int32, (rows, LANES), 0)
    wave = lane_waves(lane, me, per_device).astype(jnp.float32)
    signs = jnp.where(lane >= PAD, sign, -sign)
    for slot in range(SHARES):
        size = jnp.full((rows, LANES), table[SHARES + slot], jnp.int32).astype(jnp.float32)
        turns = turns_of(wave, (begin - table[slot]).astype(jnp.float32), size)
        cosine[slot] = cos_turns(turns)
        sine[slot] = cos_turns(turns - 0.25) * signs


def basis_of(wave_index, point, size_int, me, per_device):
    wave = lane_waves(wave_index, me, per_device).astype(jnp.float32)
    size = jnp.full(wave.shape, size_int, jnp.int32).astype(jnp.float32)
    turns = turns_of(wave, point.astype(jnp.float32), size)
    value = cos_turns(turns - jnp.where(wave_index >= PAD, 0.25, 0.0))
    high = value.astype(jnp.bfloat16)
    low = (value - high.astype(jnp.float32)).astype(jnp.bfloat16)
    return high, low


def column(row):
    count = row.shape[1]
    down = lax.broadcasted_iota(jnp.int32, (count, count), 0)
    across = lax.broadcasted_iota(jnp.int32, (count, count), 1)
    return jnp.sum(jnp.where(down == across, row, 0.0), axis=1, keepdims=True)


def group_roll(value, step):
    if step == 0:
        return value
    lane = lax.broadcasted_iota(jnp.int32, (1, LANES), 1)
    near = ((lane >> 4) & 3) < SHARES - step
    return jnp.where(
        near,
        pltpu.roll(value, LANES - GROUP * step, 1),
        pltpu.roll(value, GROUP * (SHARES - step), 1),
    )


def first_rows(lengths, devices, local):
    begins = [device * local for device in devices]

    def step(row, carry):
        stop = carry[0] + lengths[row]
        return (stop,) + tuple(
            first + jnp.where(stop <= begin, 1, 0) for first, begin in zip(carry[1:], begins)
        )

    zero = jnp.int32(0)
    return lax.fori_loop(0, lengths.shape[0], step, (zero,) * (1 + len(devices)), unroll=True)[1:]


def near(me):
    return [me ^ share for share in ORDER]


def row_arrays(first):
    lane = lax.broadcasted_iota(jnp.int32, (1, LANES), 1)
    group = (lane >> 4) & 3
    return (first + ((group - first) & 3)) >> 2


def by_row(messages, held):
    arrays = []
    for index in range(SHARES):
        value = jnp.zeros(messages[0].shape, jnp.float32)
        for array, message in zip(held, messages):
            value = value + jnp.where(array == index, message, 0.0)
        arrays.append(value)
    return arrays


def split_block(begin, blocks):
    within = begin & (BLOCK - 1)
    return jnp.minimum(begin >> 8, blocks - 1), jnp.where(within == 0, BLOCK, within)


def interleaved(message, upper):
    channels = message.shape[0] // 2
    both, second = message[:channels], message[channels:]
    odd = ((lax.broadcasted_iota(jnp.int32, (1, LANES), 1) >> 3) & 1) == 1
    return jnp.where(
        upper,
        jnp.where(odd, second, pltpu.roll(both, LANES - 8, 1)),
        jnp.where(odd, pltpu.roll(second, 8, 1), both),
    )


def padded(value):
    return jnp.pad(value, ((0, -value.shape[0] % 8), (0, 0)))


def load_fields(second, first, fields, sems):
    copies = [
        pltpu.make_async_copy(source, fields.at[index], sems.at[index])
        for index, source in enumerate((second, first))
    ]
    for copy in copies:
        copy.start()
    return copies


def analyse_kernel(per_device, lengths_held, strength_held, second, first, *refs):
    messages, (rates, kept, fields, lengths, strength, basis, cosine, sine, total, table) = (
        refs[:SHARES],
        refs[SHARES:-3],
    )
    sems, length_sem, strength_sem = refs[-3:]
    channels, local = second.shape
    blocks = local // BLOCK
    length_copy = pltpu.make_async_copy(lengths_held, lengths, length_sem)
    length_copy.start()
    strength_copy = pltpu.make_async_copy(strength_held, strength, strength_sem)
    strength_copy.start()
    copies = load_fields(second, first, fields, sems)
    me = device_id()
    length_copy.wait()
    strength_copy.wait()
    row_table(lengths, table, me, local, lengths.shape[0])
    fill_phases(table, me, per_device, blocks, cosine, sine, 1.0)
    wave_index = lax.broadcasted_iota(jnp.int32, (BLOCK, LANES), 1)
    point = lax.broadcasted_iota(jnp.int32, (BLOCK, LANES), 0)
    for slot in range(SHARES):
        high, low = basis_of(wave_index, point, table[SHARES + slot], me, per_device)
        basis[slot, :, :LANES] = high
        basis[slot, :, LANES:] = low
    total[...] = jnp.zeros_like(total)
    within = lax.broadcasted_iota(jnp.int32, (1, BLOCK), 1)

    def add_block(block, place, slot, low_end, high_end):
        keep = (within >= low_end) & (within < high_end)
        highs, lows = [], []
        for index in range(2):
            piece = jnp.where(keep, fields[index, :, pl.ds(place, BLOCK)], 0.0)
            high = piece.astype(jnp.bfloat16).astype(jnp.float32)
            highs.append(padded(high))
            lows.append(padded(piece - high))
        highs, lows = [
            jnp.concatenate(sides, axis=0).astype(jnp.bfloat16) for sides in (highs, lows)
        ]
        product = jnp.dot(highs, basis[slot], preferred_element_type=jnp.float32)
        value = product[:, :LANES] + product[:, LANES:]
        value = value + jnp.dot(
            lows, basis[slot, :, :LANES], preferred_element_type=jnp.float32
        )
        turned = (
            value * cosine[slot, pl.ds(block, 1), :]
            + pltpu.roll(value, PAD, 1) * sine[slot, pl.ds(block, 1), :]
        )
        total[slot] = total[slot] + turned

    begin_slot = table[3 * SHARES]
    for copy in copies:
        copy.wait()
    for block in range(blocks):
        place = block * BLOCK
        slot = begin_slot
        for later in range(1, SHARES):
            slot = slot + jnp.where(table[2 * SHARES + later] <= place, 1, 0)
        slot = slot & 3
        add_block(block, place, slot, 0, table[slot] + table[SHARES + slot] - place)
        at = pl.ds(place, BLOCK)
        kept[:, at] = fields[0, :, at] + fields[1, :, at]
    for later in range(1, SHARES):
        block, low_end = split_block(table[2 * SHARES + later], blocks)
        place = pl.multiple_of(block * BLOCK, BLOCK)
        add_block(block, place, (begin_slot + later) & 3, low_end, BLOCK)

    rate_first = column(strength[0:1, :])
    rate_second = column(strength[1:2, :])
    rates[...] = jnp.broadcast_to(rate_first, rates.shape)
    lane = lax.broadcasted_iota(jnp.int32, (1, LANES), 1)
    chunk = (lane >> 4) & 3
    pairs = []
    for slot in range(SHARES):
        value_second = total[slot, :channels, :]
        value_first = total[slot, total.shape[1] // 2 :, :][:channels]
        part_second = rate_second * value_second
        pairs.append((rate_first * (value_first + value_second) + part_second, part_second))
    moved = []
    for which in range(2):
        by_shift = {}
        for shift in range(1 - SHARES, SHARES):
            value = jnp.zeros((channels, LANES), jnp.float32)
            for share in range(SHARES):
                if 0 <= share + shift < SHARES:
                    value = jnp.where(chunk == share, pairs[share + shift][which], value)
            by_shift[shift] = pltpu.roll(value, (shift * GROUP) % LANES, 1) if shift else value
        moved.append(by_shift)
    for share in range(SHARES):
        for which in range(2):
            value = moved[which][-share]
            for slot in range(1, SHARES):
                value = jnp.where(chunk == slot, moved[which][slot - share], value)
            message = messages[ORDER.index(share)]
            message[pl.ds(which * channels, channels), :] = value


def in_hbm(*values):
    return [pltpu.with_memory_space_constraint(value, pltpu.HBM) for value in values]


def analyse(lengths, strength, second, first, per_device):
    channels, local = second.shape
    blocks = local // BLOCK
    phase_rows = -(-blocks // 8) * 8
    return pl.pallas_call(
        functools.partial(analyse_kernel, per_device),
        out_shape=[pltpu.VMEM((2 * channels, LANES), jnp.float32)] * SHARES
        + [
            pltpu.VMEM((channels, LANES), jnp.float32),
            pltpu.VMEM((channels, local), jnp.float32),
        ],
        in_specs=[pl.BlockSpec(memory_space=pltpu.HBM)] * 4,
        out_specs=[pl.BlockSpec(memory_space=pltpu.VMEM)] * (SHARES + 2),
        scratch_shapes=[
            pltpu.VMEM((2, channels, local), jnp.float32),
            pltpu.SMEM(lengths.shape, jnp.int32),
            pltpu.VMEM(strength.shape, jnp.float32),
            pltpu.VMEM((SHARES, BLOCK, 2 * LANES), jnp.bfloat16),
            pltpu.VMEM((SHARES, phase_rows, LANES), jnp.float32),
            pltpu.VMEM((SHARES, phase_rows, LANES), jnp.float32),
            pltpu.VMEM((SHARES, 2 * (channels + -channels % 8), LANES), jnp.float32),
            pltpu.SMEM((16,), jnp.int32),
            pltpu.SemaphoreType.DMA((2,)),
            pltpu.SemaphoreType.DMA,
            pltpu.SemaphoreType.DMA,
        ],
        compiler_params=pltpu.CompilerParams(vmem_limit_bytes=32 * 1024 * 1024),
        name="analyse",
    )(*in_hbm(lengths, strength, second, first))


def restore_kernel(*refs):
    messages, refs = refs[:SHARES], refs[SHARES:]
    kept, bases, cosine, sine, choose, mix, spectra, out, spectra_out, held, coeff = refs[:-2]
    sems, spectra_sem = refs[-2:]
    spectra_copy = pltpu.make_async_copy(spectra, spectra_out, spectra_sem)
    spectra_copy.start()
    channels, local = kept.shape
    blocks = local // BLOCK
    width = local // sems.shape[0]
    lane = lax.broadcasted_iota(jnp.int32, (1, LANES), 1)
    chunk = (lane >> 4) & 3
    coeff[...] = jnp.zeros_like(coeff)
    for slot in range(SHARES):
        value = jnp.zeros((channels, LANES), jnp.float32)
        for share in range(SHARES):
            moved = messages[RETURN.index(share)][...]
            if slot != share:
                moved = pltpu.roll(moved, ((share - slot) * GROUP) % LANES, 1)
            value = jnp.where(chunk == share, moved, value)
        coeff[slot, :channels, :] = value

    def part_value(part):
        value = coeff[0] * choose[pl.ds(SHARES * part, 1), :]
        for slot in range(1, SHARES):
            value = value + coeff[slot] * choose[pl.ds(SHARES * part + slot, 1), :]
        turned = (
            value * cosine[pl.ds(part, 1), :]
            + pltpu.roll(value, PAD, 1) * sine[pl.ds(part, 1), :]
        )
        high = turned.astype(jnp.bfloat16)
        low = (turned - high.astype(jnp.float32)).astype(jnp.bfloat16)
        left = jnp.concatenate([high, low], axis=0)
        left = jnp.concatenate([left, left], axis=1)
        product = jnp.dot(left, bases[part], preferred_element_type=jnp.float32)
        return product[:channels] + product[PAD : PAD + channels]

    ends = [part_value(blocks + index) for index in range(SHARES - 1)]
    copies = []
    for block in range(blocks):
        place = block * BLOCK
        value = part_value(block)
        for index in range(SHARES - 1):
            value = value + ends[index] * mix[pl.ds((SHARES - 1) * block + index, 1), :]
        held[:, pl.ds(place, BLOCK)] = kept[:, pl.ds(place, BLOCK)] - value
        if (place + BLOCK) % width == 0:
            at = pl.ds(place + BLOCK - width, width)
            copies.append(
                pltpu.make_async_copy(held.at[:, at], out.at[:, at], sems.at[len(copies)])
            )
            copies[-1].start()
    for copy in copies:
        copy.wait()
    spectra_copy.wait()


def restore(messages, kept, tables, spectra):
    channels, local = kept.shape
    pieces = math.gcd(local // BLOCK, 6)
    return pl.pallas_call(
        restore_kernel,
        out_shape=[
            jax.ShapeDtypeStruct((channels, local), jnp.float32),
            jax.ShapeDtypeStruct(spectra.shape, jnp.float32),
        ],
        in_specs=[pl.BlockSpec(memory_space=pltpu.VMEM)] * (SHARES + 7),
        out_specs=[pl.BlockSpec(memory_space=pl.ANY)] * 2,
        scratch_shapes=[
            pltpu.VMEM((channels, local), jnp.float32),
            pltpu.VMEM((SHARES, PAD, LANES), jnp.float32),
            pltpu.SemaphoreType.DMA((pieces,)),
            pltpu.SemaphoreType.DMA,
        ],
        compiler_params=pltpu.CompilerParams(vmem_limit_bytes=32 * 1024 * 1024),
        name="restore",
    )(*messages, kept, *tables, spectra)


def fill_tables(table, me, per_device, basis, cosine, sine, blocks):
    fill_phases(table, me, per_device, blocks, cosine, sine, -1.0)
    wave_index = lax.broadcasted_iota(jnp.int32, (LANES, BLOCK), 0)
    point = lax.broadcasted_iota(jnp.int32, (LANES, BLOCK), 1)
    for slot in range(SHARES):
        high, low = basis_of(wave_index, point, table[SHARES + slot], me, per_device)
        basis[slot, :LANES, :] = high
        basis[slot, LANES:, :] = low


def waves_kernel(per_device, local, lengths_held, after, basis, cosine, sine, table, lengths, sem):
    me = device_id()
    copy = pltpu.make_async_copy(lengths_held, lengths, sem)
    copy.start()
    copy.wait()
    row_table(lengths, table, me, local, lengths.shape[0])
    fill_tables(table, me, per_device, basis, cosine, sine, local // BLOCK)


def waves_of(lengths, after, local, per_device):
    phase_rows = -(-(local // BLOCK) // 8) * 8
    return pl.pallas_call(
        functools.partial(waves_kernel, per_device, local),
        out_shape=[
            jax.ShapeDtypeStruct((SHARES, 2 * LANES, BLOCK), jnp.bfloat16),
            jax.ShapeDtypeStruct((SHARES, phase_rows, LANES), jnp.float32),
            jax.ShapeDtypeStruct((SHARES, phase_rows, LANES), jnp.float32),
        ],
        in_specs=[pl.BlockSpec(memory_space=pltpu.HBM), pl.BlockSpec(memory_space=pl.ANY)],
        out_specs=[pl.BlockSpec(memory_space=pltpu.VMEM)] * 3,
        scratch_shapes=[
            pltpu.SMEM((16,), jnp.int32),
            pltpu.SMEM(lengths.shape, jnp.int32),
            pltpu.SemaphoreType.DMA,
        ],
        compiler_params=pltpu.CompilerParams(vmem_limit_bytes=SMALL),
        name="waves",
    )(*in_hbm(lengths), after)


def tables_kernel(
    local, lengths_held, basis, cosines, sines, bases, cosine, sine, choose, mix, *scratch
):
    table, lengths, sem = scratch
    blocks = local // BLOCK
    me = device_id()
    copy = pltpu.make_async_copy(lengths_held, lengths, sem)
    copy.start()
    copy.wait()
    row_table(lengths, table, me, local, lengths.shape[0])
    within = lax.broadcasted_iota(jnp.int32, (1, BLOCK), 1)
    begin_slot = table[3 * SHARES]

    def place_part(part, block, slot, low_end, high_end):
        keep = jnp.where((within >= low_end) & (within < high_end), 1.0, 0.0)
        bases[part] = basis[slot] * keep.astype(jnp.bfloat16)
        cosine[pl.ds(part, 1), :] = cosines[slot, pl.ds(block, 1), :]
        sine[pl.ds(part, 1), :] = sines[slot, pl.ds(block, 1), :]
        for other in range(SHARES):
            mark = jnp.where(slot == other, 1.0, 0.0)
            choose[pl.ds(SHARES * part + other, 1), :] = jnp.full((1, LANES), mark)

    for block in range(blocks):
        place = block * BLOCK
        slot = begin_slot
        for later in range(1, SHARES):
            slot = slot + jnp.where(table[2 * SHARES + later] <= place, 1, 0)
        slot = slot & 3
        place_part(block, block, slot, 0, table[slot] + table[SHARES + slot] - place)
    for later in range(1, SHARES):
        block, low_end = split_block(table[2 * SHARES + later], blocks)
        place_part(blocks + later - 1, block, (begin_slot + later) & 3, low_end, BLOCK)
        for other in range(blocks):
            mark = jnp.where(block == other, 1.0, 0.0)
            mix[pl.ds((SHARES - 1) * other + later - 1, 1), :] = jnp.full((1, BLOCK), mark)


def tables_of(lengths, waves, local):
    blocks = local // BLOCK
    parts = blocks + SHARES - 1
    shapes = [
        jax.ShapeDtypeStruct((parts, 2 * LANES, BLOCK), jnp.bfloat16),
        jax.ShapeDtypeStruct((parts, LANES), jnp.float32),
        jax.ShapeDtypeStruct((parts, LANES), jnp.float32),
        jax.ShapeDtypeStruct((SHARES * parts, LANES), jnp.float32),
        jax.ShapeDtypeStruct(((SHARES - 1) * blocks, BLOCK), jnp.float32),
    ]
    return pl.pallas_call(
        functools.partial(tables_kernel, local),
        out_shape=shapes,
        in_specs=[pl.BlockSpec(memory_space=pltpu.HBM)] + [pl.BlockSpec(memory_space=pltpu.VMEM)] * 3,
        out_specs=[pl.BlockSpec(memory_space=pltpu.VMEM)] * len(shapes),
        scratch_shapes=[
            pltpu.SMEM((16,), jnp.int32),
            pltpu.SMEM(lengths.shape, jnp.int32),
            pltpu.SemaphoreType.DMA,
        ],
        compiler_params=pltpu.CompilerParams(vmem_limit_bytes=SMALL),
        name="tables",
    )(*in_hbm(lengths), *waves)


def swapped(value, mask):
    count = lax.axis_size(AXES)
    return lax.ppermute(value, AXES, [(i, i ^ mask) for i in range(count)])


def exchanged(values, order):
    return [swapped(value, share) if share else value for value, share in zip(values, order)]


def legendre(latitude, waves):
    order = waves.astype(jnp.float32)[None, :]
    sine = jnp.sqrt(1.0 - latitude * latitude)[:, None]
    place = latitude[:, None]
    diagonal = jnp.full((latitude.shape[0], waves.shape[0]), math.sqrt(0.5), jnp.float32)
    previous = jnp.zeros_like(diagonal)
    current = jnp.zeros_like(diagonal)
    degrees = []
    for degree in range(WAVES):
        if degree:
            diagonal = diagonal * (sine * math.sqrt((2.0 * degree + 1.0) / (2.0 * degree)))
        upper = max(4.0 * degree * degree - 1.0, 0.0)
        below = float(degree - 1) ** 2
        factor_upper = jnp.sqrt(upper / jnp.maximum(float(degree * degree) - order * order, 1.0))
        factor_lower = jnp.sqrt(
            jnp.maximum(below - order * order, 0.0) / max(4.0 * below - 1.0, 1.0)
        )
        value = factor_upper * (place * current - factor_lower * previous)
        value = jnp.where(order > degree, 0.0, jnp.where(order == degree, diagonal, value))
        previous, current = current, value
        degrees.append(value)
    return jnp.stack(degrees, axis=-1)


def middle_general(received, strength, lengths, latitude, weights, local, per_device):
    rows = lengths.shape[0]
    count = lax.axis_size(AXES)
    channels = strength.shape[1]
    me = device_id()
    stops = jnp.cumsum(lengths)
    row_ids = jnp.arange(rows, dtype=jnp.int32)
    slots = jnp.arange(SHARES, dtype=jnp.int32)
    picks = []
    for share in ORDER:
        first = jnp.sum((stops <= (me ^ share) * local).astype(jnp.int32))
        held = first + ((slots - first) & 3)
        picks.append((held[:, None] == row_ids[None, :]).astype(jnp.float32))
    total = 0.0
    for pick, message in zip(picks, received):
        total = total + jnp.einsum(
            "gj,fcrgm->jfcrm",
            pick,
            message.reshape(2, channels, 2, SHARES, GROUP),
            precision=HIGHEST,
        )
    mask = SHARES
    while mask < count:
        total = total + swapped(total, mask)
        mask *= 2
    outer = jnp.arange(GROUP, dtype=jnp.int32) // per_device
    waves = per_device * ((me & 3) + SHARES * outer) + jnp.arange(GROUP) % per_device
    values = legendre(latitude, waves)
    gram = jnp.einsum("jmn,kmn->mjk", values, values, precision=HIGHEST)
    scale = jnp.where(waves == 0, 1.0, 2.0)
    rate_first = strength[0][:, None, None]
    both, second = total[:, 0], total[:, 1]
    once = jnp.einsum("mjk,kcrm->jcrm", gram, second, precision=HIGHEST)
    first = both - second - rate_first * weights[:, None, None, None] * once
    back = jnp.einsum("mjk,kcrm->jcrm", gram, first + second, precision=HIGHEST)
    back = back * (weights / lengths.astype(jnp.float32))[:, None, None, None] * scale
    replies = [
        jnp.einsum("gj,jcrm->crgm", pick, back, precision=HIGHEST).reshape(channels, LANES)
        for pick in picks
    ]
    spectrum = jnp.stack([first, second])
    begin = (me // SHARES) * per_device
    spectrum = lax.dynamic_slice_in_dim(spectrum, begin, per_device, 4)
    mine = lax.dynamic_slice_in_dim(values, begin, per_device, 1)
    factor = lax.dynamic_slice_in_dim(scale, begin, per_device, 0)
    factor = factor * (float(local * count) ** -0.5)
    result = jnp.einsum("jmn,sjcrm->scrmn", mine, spectrum, precision=HIGHEST)
    result = result * factor[:, None] * jnp.array([1.0, -1.0])[:, None, None]
    return replies, result


def least(values):
    result = values[0]
    for value in values[1:]:
        result = jnp.minimum(result, value)
    return result


def hold_rows(lengths, me, local, held):
    firsts = first_rows(lengths, near(me) + near(me ^ SHARES), local)
    for index, first in enumerate(firsts):
        held[pl.ds(index, 1), :] = row_arrays(first)
    for half in range(2):
        begin = least(firsts[half * SHARES : (half + 1) * SHARES])
        held[pl.ds(2 * SHARES + half, 1), :] = row_arrays(begin)


def prepare_kernel(count, local, lengths_held, latitude_held, weights_held, after, *refs):
    coupling, mine, factors, held, pt, square, lengths, latitude, weights, sems = refs
    copies = [
        pltpu.make_async_copy(source, target, sems.at[index])
        for index, (source, target) in enumerate(
            ((lengths_held, lengths), (latitude_held, latitude), (weights_held, weights))
        )
    ]
    for copy in copies:
        copy.start()
    for copy in copies:
        copy.wait()
    me = device_id()
    hold_rows(lengths, me, local, held)
    down = lax.broadcasted_iota(jnp.int32, (8, LANES), 0)
    lane = lax.broadcasted_iota(jnp.int32, (8, LANES), 1)
    group = (lane >> 4) & 3
    packed = down >= SHARES
    array = jnp.where(packed, (lane >> 6) * 2 + ((lane >> 3) & 1), down)
    row = SHARES * array + group
    within = lane & (GROUP - 1)
    outer = within >> 3
    order = jnp.where(
        packed, 8 * me + (lane & 7), 8 * ((me & 3) + SHARES * outer) + (lane & 7)
    ).astype(jnp.float32)
    place = jnp.zeros((8, LANES), jnp.float32)
    weight = jnp.zeros((8, LANES), jnp.float32)
    size = jnp.zeros((8, LANES), jnp.int32)
    for index in range(lengths.shape[0]):
        here = row == index
        place = jnp.where(here, latitude[index], place)
        weight = jnp.where(here, weights[index], weight)
        size = jnp.where(here, lengths[index], size)
    doubling = jnp.where(order == 0.0, 1.0, 2.0)
    scale = weight / size.astype(jnp.float32) * doubling
    sine = jnp.sqrt(1.0 - place * place)
    order_square = order * order
    diagonal = jnp.full((8, LANES), math.sqrt(0.5), jnp.float32)
    previous = jnp.zeros((8, LANES), jnp.float32)
    current = previous
    for degree in range(WAVES):
        if degree:
            diagonal = diagonal * (sine * math.sqrt((2.0 * degree + 1.0) / (2.0 * degree)))
        upper = math.sqrt(max(4.0 * degree * degree - 1.0, 0.0))
        below = float(degree - 1) ** 2
        factor_upper = upper * lax.rsqrt(jnp.maximum(float(degree * degree) - order_square, 1.0))
        factor_lower = jnp.sqrt(
            jnp.maximum(below - order_square, 0.0) * (1.0 / max(4.0 * below - 1.0, 1.0))
        )
        value = (factor_upper * place) * current - (factor_upper * factor_lower) * previous
        value = jnp.where(order > degree, 0.0, jnp.where(order == degree, diagonal, value))
        previous, current = current, value
        for index in range(SHARES + 1):
            pt[index, pl.ds(degree, 1), :] = value[index : index + 1, :]
    for step in range(SHARES):
        for source in range(SHARES):
            moved = group_roll(pt[source], step)
            for target in range(SHARES):
                square[target, pl.ds(step * SHARES + source, 1), :] = jnp.sum(
                    pt[target] * moved, axis=0, keepdims=True
                )
    twice = [jnp.zeros((GROUP, LANES), jnp.float32)] * SHARES
    for through in range(SHARES):
        weighted = square[through] * weight[through : through + 1, :]
        for step in range(SHARES):
            moved = group_roll(weighted, step)
            if step:
                moved = jnp.concatenate(
                    [moved[GROUP - SHARES * step :], moved[: GROUP - SHARES * step]], axis=0
                )
            for target in range(SHARES):
                factor = square[target, pl.ds(step * SHARES + through, 1), :]
                twice[target] = twice[target] + factor * moved
    for target in range(SHARES):
        coupling[0, target] = square[target] * scale[target : target + 1, :]
        coupling[1, target] = twice[target] * scale[target : target + 1, :]
    mine[...] = pt[SHARES]
    factors[0:1, :] = weight[SHARES : SHARES + 1, :]
    factors[1:2, :] = doubling[SHARES : SHARES + 1, :] * (float(local * count) ** -0.5)


def spectral_factors(mine, factors, poly, gram):
    products = lax.dot_general(
        mine, mine, (((0,), (0,)), ((), ())), precision=HIGHEST, preferred_element_type=jnp.float32
    )
    same = (lax.broadcasted_iota(jnp.int32, (LANES, LANES), 0) & 7) == (
        lax.broadcasted_iota(jnp.int32, (LANES, LANES), 1) & 7
    )
    products = jnp.where(same, products * factors[0:1, :], 0.0)
    turned = jnp.concatenate([mine * factors[1:2, :], jnp.zeros_like(mine)], axis=0).T
    for value, out in ((turned, poly), (products, gram)):
        high = value.astype(jnp.bfloat16)
        low = (value - high.astype(jnp.float32)).astype(jnp.bfloat16)
        out[...] = jnp.concatenate([high, high, low], axis=0)


def three_parts(value):
    rounded = value.astype(jnp.bfloat16).astype(jnp.float32)
    return [rounded, value - rounded, rounded]


SMEM = pl.BlockSpec(memory_space=pltpu.SMEM)
VMEM = pl.BlockSpec(memory_space=pltpu.VMEM)


def floats(*shape):
    return jax.ShapeDtypeStruct(shape, jnp.float32)


def prepare(lengths, latitude, weights, after, count, local):
    return pl.pallas_call(
        functools.partial(prepare_kernel, count, local),
        out_shape=[
            floats(2, SHARES, GROUP, LANES),
            floats(WAVES, LANES),
            floats(8, LANES),
            jax.ShapeDtypeStruct((GROUP, LANES), jnp.int32),
        ],
        in_specs=[pl.BlockSpec(memory_space=pltpu.HBM)] * 3 + [pl.BlockSpec(memory_space=pl.ANY)],
        out_specs=[VMEM] * 4,
        scratch_shapes=[
            pltpu.VMEM((SHARES + 1, WAVES, LANES), jnp.float32),
            pltpu.VMEM((SHARES, GROUP, LANES), jnp.float32),
            pltpu.SMEM(lengths.shape, jnp.int32),
            pltpu.SMEM(latitude.shape, jnp.float32),
            pltpu.SMEM(weights.shape, jnp.float32),
            pltpu.SemaphoreType.DMA((3,)),
        ],
        compiler_params=pltpu.CompilerParams(vmem_limit_bytes=SMALL),
        name="prepare",
    )(*in_hbm(lengths, latitude, weights), after)


def fill_window(begin, arrays, out):
    channels = out.shape[0] // WINDOW
    for index in range(WINDOW):
        value = jnp.zeros((channels, LANES), jnp.float32)
        for target in range(SHARES):
            value = jnp.where(begin + index == target, arrays[target], value)
        out[pl.ds(index * channels, channels), :] = value


def couple_kernel(half, held, rates, coupling, *refs):
    messages, out = [ref[...] for ref in refs[:SHARES]], refs[-1]
    channels = rates.shape[0]
    arrays = by_row(messages, [held[pl.ds(index, 1), :] for index in range(SHARES)])
    begin = held[pl.ds(2 * SHARES + half, 1), :]

    def factor(which, place, at):
        value = jnp.zeros((1, LANES), jnp.float32)
        for target in range(SHARES):
            value = jnp.where(begin + place == target, coupling[which, target, at, :], value)
        return value

    sums = [jnp.zeros((channels, LANES), jnp.float32)] * WINDOW
    for source in range(SHARES):
        both = arrays[source][:channels]
        second = rates[...] * arrays[source][channels:]
        for step in range(SHARES):
            moved_both = group_roll(both, step)
            moved_second = group_roll(second, step)
            at = pl.ds(step * SHARES + source, 1)
            for place in range(WINDOW):
                sums[place] = (
                    sums[place]
                    + factor(0, place, at) * moved_both
                    - factor(1, place, at) * moved_second
                )
    for place in range(WINDOW):
        out[pl.ds(place * channels, channels), :] = sums[place]


def couple(half, held, rates, coupling, messages, after=()):
    channels = rates.shape[0]
    return pl.pallas_call(
        functools.partial(couple_kernel, half),
        out_shape=floats(WINDOW * channels, LANES),
        in_specs=[VMEM] * (3 + SHARES) + [pl.BlockSpec(memory_space=pl.ANY)] * len(after),
        out_specs=VMEM,
        compiler_params=pltpu.CompilerParams(vmem_limit_bytes=SMALL),
        name=("couple", "couple_across")[half],
    )(held, rates, coupling, *messages, *after)


def pack_kernel(held, mine, factors, after, *refs):
    messages, (rows, sent, poly, gram) = [ref[...] for ref in refs[:SHARES]], refs[SHARES:]
    channels = messages[0].shape[0] // 2
    me = device_id()
    places = [held[pl.ds(index, 1), :] for index in range(SHARES)]
    near_half = by_row([interleaved(message, me >= SHARES) for message in messages], places)
    far_half = by_row([interleaved(message, me < SHARES) for message in messages], places)
    for index in range(SHARES):
        rows[pl.ds(index * channels, channels), :] = near_half[index]
    fill_window(held[pl.ds(2 * SHARES, 1), :], far_half, sent)
    spectral_factors(mine[...], factors[...], poly, gram)


def pack(held, mine, factors, after, messages):
    channels = messages[0].shape[0] // 2
    return pl.pallas_call(
        pack_kernel,
        out_shape=[floats(SHARES * channels, LANES), floats(WINDOW * channels, LANES)]
        + [jax.ShapeDtypeStruct((3 * LANES, LANES), jnp.bfloat16)] * 2,
        in_specs=[VMEM] * 3 + [pl.BlockSpec(memory_space=pl.ANY)] + [VMEM] * SHARES,
        out_specs=[VMEM] * 4,
        compiler_params=pltpu.CompilerParams(vmem_limit_bytes=SMALL),
        name="pack",
    )(held, mine, factors, after, *messages)


def hand_out_kernel(held, own, other, after, *outs):
    channels = outs[0].shape[0]
    begin = held[pl.ds(2 * SHARES, 1), :]
    sums = []
    for index in range(WINDOW):
        at = pl.ds(index * channels, channels)
        sums.append(own[at, :] + other[at, :])
    for share, out in zip(RETURN, outs):
        array = held[pl.ds(ORDER.index(share), 1), :] - begin
        value = sums[0]
        for index in range(1, WINDOW):
            value = jnp.where(array == index, sums[index], value)
        out[...] = value


def hand_out(held, own, other, after):
    channels = own.shape[0] // WINDOW
    return pl.pallas_call(
        hand_out_kernel,
        out_shape=[floats(channels, LANES)] * SHARES,
        in_specs=[VMEM] * 3 + [pl.BlockSpec(memory_space=pl.ANY)],
        out_specs=[VMEM] * SHARES,
        compiler_params=pltpu.CompilerParams(vmem_limit_bytes=SMALL),
        name="hand_out",
    )(held, own, other, after)


def spectrum_kernel(held_rows, rates, rows, far, poly, gram, out):
    channels = rates.shape[0]
    begin = held_rows[pl.ds(2 * SHARES + 1, 1), :]
    arrays = []
    for index in range(SHARES):
        value = rows[pl.ds(index * channels, channels), :]
        for place in range(WINDOW):
            piece = far[pl.ds(place * channels, channels), :]
            value = value + jnp.where(begin + place == index, piece, 0.0)
        arrays.append(value)
    across = lax.broadcasted_iota(jnp.int32, (1, LANES), 1)
    held = (across >> 6) * 2 + ((across >> 3) & 1)

    def by_lane(part, field):
        value = jnp.zeros((channels, LANES), jnp.float32)
        for index in range(SHARES):
            shift = (64 * (index >> 1) + 8 * (index & 1) - 64 * part - 8 * field) % LANES
            moved = pltpu.roll(arrays[index], shift, 1) if shift else arrays[index]
            value = jnp.where(held == index, moved, value)
        return value

    down = lax.broadcasted_iota(jnp.int32, (8, LANES), 0)
    lane = lax.broadcasted_iota(jnp.int32, (8, LANES), 1)
    match = jnp.where(down == (lane & 7), 1.0, 0.0)[None]
    for part in range(2):
        second = by_lane(part, 1)
        left = jnp.concatenate([side.astype(jnp.bfloat16) for side in three_parts(second)], axis=1)
        first = by_lane(part, 0) - second
        first = first - rates[...] * jnp.dot(left, gram[...], preferred_element_type=jnp.float32)
        for index, value in enumerate((first, second)):
            if part:
                value = -value
            high, low, _ = three_parts(value)
            sides = [
                (side[:, None, :] * match).reshape(8 * channels, LANES).astype(jnp.bfloat16)
                for side in (high, low)
            ]
            product = jnp.dot(
                jnp.concatenate(sides + sides[:1], axis=1),
                poly[...],
                preferred_element_type=jnp.float32,
            )
            out[index, :, part] = product[:, :WAVES].reshape(channels, 8, WAVES)


def spectrum(held, rates, rows, far, poly, gram):
    channels = rates.shape[0]
    return pl.pallas_call(
        spectrum_kernel,
        out_shape=pltpu.VMEM((2, channels, 2, 8, WAVES), jnp.float32),
        in_specs=[VMEM] * 6,
        out_specs=VMEM,
        compiler_params=pltpu.CompilerParams(vmem_limit_bytes=SMALL),
        name="spectrum",
    )(held, rates, rows, far, poly, gram)


def middle_small(messages, rates, lengths, latitude, weights, local, per_device, count):
    coupling, mine, factors, held = prepare(lengths, latitude, weights, rates, count, local)
    received = exchanged(messages, ORDER)
    sent_part = couple(1, held, rates, coupling, received)
    other_part = swapped(sent_part, SHARES)
    waves = waves_of(lengths, sent_part, local, per_device)
    rows, sent_rows, poly, gram = pack(held, mine, factors, waves[1], received)
    tables = tables_of(lengths, waves, local)
    far = swapped(sent_rows, SHARES)
    part = couple(0, held, rates, coupling, received, (sent_rows,))
    replies = hand_out(held, part, other_part, tables[1])
    return replies, tables, (held, rates, rows, far, poly, gram)


def on_device(cot_first, cot_second, strength, lengths, latitude, weights):
    local = cot_first.shape[1]
    count = lax.axis_size(AXES)
    per_device = WAVES // count
    *messages, rates, kept = analyse(lengths, strength, cot_second, cot_first, per_device)
    arguments = (lengths, latitude, weights, local, per_device)
    small = count == 2 * SHARES and lengths.shape[0] == GROUP
    if small:
        replies, tables, pieces = middle_small(messages, rates, *arguments, count)
    else:
        replies, grad_target = middle_general(exchanged(messages, ORDER), strength, *arguments)
        replies = [replies[ORDER.index(share)] for share in RETURN]
        tables = tables_of(lengths, waves_of(lengths, replies[0], local, per_device), local)
    answers = exchanged(replies, RETURN)
    if small:
        grad_target = spectrum(*pieces)
    grad_state, grad_target = restore(answers, kept, tables, grad_target)
    return (grad_state, grad_target)


def solution(mesh):
    return jax.shard_map(
        on_device,
        mesh=mesh,
        in_specs=(
            P("chan", ("groups", "pts", "lev")),
            P("chan", ("groups", "pts", "lev")),
            P(None, ("groups", "chan")),
            P("groups"),
            P("groups"),
            P("groups"),
        ),
        out_specs=(
            P("chan", ("groups", "pts", "lev")),
            P(None, ("groups", "chan"), None, ("pts", "lev"), None),
        ),
        check_vma=False,
    )
```
